128 devices in a mesh: seq: 16 (over z, y), dp: 8 (over x, core).
Axes of the slice: x: 4, y: 4, z: 4, core: 2. Of those that a mesh axis runs over, the one named last changes fastest.
Arguments:
- reader_rows: float32 [8, 2048, 6144], P('dp', 'seq'), may hold values from -40 to 40
- reader_targets: float32 [8, 2048, 2048], P('dp', 'seq'), may hold values from -3 to 3
- dest_pos: int32 [8, 2048], P('dp', 'seq'), may hold values from 0 to 2047, as said below
- bucket_ids: int32 [8, 2048], P('dp', 'seq'), may hold values from 0 to 15, as said below
- ref_loss: float32 [8, 2048], P('dp', 'seq'), may hold values from 0.1 to 0.6
- timesteps: int32 [8], P('dp'), may hold values from 0 to 999
- mod_weight: float32 [256, 2048], replicated, may hold values from -0.75 to 0.75
- mixture_old: float32 [16], replicated, may hold values from 0.25 to 4
Outputs:
- attended: float32 [8, 2048, 2048], P('dp', 'seq')
- qkv_grad: float32 [8, 2048, 6144], P('dp', 'seq')
- mod_weight_grad: float32 [256, 2048], replicated
- mixture: float32 [16], replicated
The draws below stay inside these ranges and needn't reach their ends.
Inputs may be any that keep to these rules, and one draw needn't show every extreme that they name: `dest_pos`: the positions of one sample form a permutation of the sequence; the rows of one device go at most 16 to any one sequence shard (positions k * 128 to (k + 1) * 128 - 1), and every device sends exactly 16 rows to some shard. `bucket_ids`: A bucket may hold no position at all.
All inputs are finite; a program needn't handle non-finite values.
Results may differ from the reference program's by a relative error of at most 0.0003.
Values sent between devices are 32-bit elements; how exact they have to be, the bound alone decides.
A program may use at most 128 MiB of HBM per device.

```python
import math
import jax
import jax.numpy as jnp
from jax import lax

HEADS = 16
HEAD_DIM = 128
FREQ_DIM = 256
BUCKETS = 16
ROWS_DEV = 128
SAMPLES = 8
SEQ_LEN = 2048
WIDTH = 2048


def draw_reader_rows(key, part):
    key = jax.random.fold_in(key, 11)
    full_shape = (SAMPLES, SEQ_LEN, 3, HEADS, HEAD_DIM)
    base = jax.random.normal(key, full_shape, jnp.float32)
    factor = jnp.array([1.0, 1.0, 6.0], jnp.float32)[None, None, :, None, None]
    return jnp.clip(base * factor, -40.0, 40.0).reshape(SAMPLES, SEQ_LEN, 3 * WIDTH)


def draw_dest_pos(key, part):
    key = jax.random.fold_in(key, 23)
    shards = SEQ_LEN // ROWS_DEV
    base_count = ROWS_DEV // shards
    key_pairs, key_shift, key_inner, key_rows = jax.random.split(key, 4)
    pair_values = jax.random.randint(key_pairs, (SAMPLES, shards // 2), 0, base_count + 1)
    pair_values = pair_values.at[:, 0].set(base_count)
    shift_table = jnp.stack([pair_values, -pair_values], axis=2).reshape(SAMPLES, shards)
    shift_table = jax.vmap(jax.random.permutation)(jax.random.split(key_shift, SAMPLES), shift_table)
    source_ids = jnp.arange(shards)
    offset_index = (source_ids[None, :] - source_ids[:, None]) % shards
    counts = base_count + shift_table[:, offset_index]
    earlier = jnp.cumsum(counts, axis=1) - counts
    end_marks = jnp.cumsum(counts, axis=2)
    start_marks = end_marks - counts
    slot_range = jnp.arange(ROWS_DEV)
    owner_shard = jnp.sum(slot_range[None, None, :, None] >= end_marks[:, :, None, :], axis=3)
    within = slot_range[None, None, :] - jnp.take_along_axis(start_marks, owner_shard, axis=2)
    rank_inside = jnp.take_along_axis(earlier, owner_shard, axis=2) + within
    inner_order = jax.vmap(lambda sub_key: jax.random.permutation(sub_key, ROWS_DEV))(jax.random.split(key_inner, SAMPLES * shards)).reshape(SAMPLES, shards * ROWS_DEV)
    flat_index = (owner_shard * ROWS_DEV + rank_inside).reshape(SAMPLES, shards * ROWS_DEV)
    positions = owner_shard.reshape(SAMPLES, shards * ROWS_DEV) * ROWS_DEV + jnp.take_along_axis(inner_order, flat_index, axis=1)
    reorder = jax.vmap(lambda sub_key: jax.random.permutation(sub_key, ROWS_DEV))(jax.random.split(key_rows, SAMPLES * shards)).reshape(SAMPLES, shards, ROWS_DEV)
    positions = jnp.take_along_axis(positions.reshape(SAMPLES, shards, ROWS_DEV), reorder, axis=2)
    return positions.reshape(SAMPLES, SEQ_LEN).astype(jnp.int32)


def draw_bucket_ids(key, part):
    key = jax.random.fold_in(key, 37)
    key_rank, key_order, key_empty = jax.random.split(key, 3)
    bucket_weights = jnp.array([840 // (rank_index + 1) for rank_index in range(BUCKETS)], jnp.int32)
    bucket_ends = jnp.cumsum(bucket_weights)
    raw_draws = jax.random.randint(key_rank, (SAMPLES, SEQ_LEN), 0, bucket_ends[BUCKETS - 1])
    rank_list = jnp.sum(raw_draws[:, :, None] >= bucket_ends[None, None, :], axis=2).astype(jnp.int32)
    order_table = jax.random.permutation(key_order, BUCKETS).astype(jnp.int32)
    bucket_list = order_table[rank_list]
    empty_bucket = jax.random.randint(key_empty, (), 1, BUCKETS - 1).astype(jnp.int32)
    bucket_list = jnp.where(bucket_list == empty_bucket, empty_bucket + 1, bucket_list)
    bucket_list = bucket_list.at[0, 0].set(0).at[0, 1].set(BUCKETS - 1)
    return bucket_list.astype(jnp.int32)


def set_ends(drawn, rng, smallest, largest):
    longest = drawn.shape.index(max(drawn.shape))
    spots = []
    for shift in (0, 1):
        where = [jax.random.randint(jax.random.fold_in(rng, axis), (), 0, length) for axis, length in enumerate(drawn.shape)]
        where[longest] = (where[longest] + shift) % drawn.shape[longest]
        spots.append(tuple(where))
    return drawn.at[spots[0]].set(smallest).at[spots[1]].set(largest)


def levels(rng, extent, cuts, least, top_value):
    def one(dim, parts):
        steps = jax.random.uniform(jax.random.fold_in(jax.random.fold_in(rng, 6), dim), (parts,), jnp.float32, least / len(cuts), top_value / len(cuts))
        return jnp.repeat(jnp.exp(steps), extent[dim] // parts).reshape((-1,) + (1,) * (len(extent) - dim - 1))

    loudness = one(*cuts[0])
    for cut in cuts[1:]:
        loudness = loudness * one(*cut)
    return loudness


def bell_draw(rng, extent, spread, bound, cuts=(), held_as=jnp.bfloat16):
    gain = levels(rng, extent, cuts, -0.22, 0.18) if cuts else 1.0
    values = jax.random.normal(rng, extent, jnp.float32) * spread * gain
    return jnp.minimum(jnp.maximum(values, -bound), bound).astype(held_as)


def setup_inputs(seed: int = 0) -> dict:
    key_of = jax.random.split(jax.random.key(seed), 9)
    return {
        "reader_rows": draw_reader_rows(jax.random.fold_in(key_of[8], 71), 0),
        "reader_targets": bell_draw(key_of[1], (SAMPLES, SEQ_LEN, WIDTH), 0.5, 3.0, ((0, 8), (1, 16)), jnp.float32),
        "dest_pos": draw_dest_pos(jax.random.fold_in(key_of[8], 71), 0),
        "bucket_ids": draw_bucket_ids(jax.random.fold_in(key_of[8], 71), 0),
        "ref_loss": jnp.clip(0.1 + 0.5 * jax.random.uniform(key_of[4], (SAMPLES, SEQ_LEN), jnp.float32) ** levels(key_of[4], (SAMPLES, SEQ_LEN), ((0, 8), (1, 16)), -0.2, 0.2), 0.1, 0.6),
        "timesteps": set_ends(jax.random.randint(key_of[5], (SAMPLES,), 0, 1000), jax.random.fold_in(key_of[5], 1), 0, 999).astype(jnp.int32),
        "mod_weight": bell_draw(key_of[6], (FREQ_DIM, WIDTH), 0.125, 0.75, (), jnp.float32),
        "mixture_old": jnp.clip(jnp.exp(jax.random.uniform(key_of[7], (BUCKETS,), jnp.float32, math.log(0.25), math.log(4.0))), 0.25, 4.0),
    }


highest = lax.Precision.HIGHEST
excess_rate = 10.0


def embed_time(timesteps):
    half_dim = FREQ_DIM // 2
    frequency = jnp.exp(-math.log(10000.0) * jnp.arange(half_dim, dtype=jnp.float32) / half_dim)
    angles = timesteps.astype(jnp.float32)[:, None] * frequency[None, :]
    return jax.nn.silu(jnp.concatenate([jnp.cos(angles), jnp.sin(angles)], axis=1))


def head_pass(query_rows, key_rows, value_rows, aim_rows, gain_row, row_weight):
    softmax_scale = HEAD_DIM ** -0.5
    scores = jnp.dot(query_rows, key_rows.T, precision=highest) * softmax_scale
    row_top = jnp.max(scores, axis=1, keepdims=True)
    expweights = jnp.exp(scores - row_top)
    probability = expweights / jnp.sum(expweights, axis=1, keepdims=True)
    head_output = jnp.dot(probability, value_rows, precision=highest)
    attended = gain_row[None, :] * head_output
    upstream_a = row_weight[:, None] * (attended - aim_rows)
    upstream = gain_row[None, :] * upstream_a
    gain_grad = jnp.sum(upstream_a * head_output, axis=0)
    prob_grad = jnp.dot(upstream, value_rows.T, precision=highest)
    row_delta = jnp.sum(upstream * head_output, axis=1, keepdims=True)
    score_grad = probability * (prob_grad - row_delta)
    query_grad = softmax_scale * jnp.dot(score_grad, key_rows, precision=highest)
    key_grad = softmax_scale * jnp.dot(score_grad.T, query_rows, precision=highest)
    value_grad = jnp.dot(probability.T, upstream, precision=highest)
    return attended, jnp.stack([query_grad, key_grad, value_grad]), gain_grad


def reference(reader_rows, reader_targets, dest_pos, bucket_ids, ref_loss, timesteps, mod_weight, mixture_old):
    def place(row_block, positions):
        return jnp.zeros_like(row_block).at[positions].set(row_block)

    seq_rows = jax.vmap(place)(reader_rows, dest_pos)
    seq_targets = jax.vmap(place)(reader_targets, dest_pos)
    embedding = embed_time(timesteps)
    modulation = 1.0 + jnp.dot(embedding, mod_weight, precision=highest)
    row_weights = mixture_old[bucket_ids]

    def one_sample(packed):
        sample_rows, sample_aims, sample_gain, sample_weight = packed
        trios = sample_rows.reshape(SEQ_LEN, 3, HEADS, HEAD_DIM).transpose(2, 1, 0, 3)
        aim_heads = sample_aims.reshape(SEQ_LEN, HEADS, HEAD_DIM).transpose(1, 0, 2)
        gain_heads = sample_gain.reshape(HEADS, HEAD_DIM)

        def one_head(item):
            trio, aim_rows, gain_row = item
            return head_pass(trio[0], trio[1], trio[2], aim_rows, gain_row, sample_weight)

        head_att, head_grads, head_gains = lax.map(one_head, (trios, aim_heads, gain_heads))
        sample_att = head_att.transpose(1, 0, 2).reshape(SEQ_LEN, WIDTH)
        sample_grads = head_grads.transpose(2, 1, 0, 3).reshape(SEQ_LEN, 3 * WIDTH)
        return sample_att, sample_grads, head_gains.reshape(WIDTH)

    attended, qkv_grad, gain_grad = lax.map(one_sample, (seq_rows, seq_targets, modulation, row_weights))
    mod_weight_grad = jnp.dot(embedding.T, gain_grad, precision=highest)
    row_loss = 0.5 * jnp.mean((attended - seq_targets) ** 2, axis=2)
    excess = jnp.maximum(row_loss - ref_loss, 0.0)
    onehot = (bucket_ids[:, :, None] == jnp.arange(BUCKETS)[None, None, :]).astype(jnp.float32)
    bucket_sums = jnp.sum(onehot * excess[:, :, None], axis=(0, 1))
    bucket_counts = jnp.sum(onehot, axis=(0, 1))
    bucket_excess = bucket_sums / jnp.maximum(bucket_counts, 1.0)
    updated = mixture_old * (1.0 + excess_rate * bucket_excess)
    mixture = BUCKETS * updated / jnp.sum(updated)
    return attended, qkv_grad, mod_weight_grad, mixture
```

```python
import functools
import math

import jax
import jax.numpy as jnp
import numpy as np
from jax import lax
from jax.experimental import pallas as pl
from jax.experimental.pallas import tpu as pltpu
from jax.sharding import PartitionSpec as P

HEADS = 16
DIM = 128
FREQ_DIM = 256
BUCKETS = 16
WIDTH = HEADS * DIM
RATE = 10.0
CHUNK = 64
LOG2E = 1.4426950408889634
SCALE = DIM ** (-0.5)
MESH = pl.DeviceIdType.MESH
HIGHEST = lax.Precision.HIGHEST
BF16 = jnp.bfloat16
F32 = jnp.float32

OFFSETS = (
    (0, 2), (2, 0), (2, 2), (1, 2), (-1, 2), (2, 1), (2, -1),
    (1, 1), (-1, -1), (1, -1), (-1, 1), (0, 1), (1, 0), (0, -1), (-1, 0),
)
POS, WEIGHT, BUCKET, REF, EMB, MIX = 0, 1, 2, 3, 4, 6
KEY, QUERY, VALUE, AIM = 0, 1, 2, 3
SLOT = {AIM: KEY, VALUE: QUERY, QUERY: VALUE, KEY: AIM}
PART_COLUMN = {KEY: WIDTH, QUERY: 0, VALUE: 2 * WIDTH, AIM: 0}


def split(x):
    hi = x.astype(BF16)
    return hi, (x - hi.astype(F32)).astype(BF16)


def dot(a, b):
    return lax.dot_general(a, b, (((1,), (0,)), ((), ())), preferred_element_type=F32)


def dot_nt(a, b):
    return lax.dot_general(a, b, (((1,), (1,)), ((), ())), preferred_element_type=F32)


def kernel(
    shards, copies, rows, aims, places, buckets, ref_row, steps, old, frequency, mod_w,
    att_out, grad_out, weight_out, mix_out,
    meta, meta_all, got, mod_buf, perm, cat, k3, kt, q3, v3, vt, u3, e_hi, e_lo, head_out, inv_sum, delta,
    gain_sum, score_a, score_b, loss_rows, stage1, tile1, stage2, tile2, stage3, tile3,
    send_sem, recv_sem, back_send, back_recv, small_send, small_recv, mod_sem,
):
    length = shards * DIM
    me = lax.axis_index("seq")
    sample = lax.axis_index("dp")
    my_z, my_y = me // 4, lax.rem(me, 4)

    def peer(step):
        return lax.rem(my_z + step[0] + 4, 4) * 4 + lax.rem(my_y + step[1] + 4, 4)

    barrier = pltpu.get_barrier_semaphore()
    for step in OFFSETS:
        pl.semaphore_signal(barrier, inc=1, device_id={"seq": peer(step)}, device_id_type=MESH)
    for turn in range(1, copies):
        other = lax.rem(sample + turn, copies)
        pl.semaphore_signal(barrier, inc=1, device_id={"dp": other}, device_id_type=MESH)

    meta[POS : POS + 1, :] = places[...].astype(F32)
    bucket_row = buckets[...]
    lane = lax.broadcasted_iota(jnp.int32, (1, DIM), 1)
    weight_row = jnp.zeros((1, DIM), F32)
    old_row = jnp.zeros((1, DIM), F32)
    for bucket in range(BUCKETS):
        weight_row = weight_row + jnp.where(bucket_row == bucket, old[bucket], 0.0)
        old_row = old_row + jnp.where(lane == bucket, old[bucket], 0.0)
    meta[WEIGHT : WEIGHT + 1, :] = weight_row
    meta[BUCKET : BUCKET + 1, :] = bucket_row.astype(F32)
    meta[REF : REF + 1, :] = ref_row[...]
    angles = steps[0].astype(F32) * frequency[...]
    for row, wave in ((EMB, jnp.cos(angles)), (EMB + 1, jnp.sin(angles))):
        meta[row : row + 1, :] = wave / (1.0 + jnp.exp(-wave))
    meta[MIX : MIX + 1, :] = old_row
    meta[MIX + 1 : MIX + 2, :] = jnp.zeros((1, DIM), F32)
    pl.semaphore_wait(barrier, shards - 1 + copies - 1)

    meta_all[me] = meta[...]
    for step in OFFSETS:
        pltpu.make_async_remote_copy(
            meta, meta_all.at[me], small_send.at[0], small_recv.at[0],
            device_id={"seq": peer(step)}, device_id_type=MESH,
        ).start()
    mod_copy = pltpu.make_async_copy(
        mod_w.at[:, pl.ds(pl.multiple_of(me * DIM, DIM), DIM)], mod_buf, mod_sem
    )
    mod_copy.start()

    def source(part, head):
        base = aims if part == AIM else rows
        return base.at[:, pl.ds(pl.multiple_of(PART_COLUMN[part] + head * DIM, DIM), DIM)]

    def landing(part):
        return got.at[part, pl.ds(pl.multiple_of(me * DIM, DIM), DIM), :]

    for part in (KEY, QUERY, VALUE, AIM):
        pltpu.make_async_copy(source(part, me), landing(part), recv_sem.at[part]).start()
        for step in OFFSETS:
            head = peer(step)
            pltpu.make_async_remote_copy(
                source(part, head), landing(part), send_sem.at[part], recv_sem.at[part],
                device_id={"seq": head}, device_id_type=MESH,
            ).start()

    def wait_small(stage, buffer, count):
        pltpu.make_async_copy(buffer.at[pl.ds(0, count)], buffer.at[pl.ds(0, count)], small_recv.at[stage]).wait()

    def wait_small_send(stage, buffer, count):
        pltpu.make_async_copy(buffer.at[pl.ds(0, count)], buffer.at[pl.ds(0, count)], small_send.at[stage]).wait()

    mod_copy.wait()
    embedding = jnp.concatenate([meta[EMB : EMB + 1, :], meta[EMB + 1 : EMB + 2, :]], axis=1)
    embedding = jnp.broadcast_to(embedding, (8, FREQ_DIM))
    gain_row = 1.0 + lax.dot_general(
        embedding, mod_buf[...], (((1,), (0,)), ((), ())), precision=HIGHEST, preferred_element_type=F32
    )
    gain = jnp.broadcast_to(gain_row[0:1, :], (DIM, DIM)).T

    wait_small(0, meta_all, shards - 1)

    def perm_block(block, carry):
        at = pl.multiple_of(block * 256, 256)
        place = (lax.broadcasted_iota(jnp.int32, (256, DIM), 0) + at).astype(F32)
        for shard in range(shards):
            hit = place == meta_all[shard, POS : POS + 1, :]
            perm[pl.ds(at, 256), shard * DIM : (shard + 1) * DIM] = jnp.where(hit, 1.0, 0.0).astype(BF16)
        return carry

    lax.fori_loop(0, length // 256, perm_block, 0)

    def pipeline(count, make, use, finish=None):
        def both(at, last):
            make(at + 1, score_b)
            use(at, score_a)
            if not last:
                make(at + 2, score_a)
            use(at + 1, score_b)
            if finish is not None:
                finish(at)
                finish(at + 1)

        def one(pair, carry):
            both(2 * pair, False)
            return carry

        make(0, score_a)
        lax.fori_loop(0, count // 2 - 1, one, 0)
        both(count - 2, True)

    def arrive(part, factor):
        pltpu.make_async_copy(got.at[part], got.at[part], recv_sem.at[part]).wait()

        def one(block, carry):
            at = pl.multiple_of(block * 256, 256)
            hi, lo = split(got[part, pl.ds(at, 256), :] * factor)
            cat[pl.ds(at, 256), 0:DIM] = hi
            cat[pl.ds(at, 256), DIM : 2 * DIM] = lo
            return carry

        lax.fori_loop(0, length // 256, one, 0)

    def reorder(part, factor, into, transposed):
        arrive(part, factor)

        def make(block, buffer):
            at = pl.multiple_of(block * 512, 512)
            buffer[0:512, :] = dot(perm[pl.ds(at, 512), :], cat[...])

        def use(block, buffer):
            at = pl.multiple_of(block * 512, 512)
            placed = buffer[0:512, :]
            hi, lo = placed[:, :DIM].astype(BF16), placed[:, DIM:].astype(BF16)
            into[pl.ds(at, 512), 0:DIM] = hi
            into[pl.ds(at, 512), DIM : 2 * DIM] = hi if part == QUERY else lo
            into[pl.ds(at, 512), 2 * DIM : 3 * DIM] = lo if part == QUERY else hi
            if transposed is not None:
                hi, lo = split((placed[:, :DIM] + placed[:, DIM:]).T)
                transposed[0:DIM, pl.ds(at, 512)] = hi
                transposed[DIM : 2 * DIM, pl.ds(at, 512)] = lo

        pipeline(length // 512, make, use)

    def by_columns(left, high, low):
        full = dot(left[...], high)
        return full[:DIM] + full[DIM:] + dot(left[0:DIM, :], low)

    def by_rows(at, right):
        full = dot(e_hi[pl.ds(at, 512), :], right[...])
        return full[:, :DIM] + full[:, DIM:] + dot(e_lo[pl.ds(at, 512), :], right[:, 0:DIM])

    reorder(KEY, 1.0, k3, kt)
    reorder(QUERY, SCALE * LOG2E, q3, None)

    def score_block(block, buffer):
        at = pl.multiple_of(block * 256, 256)
        buffer[...] = dot_nt(k3[...], q3[pl.ds(at, 256), :])

    def softmax_block(block, buffer):
        at = pl.multiple_of(block * 256, 256)
        top = jnp.full((8, 256), -jnp.inf, F32)
        for row in range(0, length, CHUNK):
            top = jnp.maximum(top, jnp.max(buffer[row : row + CHUNK, :].reshape(CHUNK // 8, 8, 256), axis=0))
        top = jnp.max(top, axis=0, keepdims=True)
        sums = jnp.zeros((8, 256), F32)
        for row in range(0, length, CHUNK):
            weights = jnp.exp2(buffer[row : row + CHUNK, :] - top)
            sums = sums + jnp.sum(weights.reshape(CHUNK // 8, 8, 256), axis=0)
            hi, lo = split(weights)
            e_hi[row : row + CHUNK, pl.ds(at, 256)] = hi
            e_lo[row : row + CHUNK, pl.ds(at, 256)] = lo
        inv_sum[:, pl.ds(at, 256)] = jnp.broadcast_to(1.0 / jnp.sum(sums, axis=0, keepdims=True), (8, 256))

    pipeline(length // 256, score_block, softmax_block)

    def target(part):
        base = att_out if part == AIM else grad_out
        return base.at[:, pl.ds(pl.multiple_of(PART_COLUMN[part] + me * DIM, DIM), DIM)]

    def give(part, shard):
        block = got.at[SLOT[part], pl.ds(pl.multiple_of(shard * DIM, DIM), DIM), :]

        @pl.when(shard != me)
        def _():
            pltpu.make_async_remote_copy(
                block, target(part), back_send.at[part], back_recv.at[part],
                device_id={"seq": shard}, device_id_type=MESH,
            ).start()

        @pl.when(shard == me)
        def _():
            pltpu.make_async_copy(block, target(part), back_recv.at[part]).start()

    def pair_of(turn):
        return lax.rem(my_z + 2 + turn // 2, 4) * 2 + lax.rem(my_y // 2 + 1 + lax.rem(turn, 2), 2)

    def row_of(turn):
        return lax.rem(my_z + 2 + turn, 4)

    reorder(VALUE, 1.0, v3, vt)

    def output_block(turn, buffer):
        at = pl.multiple_of(pair_of(turn) * 256, 256)
        buffer[0:DIM, :] = by_columns(vt, e_hi[:, pl.ds(at, 256)], e_lo[:, pl.ds(at, 256)])

    def attended_block(turn, buffer):
        at = pl.multiple_of(pair_of(turn) * 256, 256)
        out = buffer[0:DIM, :] * inv_sum[0:1, pl.ds(at, 256)]
        head_out[:, pl.ds(at, 256)] = out
        for half in range(2):
            begin = pl.multiple_of(at + half * DIM, DIM)
            got[SLOT[AIM], pl.ds(begin, DIM), :] = (gain * out[:, half * DIM : (half + 1) * DIM]).T

    def give_pair(part):
        def finish(turn):
            for half in range(2):
                give(part, pair_of(turn) * 2 + half)

        return finish

    pipeline(shards // 2, output_block, attended_block, give_pair(AIM))

    arrive(AIM, 1.0)

    def aim_block(block, buffer):
        at = pl.multiple_of(block * 512, 512)
        buffer[0:512, :] = dot(perm[pl.ds(at, 512), :], cat[...])

    gain_sum[...] = jnp.zeros((DIM, DIM), F32)

    def upstream_block(block, buffer):
        at = pl.multiple_of(block * 512, 512)
        placed = buffer[0:512, :]
        aim = placed[:, :DIM] + placed[:, DIM:]
        total = jnp.zeros((DIM, DIM), F32)
        for quarter in range(4):
            shard = block * 4 + quarter
            begin = pl.multiple_of(at + quarter * DIM, DIM)
            out = head_out[:, pl.ds(begin, DIM)]
            gap = gain * out - aim[quarter * DIM : (quarter + 1) * DIM, :].T
            loss_rows[shard] = jnp.broadcast_to(jnp.sum(gap * gap, axis=0, keepdims=True), (8, DIM))
            up_a = gap * meta_all[shard, WEIGHT : WEIGHT + 1, :]
            total = total + up_a * out
            up = gain * up_a * inv_sum[0:1, pl.ds(begin, DIM)]
            delta[:, pl.ds(begin, DIM)] = jnp.broadcast_to(jnp.sum(up * out, axis=0, keepdims=True), (8, DIM))
            hi, lo = split(up.T)
            u3[pl.ds(begin, DIM), 0:DIM] = hi
            u3[pl.ds(begin, DIM), DIM : 2 * DIM] = hi
            u3[pl.ds(begin, DIM), 2 * DIM : 3 * DIM] = lo
        gain_sum[...] += total

    pipeline(length // 512, aim_block, upstream_block)

    gain_grad = jnp.sum(gain_sum[...].T, axis=0, keepdims=True)
    row_index = lax.broadcasted_iota(jnp.int32, (8, DIM), 0)
    for shard in range(shards):
        tile1[shard] = jnp.where(row_index == 0, loss_rows[shard], jnp.broadcast_to(gain_grad, (8, DIM)))
    stage1[me] = tile1[me]
    for step in OFFSETS:
        shard = peer(step)
        pltpu.make_async_remote_copy(
            tile1.at[shard], stage1.at[me], small_send.at[1], small_recv.at[1],
            device_id={"seq": shard}, device_id_type=MESH,
        ).start()

    def value_grad_block(turn, carry):
        block = row_of(turn)
        at = pl.multiple_of(block * 512, 512)
        got[SLOT[VALUE], pl.ds(at, 512), :] = by_rows(at, u3.at[:, DIM : 3 * DIM])
        for quarter in range(4):
            give(VALUE, block * 4 + quarter)
        return carry

    lax.fori_loop(0, shards // 4, value_grad_block, 0)

    hi_a, lo_a, hi_b, lo_b = (perm.at[:, at : at + 256] for at in range(0, 1024, 256))

    def prob_grad_block(turn, buffer):
        at = pl.multiple_of(pair_of(turn) * 256, 256)
        buffer[...] = dot_nt(v3[...], u3[pl.ds(at, 256), :])

    def score_grad_block(turn, buffer, high, low):
        at = pl.multiple_of(pair_of(turn) * 256, 256)
        shift = delta[0:1, pl.ds(at, 256)]
        for row in range(0, length, CHUNK):
            here = (slice(row, row + CHUNK), pl.ds(at, 256))
            weights = e_hi[here].astype(F32) + e_lo[here].astype(F32)
            hi, lo = split((buffer[row : row + CHUNK, :] - shift) * weights)
            high[row : row + CHUNK, :] = hi
            low[row : row + CHUNK, :] = lo
            e_hi[here] = hi
            e_lo[here] = lo

    def query_grad_block(turn, high, low):
        at = pl.multiple_of(pair_of(turn) * 256, 256)
        grad = by_columns(kt, high[...], low[...]) * SCALE
        for half in range(2):
            begin = pl.multiple_of(at + half * DIM, DIM)
            got[SLOT[QUERY], pl.ds(begin, DIM), :] = grad[:, half * DIM : (half + 1) * DIM].T

    give_queries = give_pair(QUERY)
    prob_grad_block(0, score_a)
    prob_grad_block(1, score_b)
    score_grad_block(0, score_a, hi_a, lo_a)

    def gradient_pair(pair, carry):
        turn = 2 * pair + 1
        prob_grad_block(turn + 1, score_a)
        score_grad_block(turn, score_b, hi_b, lo_b)
        query_grad_block(turn - 1, hi_a, lo_a)
        prob_grad_block(turn + 2, score_b)
        score_grad_block(turn + 1, score_a, hi_a, lo_a)
        query_grad_block(turn, hi_b, lo_b)
        give_queries(turn - 1)
        give_queries(turn)
        return carry

    last = shards // 2 - 1
    lax.fori_loop(0, last // 2, gradient_pair, 0)
    score_grad_block(last, score_b, hi_b, lo_b)
    query_grad_block(last - 1, hi_a, lo_a)
    query_grad_block(last, hi_b, lo_b)
    give_queries(last - 1)
    give_queries(last)

    wait_small(1, stage1, shards - 1)
    loss = jnp.zeros((1, DIM), F32)
    for shard in range(shards):
        loss = loss + stage1[shard, 0:1, :]
    excess = jnp.maximum(0.5 * loss / WIDTH - meta[REF : REF + 1, :], 0.0)
    hit = lax.broadcasted_iota(jnp.int32, (DIM, DIM), 0).astype(F32) == meta[BUCKET : BUCKET + 1, :]
    sums = lax.dot_general(
        jnp.where(row_index == 0, jnp.broadcast_to(excess, (8, DIM)), 1.0), jnp.where(hit, 1.0, 0.0),
        (((1,), (1,)), ((), ())), precision=HIGHEST, preferred_element_type=F32,
    )
    for shard in range(shards):
        tile2[shard : shard + 1, :] = stage1[shard, 1:2, :]
    tile2[shards : shards + 8, :] = sums
    tile2[shards + 2 : shards + 4, :] = meta[EMB : EMB + 2, :]
    stage2[sample] = tile2[...]
    for turn in range(1, copies):
        other = lax.rem(sample + turn, copies)
        pltpu.make_async_remote_copy(
            tile2, stage2.at[sample], small_send.at[2], small_recv.at[2],
            device_id={"dp": other}, device_id_type=MESH,
        ).start()

    def key_grad_block(turn, carry):
        block = row_of(turn)
        at = pl.multiple_of(block * 512, 512)
        got[SLOT[KEY], pl.ds(at, 512), :] = by_rows(at, q3.at[:, DIM : 3 * DIM]) * (1.0 / LOG2E)
        for quarter in range(4):
            give(KEY, block * 4 + quarter)
        return carry

    lax.fori_loop(0, shards // 4, key_grad_block, 0)

    if copies > 1:
        wait_small(2, stage2, copies - 1)
    sums = jnp.zeros((8, DIM), F32)
    for other in range(copies):
        sums = sums + stage2[other, shards : shards + 8, :]
    tile3[...] = sums
    stage3[me] = sums
    for step in OFFSETS:
        pltpu.make_async_remote_copy(
            tile3, stage3.at[me], small_send.at[3], small_recv.at[3],
            device_id={"seq": peer(step)}, device_id_type=MESH,
        ).start()

    by_sample = jnp.concatenate(
        [
            jnp.concatenate([stage2[other, row : row + 1, :] for row in (shards + 2, shards + 3)], axis=1)
            for other in range(copies)
        ],
        axis=0,
    )
    by_frequency = by_sample.T
    for head in range(shards):
        gains = jnp.concatenate([stage2[other, head : head + 1, :] for other in range(copies)], axis=0)
        weight_out[:, head * DIM : (head + 1) * DIM] = lax.dot_general(
            by_frequency, gains, (((1,), (0,)), ((), ())), precision=HIGHEST, preferred_element_type=F32
        )
    wait_small(3, stage3, shards - 1)
    sums = jnp.zeros((8, DIM), F32)
    for shard in range(shards):
        sums = sums + stage3[shard]
    mean = sums[0:1, :] / jnp.maximum(sums[1:2, :], 1.0)
    updated = meta[MIX : MIX + 1, :] * (1.0 + RATE * mean)
    updated = jnp.where(lane < BUCKETS, updated, 0.0)
    mixture = BUCKETS * updated / jnp.sum(updated, axis=1, keepdims=True)
    mix_out[...] = mixture[:, :BUCKETS]

    others = (shards - 1) * DIM
    for part in (KEY, QUERY, VALUE, AIM):
        sent = got.at[part, pl.ds(0, others), :]
        pltpu.make_async_copy(sent, sent, send_sem.at[part]).wait()
        sent = got.at[SLOT[part], pl.ds(0, others), :]
        pltpu.make_async_copy(sent, sent, back_send.at[part]).wait()
        base = att_out if part == AIM else grad_out
        landed = base.at[:, PART_COLUMN[part] : PART_COLUMN[part] + WIDTH]
        pltpu.make_async_copy(landed, landed, back_recv.at[part]).wait()
    wait_small_send(0, meta_all, shards - 1)
    wait_small_send(1, stage1, shards - 1)
    if copies > 1:
        wait_small_send(2, stage2, copies - 1)
    wait_small_send(3, stage3, shards - 1)


def body(reader_rows, reader_targets, dest_pos, bucket_ids, ref_loss, timesteps, mod_weight, mixture_old):
    shards, copies = lax.axis_size("seq"), lax.axis_size("dp")
    length = shards * DIM
    half = FREQ_DIM // 2
    frequency = np.exp(-math.log(10000.0) * np.arange(half) / half).astype(np.float32)[None, :]
    any_spec = pl.BlockSpec(memory_space=pl.ANY)
    vmem_spec = pl.BlockSpec(memory_space=pltpu.VMEM)
    dma = pltpu.SemaphoreType.DMA
    smem_spec = pl.BlockSpec(memory_space=pltpu.SMEM)
    attended, grads, weight_grad, mixture = pl.pallas_call(
        functools.partial(kernel, shards, copies),
        out_shape=(
            pltpu.VMEM((DIM, WIDTH), F32),
            pltpu.VMEM((DIM, 3 * WIDTH), F32),
            pltpu.VMEM((FREQ_DIM, WIDTH), F32),
            jax.ShapeDtypeStruct((1, BUCKETS), F32),
        ),
        in_specs=[any_spec, any_spec, vmem_spec, vmem_spec, vmem_spec, smem_spec, smem_spec, vmem_spec, any_spec],
        out_specs=(vmem_spec, vmem_spec, vmem_spec, vmem_spec),
        scratch_shapes=[
            pltpu.VMEM((8, DIM), F32),
            pltpu.VMEM((shards, 8, DIM), F32),
            pltpu.VMEM((4, length, DIM), F32),
            pltpu.VMEM((FREQ_DIM, DIM), F32),
            pltpu.VMEM((length, length), BF16),
            pltpu.VMEM((length, 2 * DIM), BF16),
            pltpu.VMEM((length, 3 * DIM), BF16),
            pltpu.VMEM((2 * DIM, length), BF16),
            pltpu.VMEM((length, 3 * DIM), BF16),
            pltpu.VMEM((length, 3 * DIM), BF16),
            pltpu.VMEM((2 * DIM, length), BF16),
            pltpu.VMEM((length, 3 * DIM), BF16),
            pltpu.VMEM((length, length), BF16),
            pltpu.VMEM((length, length), BF16),
            pltpu.VMEM((DIM, length), F32),
            pltpu.VMEM((8, length), F32),
            pltpu.VMEM((8, length), F32),
            pltpu.VMEM((DIM, DIM), F32),
            pltpu.VMEM((length, 256), F32),
            pltpu.VMEM((length, 256), F32),
            pltpu.VMEM((shards, 8, DIM), F32),
            pltpu.VMEM((shards, 8, DIM), F32),
            pltpu.VMEM((shards, 8, DIM), F32),
            pltpu.VMEM((copies, shards + 8, DIM), F32),
            pltpu.VMEM((shards + 8, DIM), F32),
            pltpu.VMEM((shards, 8, DIM), F32),
            pltpu.VMEM((8, DIM), F32),
            dma((4,)), dma((4,)), dma((4,)), dma((4,)), dma((4,)), dma((4,)), dma,
        ],
        compiler_params=pltpu.CompilerParams(
            collective_id=0, has_side_effects=True, vmem_limit_bytes=56 * 1024 * 1024
        ),
        name="attend",
    )(reader_rows[0], reader_targets[0], dest_pos, bucket_ids, ref_loss, timesteps, mixture_old, frequency, mod_weight)
    return attended[None], grads[None], weight_grad, mixture[0]


def solution(mesh):
    return jax.shard_map(
        body,
        mesh=mesh,
        in_specs=(
            P("dp", "seq", None), P("dp", "seq", None), P("dp", "seq"), P("dp", "seq"),
            P("dp", "seq"), P("dp"), P(), P(),
        ),
        out_specs=(P("dp", "seq", None), P("dp", "seq", None), P(), P()),
        check_vma=False,
    )
```

```python
import functools
import math

import jax
import jax.numpy as jnp
import numpy as np
from jax import lax
from jax.experimental import pallas as pl
from jax.experimental.pallas import tpu as pltpu
from jax.sharding import PartitionSpec as P

HEADS = 16
DIM = 128
FREQ_DIM = 256
BUCKETS = 16
WIDTH = HEADS * DIM
RATE = 10.0
CHUNK = 64
LOG2E = 1.4426950408889634
SCALE = DIM ** (-0.5)
MESH = pl.DeviceIdType.MESH
HIGHEST = lax.Precision.HIGHEST
BF16 = jnp.bfloat16
F32 = jnp.float32

OFFSETS = (
    (0, 1), (1, 0), (0, -1), (-1, 0), (1, 1), (-1, -1), (1, -1), (-1, 1),
    (0, 2), (2, 0), (1, 2), (2, 1), (-1, 2), (2, -1), (2, 2),
)
POS, WEIGHT, BUCKET, REF, EMB, MIX = 0, 1, 2, 3, 4, 6
KEY, QUERY, VALUE, AIM = 0, 1, 2, 3
SLOT = {AIM: KEY, VALUE: QUERY, QUERY: VALUE, KEY: AIM}
PART_COLUMN = {KEY: WIDTH, QUERY: 0, VALUE: 2 * WIDTH, AIM: 0}


def split(x):
    hi = x.astype(BF16)
    return hi, (x - hi.astype(F32)).astype(BF16)


def dot(a, b):
    return lax.dot_general(a, b, (((1,), (0,)), ((), ())), preferred_element_type=F32)


def dot_nt(a, b):
    return lax.dot_general(a, b, (((1,), (1,)), ((), ())), preferred_element_type=F32)


def kernel(
    shards, copies, rows, aims, places, buckets, ref_row, steps, old, frequency, mod_w,
    att_out, grad_out, weight_out, mix_out,
    meta, meta_all, got, mod_buf, perm, cat, k3, kt, q3, v3, vt, u3, e_hi, e_lo, head_out, inv_sum, delta,
    gain_sum, score_a, score_b, loss_rows, stage1, tile1, stage2, tile2, stage3, tile3,
    send_sem, recv_sem, back_send, back_recv, small_send, small_recv, mod_sem,
):
    length = shards * DIM
    me = lax.axis_index("seq")
    sample = lax.axis_index("dp")
    my_z, my_y = me // 4, lax.rem(me, 4)

    side = 1 - 2 * lax.rem(sample, 2)

    def peer(step):
        return lax.rem(my_z + side * step[0] + 4, 4) * 4 + lax.rem(my_y + side * step[1] + 4, 4)

    barrier = pltpu.get_barrier_semaphore()
    for step in OFFSETS:
        pl.semaphore_signal(barrier, inc=1, device_id={"seq": peer(step)}, device_id_type=MESH)
    for turn in range(1, copies):
        other = lax.rem(sample + turn, copies)
        pl.semaphore_signal(barrier, inc=1, device_id={"dp": other}, device_id_type=MESH)

    meta[POS : POS + 1, :] = places[...].astype(F32)
    bucket_row = buckets[...]
    lane = lax.broadcasted_iota(jnp.int32, (1, DIM), 1)
    weight_row = jnp.zeros((1, DIM), F32)
    old_row = jnp.zeros((1, DIM), F32)
    for bucket in range(BUCKETS):
        weight_row = weight_row + jnp.where(bucket_row == bucket, old[bucket], 0.0)
        old_row = old_row + jnp.where(lane == bucket, old[bucket], 0.0)
    meta[WEIGHT : WEIGHT + 1, :] = weight_row
    meta[BUCKET : BUCKET + 1, :] = bucket_row.astype(F32)
    meta[REF : REF + 1, :] = ref_row[...]
    angles = steps[0].astype(F32) * frequency[...]
    for row, wave in ((EMB, jnp.cos(angles)), (EMB + 1, jnp.sin(angles))):
        meta[row : row + 1, :] = wave / (1.0 + jnp.exp(-wave))
    meta[MIX : MIX + 1, :] = old_row
    meta[MIX + 1 : MIX + 2, :] = jnp.zeros((1, DIM), F32)
    pl.semaphore_wait(barrier, shards - 1 + copies - 1)

    meta_all[me] = meta[...]
    for step in OFFSETS:
        pltpu.make_async_remote_copy(
            meta, meta_all.at[me], small_send.at[0], small_recv.at[0],
            device_id={"seq": peer(step)}, device_id_type=MESH,
        ).start()
    mod_copy = pltpu.make_async_copy(
        mod_w.at[:, pl.ds(pl.multiple_of(me * DIM, DIM), DIM)], mod_buf, mod_sem
    )
    mod_copy.start()

    def source(part, head):
        base = aims if part == AIM else rows
        return base.at[:, pl.ds(pl.multiple_of(PART_COLUMN[part] + head * DIM, DIM), DIM)]

    def landing(part):
        return got.at[part, pl.ds(pl.multiple_of(me * DIM, DIM), DIM), :]

    def send(part):
        pltpu.make_async_copy(source(part, me), landing(part), recv_sem.at[part]).start()
        for step in OFFSETS:
            head = peer(step)
            pltpu.make_async_remote_copy(
                source(part, head), landing(part), send_sem.at[part], recv_sem.at[part],
                device_id={"seq": head}, device_id_type=MESH,
            ).start()

    def wait_sent(part):
        sent = got.at[part, pl.ds(0, (shards - 1) * DIM), :]
        pltpu.make_async_copy(sent, sent, send_sem.at[part]).wait()

    send(KEY)
    send(QUERY)

    def wait_small(stage, buffer, count):
        pltpu.make_async_copy(buffer.at[pl.ds(0, count)], buffer.at[pl.ds(0, count)], small_recv.at[stage]).wait()

    def wait_small_send(stage, buffer, count):
        pltpu.make_async_copy(buffer.at[pl.ds(0, count)], buffer.at[pl.ds(0, count)], small_send.at[stage]).wait()

    mod_copy.wait()
    embedding = jnp.concatenate([meta[EMB : EMB + 1, :], meta[EMB + 1 : EMB + 2, :]], axis=1)
    embedding = jnp.broadcast_to(embedding, (8, FREQ_DIM))
    gain_row = 1.0 + lax.dot_general(
        embedding, mod_buf[...], (((1,), (0,)), ((), ())), precision=HIGHEST, preferred_element_type=F32
    )
    gain = jnp.broadcast_to(gain_row[0:1, :], (DIM, DIM)).T

    wait_small(0, meta_all, shards - 1)

    def perm_block(block, carry):
        at = pl.multiple_of(block * 256, 256)
        place = (lax.broadcasted_iota(jnp.int32, (256, DIM), 0) + at).astype(F32)
        for shard in range(shards):
            hit = place == meta_all[shard, POS : POS + 1, :]
            perm[pl.ds(at, 256), shard * DIM : (shard + 1) * DIM] = jnp.where(hit, 1.0, 0.0).astype(BF16)
        return carry

    lax.fori_loop(0, length // 256, perm_block, 0)

    def pipeline(count, make, use, finish=None):
        def both(at, last):
            make(at + 1, score_b)
            use(at, score_a)
            if not last:
                make(at + 2, score_a)
            use(at + 1, score_b)
            if finish is not None:
                finish(at)
                finish(at + 1)

        def one(pair, carry):
            both(2 * pair, False)
            return carry

        make(0, score_a)
        lax.fori_loop(0, count // 2 - 1, one, 0)
        both(count - 2, True)

    def arrive(part, factor):
        pltpu.make_async_copy(got.at[part], got.at[part], recv_sem.at[part]).wait()

        def one(block, carry):
            at = pl.multiple_of(block * 256, 256)
            hi, lo = split(got[part, pl.ds(at, 256), :] * factor)
            cat[pl.ds(at, 256), 0:DIM] = hi
            cat[pl.ds(at, 256), DIM : 2 * DIM] = lo
            return carry

        lax.fori_loop(0, length // 256, one, 0)

    def reorder(part, factor, into, transposed):
        arrive(part, factor)

        def make(block, buffer):
            at = pl.multiple_of(block * 512, 512)
            buffer[0:512, :] = dot(perm[pl.ds(at, 512), :], cat[...])

        def use(block, buffer):
            at = pl.multiple_of(block * 512, 512)
            placed = buffer[0:512, :]
            hi, lo = placed[:, :DIM].astype(BF16), placed[:, DIM:].astype(BF16)
            into[pl.ds(at, 512), 0:DIM] = hi
            into[pl.ds(at, 512), DIM : 2 * DIM] = hi if part == QUERY else lo
            into[pl.ds(at, 512), 2 * DIM : 3 * DIM] = lo if part == QUERY else hi
            if transposed is not None:
                hi, lo = split((placed[:, :DIM] + placed[:, DIM:]).T)
                transposed[0:DIM, pl.ds(at, 512)] = hi
                transposed[DIM : 2 * DIM, pl.ds(at, 512)] = lo

        pipeline(length // 512, make, use)

    def by_columns(left, high, low):
        full = dot(left[...], high)
        return full[:DIM] + full[DIM:] + dot(left[0:DIM, :], low)

    def by_rows(at, right):
        full = dot(e_hi[pl.ds(at, 512), :], right[...])
        return full[:, :DIM] + full[:, DIM:] + dot(e_lo[pl.ds(at, 512), :], right[:, 0:DIM])

    wait_sent(KEY)
    send(VALUE)
    reorder(KEY, 1.0, k3, kt)
    wait_sent(QUERY)
    send(AIM)
    reorder(QUERY, SCALE * LOG2E, q3, None)

    def score_block(block, buffer):
        at = pl.multiple_of(block * 256, 256)
        buffer[...] = dot_nt(k3[...], q3[pl.ds(at, 256), :])

    def softmax_block(block, buffer):
        at = pl.multiple_of(block * 256, 256)
        top = jnp.full((8, 256), -jnp.inf, F32)
        for row in range(0, length, CHUNK):
            top = jnp.maximum(top, jnp.max(buffer[row : row + CHUNK, :].reshape(CHUNK // 8, 8, 256), axis=0))
        top = jnp.max(top, axis=0, keepdims=True)
        sums = jnp.zeros((8, 256), F32)
        for row in range(0, length, CHUNK):
            weights = jnp.exp2(buffer[row : row + CHUNK, :] - top)
            sums = sums + jnp.sum(weights.reshape(CHUNK // 8, 8, 256), axis=0)
            hi, lo = split(weights)
            e_hi[row : row + CHUNK, pl.ds(at, 256)] = hi
            e_lo[row : row + CHUNK, pl.ds(at, 256)] = lo
        inv_sum[:, pl.ds(at, 256)] = jnp.broadcast_to(1.0 / jnp.sum(sums, axis=0, keepdims=True), (8, 256))

    pipeline(length // 256, score_block, softmax_block)

    def target(part):
        base = att_out if part == AIM else grad_out
        return base.at[:, pl.ds(pl.multiple_of(PART_COLUMN[part] + me * DIM, DIM), DIM)]

    def give(part, shard):
        block = got.at[SLOT[part], pl.ds(pl.multiple_of(shard * DIM, DIM), DIM), :]

        @pl.when(shard != me)
        def _():
            pltpu.make_async_remote_copy(
                block, target(part), back_send.at[part], back_recv.at[part],
                device_id={"seq": shard}, device_id_type=MESH,
            ).start()

        @pl.when(shard == me)
        def _():
            pltpu.make_async_copy(block, target(part), back_recv.at[part]).start()

    def pair_of(turn):
        return lax.rem(my_z + 6 + side * (turn // 2), 4) * 2 + lax.rem(my_y // 2 + 1 + lax.rem(turn, 2), 2)

    def row_of(turn):
        return lax.rem(my_z + 6 + side * turn, 4)

    reorder(VALUE, 1.0, v3, vt)

    def output_block(turn, buffer):
        at = pl.multiple_of(pair_of(turn) * 256, 256)
        buffer[0:DIM, :] = by_columns(vt, e_hi[:, pl.ds(at, 256)], e_lo[:, pl.ds(at, 256)])

    def attended_block(turn, buffer):
        at = pl.multiple_of(pair_of(turn) * 256, 256)
        out = buffer[0:DIM, :] * inv_sum[0:1, pl.ds(at, 256)]
        head_out[:, pl.ds(at, 256)] = out
        for half in range(2):
            begin = pl.multiple_of(at + half * DIM, DIM)
            got[SLOT[AIM], pl.ds(begin, DIM), :] = (gain * out[:, half * DIM : (half + 1) * DIM]).T

    def give_pair(part):
        def finish(turn):
            for half in range(2):
                give(part, pair_of(turn) * 2 + half)

        return finish

    pipeline(shards // 2, output_block, attended_block, give_pair(AIM))

    arrive(AIM, 1.0)

    def aim_block(block, buffer):
        at = pl.multiple_of(block * 512, 512)
        buffer[0:512, :] = dot(perm[pl.ds(at, 512), :], cat[...])

    gain_sum[...] = jnp.zeros((DIM, DIM), F32)

    def upstream_block(block, buffer):
        at = pl.multiple_of(block * 512, 512)
        placed = buffer[0:512, :]
        aim = placed[:, :DIM] + placed[:, DIM:]
        total = jnp.zeros((DIM, DIM), F32)
        for quarter in range(4):
            shard = block * 4 + quarter
            begin = pl.multiple_of(at + quarter * DIM, DIM)
            out = head_out[:, pl.ds(begin, DIM)]
            gap = gain * out - aim[quarter * DIM : (quarter + 1) * DIM, :].T
            loss_rows[shard] = jnp.broadcast_to(jnp.sum(gap * gap, axis=0, keepdims=True), (8, DIM))
            up_a = gap * meta_all[shard, WEIGHT : WEIGHT + 1, :]
            total = total + up_a * out
            up = gain * up_a * inv_sum[0:1, pl.ds(begin, DIM)]
            delta[:, pl.ds(begin, DIM)] = jnp.broadcast_to(jnp.sum(up * out, axis=0, keepdims=True), (8, DIM))
            hi, lo = split(up.T)
            u3[pl.ds(begin, DIM), 0:DIM] = hi
            u3[pl.ds(begin, DIM), DIM : 2 * DIM] = hi
            u3[pl.ds(begin, DIM), 2 * DIM : 3 * DIM] = lo
        gain_sum[...] += total

    pipeline(length // 512, aim_block, upstream_block)

    gain_grad = jnp.sum(gain_sum[...].T, axis=0, keepdims=True)
    row_index = lax.broadcasted_iota(jnp.int32, (8, DIM), 0)
    for shard in range(shards):
        tile1[shard] = jnp.where(row_index == 0, loss_rows[shard], jnp.broadcast_to(gain_grad, (8, DIM)))
    stage1[me] = tile1[me]
    for step in OFFSETS:
        shard = peer(step)
        pltpu.make_async_remote_copy(
            tile1.at[shard], stage1.at[me], small_send.at[1], small_recv.at[1],
            device_id={"seq": shard}, device_id_type=MESH,
        ).start()

    def value_grad_block(turn, carry):
        block = row_of(turn)
        at = pl.multiple_of(block * 512, 512)
        got[SLOT[VALUE], pl.ds(at, 512), :] = by_rows(at, u3.at[:, DIM : 3 * DIM])
        for quarter in range(4):
            give(VALUE, block * 4 + quarter)
        return carry

    lax.fori_loop(0, shards // 4, value_grad_block, 0)

    hi_a, lo_a, hi_b, lo_b = (perm.at[:, at : at + 256] for at in range(0, 1024, 256))

    def prob_grad_block(turn, buffer):
        at = pl.multiple_of(pair_of(turn) * 256, 256)
        buffer[...] = dot_nt(v3[...], u3[pl.ds(at, 256), :])

    def score_grad_block(turn, buffer, high, low):
        at = pl.multiple_of(pair_of(turn) * 256, 256)
        shift = delta[0:1, pl.ds(at, 256)]
        for row in range(0, length, CHUNK):
            here = (slice(row, row + CHUNK), pl.ds(at, 256))
            weights = e_hi[here].astype(F32) + e_lo[here].astype(F32)
            hi, lo = split((buffer[row : row + CHUNK, :] - shift) * weights)
            high[row : row + CHUNK, :] = hi
            low[row : row + CHUNK, :] = lo
            e_hi[here] = hi
            e_lo[here] = lo

    def query_grad_block(turn, high, low):
        at = pl.multiple_of(pair_of(turn) * 256, 256)
        grad = by_columns(kt, high[...], low[...]) * SCALE
        for half in range(2):
            begin = pl.multiple_of(at + half * DIM, DIM)
            got[SLOT[QUERY], pl.ds(begin, DIM), :] = grad[:, half * DIM : (half + 1) * DIM].T

    give_queries = give_pair(QUERY)
    prob_grad_block(0, score_a)
    prob_grad_block(1, score_b)
    score_grad_block(0, score_a, hi_a, lo_a)

    def gradient_pair(pair, carry):
        turn = 2 * pair + 1
        prob_grad_block(turn + 1, score_a)
        score_grad_block(turn, score_b, hi_b, lo_b)
        query_grad_block(turn - 1, hi_a, lo_a)
        prob_grad_block(turn + 2, score_b)
        score_grad_block(turn + 1, score_a, hi_a, lo_a)
        query_grad_block(turn, hi_b, lo_b)
        give_queries(turn - 1)
        give_queries(turn)
        return carry

    last = shards // 2 - 1
    lax.fori_loop(0, last // 2, gradient_pair, 0)
    score_grad_block(last, score_b, hi_b, lo_b)
    query_grad_block(last - 1, hi_a, lo_a)
    query_grad_block(last, hi_b, lo_b)
    give_queries(last - 1)
    give_queries(last)

    wait_small(1, stage1, shards - 1)
    loss = jnp.zeros((1, DIM), F32)
    for shard in range(shards):
        loss = loss + stage1[shard, 0:1, :]
    excess = jnp.maximum(0.5 * loss / WIDTH - meta[REF : REF + 1, :], 0.0)
    hit = lax.broadcasted_iota(jnp.int32, (DIM, DIM), 0).astype(F32) == meta[BUCKET : BUCKET + 1, :]
    sums = lax.dot_general(
        jnp.where(row_index == 0, jnp.broadcast_to(excess, (8, DIM)), 1.0), jnp.where(hit, 1.0, 0.0),
        (((1,), (1,)), ((), ())), precision=HIGHEST, preferred_element_type=F32,
    )
    for shard in range(shards):
        tile2[shard : shard + 1, :] = stage1[shard, 1:2, :]
    tile2[shards : shards + 8, :] = sums
    tile2[shards + 2 : shards + 4, :] = meta[EMB : EMB + 2, :]
    stage2[sample] = tile2[...]
    for turn in range(1, copies):
        other = lax.rem(sample + turn, copies)
        pltpu.make_async_remote_copy(
            tile2, stage2.at[sample], small_send.at[2], small_recv.at[2],
            device_id={"dp": other}, device_id_type=MESH,
        ).start()

    def key_grad_block(turn, carry):
        block = row_of(turn)
        at = pl.multiple_of(block * 512, 512)
        got[SLOT[KEY], pl.ds(at, 512), :] = by_rows(at, q3.at[:, DIM : 3 * DIM]) * (1.0 / LOG2E)
        for quarter in range(4):
            give(KEY, block * 4 + quarter)
        return carry

    lax.fori_loop(0, shards // 4, key_grad_block, 0)

    if copies > 1:
        wait_small(2, stage2, copies - 1)
    sums = jnp.zeros((8, DIM), F32)
    for other in range(copies):
        sums = sums + stage2[other, shards : shards + 8, :]
    tile3[...] = sums
    stage3[me] = sums
    for step in OFFSETS:
        pltpu.make_async_remote_copy(
            tile3, stage3.at[me], small_send.at[3], small_recv.at[3],
            device_id={"seq": peer(step)}, device_id_type=MESH,
        ).start()

    by_sample = jnp.concatenate(
        [
            jnp.concatenate([stage2[other, row : row + 1, :] for row in (shards + 2, shards + 3)], axis=1)
            for other in range(copies)
        ],
        axis=0,
    )
    by_frequency = by_sample.T
    for head in range(shards):
        gains = jnp.concatenate([stage2[other, head : head + 1, :] for other in range(copies)], axis=0)
        weight_out[:, head * DIM : (head + 1) * DIM] = lax.dot_general(
            by_frequency, gains, (((1,), (0,)), ((), ())), precision=HIGHEST, preferred_element_type=F32
        )
    wait_small(3, stage3, shards - 1)
    sums = jnp.zeros((8, DIM), F32)
    for shard in range(shards):
        sums = sums + stage3[shard]
    mean = sums[0:1, :] / jnp.maximum(sums[1:2, :], 1.0)
    updated = meta[MIX : MIX + 1, :] * (1.0 + RATE * mean)
    updated = jnp.where(lane < BUCKETS, updated, 0.0)
    mixture = BUCKETS * updated / jnp.sum(updated, axis=1, keepdims=True)
    mix_out[...] = mixture[:, :BUCKETS]

    others = (shards - 1) * DIM
    for part in (KEY, QUERY, VALUE, AIM):
        if part in (VALUE, AIM):
            wait_sent(part)
        sent = got.at[SLOT[part], pl.ds(0, others), :]
        pltpu.make_async_copy(sent, sent, back_send.at[part]).wait()
        base = att_out if part == AIM else grad_out
        landed = base.at[:, PART_COLUMN[part] : PART_COLUMN[part] + WIDTH]
        pltpu.make_async_copy(landed, landed, back_recv.at[part]).wait()
    wait_small_send(0, meta_all, shards - 1)
    wait_small_send(1, stage1, shards - 1)
    if copies > 1:
        wait_small_send(2, stage2, copies - 1)
    wait_small_send(3, stage3, shards - 1)


def move_out(*refs):
    count = len(refs) // 2
    sources, outputs, sems = refs[:count], refs[count : 2 * count], refs[-1]
    moves = []
    for source, output in zip(sources, outputs):
        pieces = 4 if source.shape[0] >= DIM else 1
        rows = source.shape[0] // pieces
        for piece in range(pieces):
            part = pl.ds(piece * rows, rows)
            moves.append(pltpu.make_async_copy(source.at[part], output.at[part], sems.at[len(moves)]))
    for move in moves:
        move.start()
    for move in moves:
        move.wait()


def body(reader_rows, reader_targets, dest_pos, bucket_ids, ref_loss, timesteps, mod_weight, mixture_old):
    shards, copies = lax.axis_size("seq"), lax.axis_size("dp")
    length = shards * DIM
    half = FREQ_DIM // 2
    frequency = np.exp(-math.log(10000.0) * np.arange(half) / half).astype(np.float32)[None, :]
    any_spec = pl.BlockSpec(memory_space=pl.ANY)
    vmem_spec = pl.BlockSpec(memory_space=pltpu.VMEM)
    dma = pltpu.SemaphoreType.DMA
    smem_spec = pl.BlockSpec(memory_space=pltpu.SMEM)
    attended, grads, weight_grad, mixture = pl.pallas_call(
        functools.partial(kernel, shards, copies),
        out_shape=(
            pltpu.VMEM((DIM, WIDTH), F32),
            pltpu.VMEM((DIM, 3 * WIDTH), F32),
            pltpu.VMEM((FREQ_DIM, WIDTH), F32),
            pltpu.VMEM((1, BUCKETS), F32),
        ),
        in_specs=[any_spec, any_spec, vmem_spec, vmem_spec, vmem_spec, smem_spec, smem_spec, vmem_spec, any_spec],
        out_specs=(vmem_spec, vmem_spec, vmem_spec, vmem_spec),
        scratch_shapes=[
            pltpu.VMEM((8, DIM), F32),
            pltpu.VMEM((shards, 8, DIM), F32),
            pltpu.VMEM((4, length, DIM), F32),
            pltpu.VMEM((FREQ_DIM, DIM), F32),
            pltpu.VMEM((length, length), BF16),
            pltpu.VMEM((length, 2 * DIM), BF16),
            pltpu.VMEM((length, 3 * DIM), BF16),
            pltpu.VMEM((2 * DIM, length), BF16),
            pltpu.VMEM((length, 3 * DIM), BF16),
            pltpu.VMEM((length, 3 * DIM), BF16),
            pltpu.VMEM((2 * DIM, length), BF16),
            pltpu.VMEM((length, 3 * DIM), BF16),
            pltpu.VMEM((length, length), BF16),
            pltpu.VMEM((length, length), BF16),
            pltpu.VMEM((DIM, length), F32),
            pltpu.VMEM((8, length), F32),
            pltpu.VMEM((8, length), F32),
            pltpu.VMEM((DIM, DIM), F32),
            pltpu.VMEM((length, 256), F32),
            pltpu.VMEM((length, 256), F32),
            pltpu.VMEM((shards, 8, DIM), F32),
            pltpu.VMEM((shards, 8, DIM), F32),
            pltpu.VMEM((shards, 8, DIM), F32),
            pltpu.VMEM((copies, shards + 8, DIM), F32),
            pltpu.VMEM((shards + 8, DIM), F32),
            pltpu.VMEM((shards, 8, DIM), F32),
            pltpu.VMEM((8, DIM), F32),
            dma((4,)), dma((4,)), dma((4,)), dma((4,)), dma((4,)), dma((4,)), dma,
        ],
        compiler_params=pltpu.CompilerParams(
            collective_id=0, has_side_effects=True, vmem_limit_bytes=56 * 1024 * 1024
        ),
        name="attend",
    )(reader_rows[0], reader_targets[0], dest_pos, bucket_ids, ref_loss, timesteps, mixture_old, frequency, mod_weight)
    results = (attended, grads, weight_grad, mixture)
    attended, grads, weight_grad, mixture = pl.pallas_call(
        move_out,
        out_shape=tuple(jax.ShapeDtypeStruct(item.shape, F32) for item in results),
        in_specs=[vmem_spec] * 4,
        out_specs=(any_spec,) * 4,
        scratch_shapes=[dma((13,))],
        name="move_out",
    )(*results)
    return attended[None], grads[None], weight_grad, mixture[0]


def solution(mesh):
    return jax.shard_map(
        body,
        mesh=mesh,
        in_specs=(
            P("dp", "seq", None), P("dp", "seq", None), P("dp", "seq"), P("dp", "seq"),
            P("dp", "seq"), P("dp"), P(), P(),
        ),
        out_specs=(P("dp", "seq", None), P("dp", "seq", None), P(), P()),
        check_vma=False,
    )
```

```python
import functools
import math

import jax
import jax.numpy as jnp
import numpy as np
from jax import lax
from jax.experimental import pallas as pl
from jax.experimental.pallas import tpu as pltpu
from jax.sharding import PartitionSpec as P

HEADS = 16
DIM = 128
FREQ_DIM = 256
BUCKETS = 16
WIDTH = HEADS * DIM
RATE = 10.0
CHUNK = 64
LOG2E = 1.4426950408889634
SCALE = DIM ** (-0.5)
MESH = pl.DeviceIdType.MESH
HIGHEST = lax.Precision.HIGHEST
BF16 = jnp.bfloat16
F32 = jnp.float32

POS, WEIGHT, BUCKET, REF, EMB, MIX = 0, 1, 2, 3, 4, 6
KEY, QUERY, VALUE, AIM = 0, 1, 2, 3
SLOT = {AIM: KEY, VALUE: QUERY, QUERY: VALUE, KEY: AIM}
PART_COLUMN = {KEY: WIDTH, QUERY: 0, VALUE: 2 * WIDTH, AIM: 0}


def split(x):
    hi = x.astype(BF16)
    return hi, (x - hi.astype(F32)).astype(BF16)


def dot(a, b):
    return lax.dot_general(a, b, (((1,), (0,)), ((), ())), preferred_element_type=F32)


def dot_nt(a, b):
    return lax.dot_general(a, b, (((1,), (1,)), ((), ())), preferred_element_type=F32)


def kernel(
    shards, copies, rows, aims, places, buckets, ref_row, steps, old, frequency, mod_w,
    att_out, grad_out, weight_out, mix_out,
    meta, meta_all, got, mod_buf, perm, cat, k3, kt, q3, v3, vt, u3, e_hi, e_lo, head_out, inv_sum, delta,
    gain_sum, score_a, score_b, loss_rows, stage1, tile1, stage2, tile2, stage3, tile3,
    send_sem, recv_sem, back_send, back_recv, small_send, small_recv, mod_sem,
):
    length = shards * DIM
    me = lax.axis_index("seq")
    sample = lax.axis_index("dp")
    my_z, my_y = me // 4, lax.rem(me, 4)

    side = 1 - 2 * lax.rem(sample, 2)

    def shard_at(slot):
        along, shift = lax.rem(slot, 4), slot // 4
        return lax.rem(my_z + 4 + side * along, 4) * 4 + lax.rem(my_y + 8 + side * (along + shift), 4)

    peers = [shard_at(slot) for slot in range(1, shards)]

    barrier = pltpu.get_barrier_semaphore()
    for peer in peers:
        pl.semaphore_signal(barrier, inc=1, device_id={"seq": peer}, device_id_type=MESH)
    for turn in range(1, copies):
        other = lax.rem(sample + turn, copies)
        pl.semaphore_signal(barrier, inc=1, device_id={"dp": other}, device_id_type=MESH)

    meta[POS : POS + 1, :] = places[...].astype(F32)
    bucket_row = buckets[...]
    lane = lax.broadcasted_iota(jnp.int32, (1, DIM), 1)
    weight_row = jnp.zeros((1, DIM), F32)
    old_row = jnp.zeros((1, DIM), F32)
    for bucket in range(BUCKETS):
        weight_row = weight_row + jnp.where(bucket_row == bucket, old[bucket], 0.0)
        old_row = old_row + jnp.where(lane == bucket, old[bucket], 0.0)
    meta[WEIGHT : WEIGHT + 1, :] = weight_row
    meta[BUCKET : BUCKET + 1, :] = bucket_row.astype(F32)
    meta[REF : REF + 1, :] = ref_row[...]
    angles = steps[0].astype(F32) * frequency[...]
    for row, wave in ((EMB, jnp.cos(angles)), (EMB + 1, jnp.sin(angles))):
        meta[row : row + 1, :] = wave / (1.0 + jnp.exp(-wave))
    meta[MIX : MIX + 1, :] = old_row
    meta[MIX + 1 : MIX + 2, :] = jnp.zeros((1, DIM), F32)
    pl.semaphore_wait(barrier, shards - 1 + copies - 1)

    meta_all[me] = meta[...]
    for peer in peers:
        pltpu.make_async_remote_copy(
            meta, meta_all.at[me], small_send.at[0], small_recv.at[0],
            device_id={"seq": peer}, device_id_type=MESH,
        ).start()
    mod_copy = pltpu.make_async_copy(
        mod_w.at[:, pl.ds(pl.multiple_of(me * DIM, DIM), DIM)], mod_buf, mod_sem
    )
    mod_copy.start()

    def source(part, head):
        base = aims if part == AIM else rows
        return base.at[:, pl.ds(pl.multiple_of(PART_COLUMN[part] + head * DIM, DIM), DIM)]

    def landing(part):
        return got.at[part, pl.ds(pl.multiple_of(me * DIM, DIM), DIM), :]

    def send(part):
        pltpu.make_async_copy(source(part, me), landing(part), recv_sem.at[part]).start()
        for peer in peers:
            pltpu.make_async_remote_copy(
                source(part, peer), landing(part), send_sem.at[part], recv_sem.at[part],
                device_id={"seq": peer}, device_id_type=MESH,
            ).start()

    def wait_sent(part):
        sent = got.at[part, pl.ds(0, (shards - 1) * DIM), :]
        pltpu.make_async_copy(sent, sent, send_sem.at[part]).wait()

    send(KEY)
    send(QUERY)

    def wait_small(stage, buffer, count):
        pltpu.make_async_copy(buffer.at[pl.ds(0, count)], buffer.at[pl.ds(0, count)], small_recv.at[stage]).wait()

    def wait_small_send(stage, buffer, count):
        pltpu.make_async_copy(buffer.at[pl.ds(0, count)], buffer.at[pl.ds(0, count)], small_send.at[stage]).wait()

    mod_copy.wait()
    embedding = jnp.concatenate([meta[EMB : EMB + 1, :], meta[EMB + 1 : EMB + 2, :]], axis=1)
    embedding = jnp.broadcast_to(embedding, (8, FREQ_DIM))
    gain_row = 1.0 + lax.dot_general(
        embedding, mod_buf[...], (((1,), (0,)), ((), ())), precision=HIGHEST, preferred_element_type=F32
    )
    gain = jnp.broadcast_to(gain_row[0:1, :], (DIM, DIM)).T

    wait_small(0, meta_all, shards - 1)

    def perm_block(block, carry):
        at = pl.multiple_of(block * 256, 256)
        inside = lax.broadcasted_iota(jnp.int32, (DIM, DIM), 0)
        place = jnp.concatenate([inside + shard_at(2 * block + half) * DIM for half in range(2)], axis=0).astype(F32)
        for shard in range(shards):
            hit = place == meta_all[shard, POS : POS + 1, :]
            perm[pl.ds(at, 256), shard * DIM : (shard + 1) * DIM] = jnp.where(hit, 1.0, 0.0).astype(BF16)
        return carry

    lax.fori_loop(0, length // 256, perm_block, 0)

    def pipeline(count, make, use, finish=None):
        def both(at, last):
            make(at + 1, score_b)
            use(at, score_a)
            if not last:
                make(at + 2, score_a)
            use(at + 1, score_b)
            if finish is not None:
                finish(at)
                finish(at + 1)

        def one(pair, carry):
            both(2 * pair, False)
            return carry

        make(0, score_a)
        lax.fori_loop(0, count // 2 - 1, one, 0)
        both(count - 2, True)

    def arrive(part, factor):
        pltpu.make_async_copy(got.at[part], got.at[part], recv_sem.at[part]).wait()

        def one(block, carry):
            at = pl.multiple_of(block * 256, 256)
            hi, lo = split(got[part, pl.ds(at, 256), :] * factor)
            cat[pl.ds(at, 256), 0:DIM] = hi
            cat[pl.ds(at, 256), DIM : 2 * DIM] = lo
            return carry

        lax.fori_loop(0, length // 256, one, 0)

    def reorder(part, factor, into, transposed):
        arrive(part, factor)

        def make(block, buffer):
            at = pl.multiple_of(block * 512, 512)
            buffer[0:512, :] = dot(perm[pl.ds(at, 512), :], cat[...])

        def use(block, buffer):
            at = pl.multiple_of(block * 512, 512)
            placed = buffer[0:512, :]
            hi, lo = placed[:, :DIM].astype(BF16), placed[:, DIM:].astype(BF16)
            into[pl.ds(at, 512), 0:DIM] = hi
            into[pl.ds(at, 512), DIM : 2 * DIM] = hi if part == QUERY else lo
            into[pl.ds(at, 512), 2 * DIM : 3 * DIM] = lo if part == QUERY else hi
            if transposed is not None:
                hi, lo = split((placed[:, :DIM] + placed[:, DIM:]).T)
                transposed[0:DIM, pl.ds(at, 512)] = hi
                transposed[DIM : 2 * DIM, pl.ds(at, 512)] = lo

        pipeline(length // 512, make, use)

    def by_columns(left, high, low):
        full = dot(left[...], high)
        return full[:DIM] + full[DIM:] + dot(left[0:DIM, :], low)

    def by_rows(at, right):
        full = dot(e_hi[pl.ds(at, 512), :], right[...])
        return full[:, :DIM] + full[:, DIM:] + dot(e_lo[pl.ds(at, 512), :], right[:, 0:DIM])

    wait_sent(KEY)
    send(VALUE)
    reorder(KEY, 1.0, k3, kt)
    wait_sent(QUERY)
    send(AIM)
    reorder(QUERY, SCALE * LOG2E, q3, None)

    def score_block(block, buffer):
        at = pl.multiple_of(block * 256, 256)
        buffer[...] = dot_nt(k3[...], q3[pl.ds(at, 256), :])

    def softmax_block(block, buffer):
        at = pl.multiple_of(block * 256, 256)
        top = jnp.full((8, 256), -jnp.inf, F32)
        for row in range(0, length, CHUNK):
            top = jnp.maximum(top, jnp.max(buffer[row : row + CHUNK, :].reshape(CHUNK // 8, 8, 256), axis=0))
        top = jnp.max(top, axis=0, keepdims=True)
        sums = jnp.zeros((8, 256), F32)
        for row in range(0, length, CHUNK):
            weights = jnp.exp2(buffer[row : row + CHUNK, :] - top)
            sums = sums + jnp.sum(weights.reshape(CHUNK // 8, 8, 256), axis=0)
            hi, lo = split(weights)
            e_hi[row : row + CHUNK, pl.ds(at, 256)] = hi
            e_lo[row : row + CHUNK, pl.ds(at, 256)] = lo
        inv_sum[:, pl.ds(at, 256)] = jnp.broadcast_to(1.0 / jnp.sum(sums, axis=0, keepdims=True), (8, 256))

    pipeline(length // 256, score_block, softmax_block)

    def target(part):
        base = att_out if part == AIM else grad_out
        return base.at[:, pl.ds(pl.multiple_of(PART_COLUMN[part] + me * DIM, DIM), DIM)]

    def give(part, slot):
        block = got.at[SLOT[part], pl.ds(pl.multiple_of(slot * DIM, DIM), DIM), :]
        shard = shard_at(slot)

        @pl.when(shard != me)
        def _():
            pltpu.make_async_remote_copy(
                block, target(part), back_send.at[part], back_recv.at[part],
                device_id={"seq": shard}, device_id_type=MESH,
            ).start()

        @pl.when(shard == me)
        def _():
            pltpu.make_async_copy(block, target(part), back_recv.at[part]).start()

    reorder(VALUE, 1.0, v3, vt)

    def output_block(turn, buffer):
        at = pl.multiple_of(turn * 256, 256)
        buffer[0:DIM, :] = by_columns(vt, e_hi[:, pl.ds(at, 256)], e_lo[:, pl.ds(at, 256)])

    def attended_block(turn, buffer):
        at = pl.multiple_of(turn * 256, 256)
        out = buffer[0:DIM, :] * inv_sum[0:1, pl.ds(at, 256)]
        head_out[:, pl.ds(at, 256)] = out
        for half in range(2):
            begin = pl.multiple_of(at + half * DIM, DIM)
            got[SLOT[AIM], pl.ds(begin, DIM), :] = (gain * out[:, half * DIM : (half + 1) * DIM]).T

    def give_pair(part):
        def finish(turn):
            for half in range(2):
                give(part, turn * 2 + half)

        return finish

    pipeline(shards // 2, output_block, attended_block, give_pair(AIM))

    arrive(AIM, 1.0)

    def aim_block(block, buffer):
        at = pl.multiple_of(block * 512, 512)
        buffer[0:512, :] = dot(perm[pl.ds(at, 512), :], cat[...])

    gain_sum[...] = jnp.zeros((DIM, DIM), F32)

    def upstream_block(block, buffer):
        at = pl.multiple_of(block * 512, 512)
        placed = buffer[0:512, :]
        aim = placed[:, :DIM] + placed[:, DIM:]
        total = jnp.zeros((DIM, DIM), F32)
        for quarter in range(4):
            slot = block * 4 + quarter
            begin = pl.multiple_of(at + quarter * DIM, DIM)
            out = head_out[:, pl.ds(begin, DIM)]
            gap = gain * out - aim[quarter * DIM : (quarter + 1) * DIM, :].T
            loss_rows[slot] = jnp.broadcast_to(jnp.sum(gap * gap, axis=0, keepdims=True), (8, DIM))
            up_a = gap * meta_all[shard_at(slot), WEIGHT : WEIGHT + 1, :]
            total = total + up_a * out
            up = gain * up_a * inv_sum[0:1, pl.ds(begin, DIM)]
            delta[:, pl.ds(begin, DIM)] = jnp.broadcast_to(jnp.sum(up * out, axis=0, keepdims=True), (8, DIM))
            hi, lo = split(up.T)
            u3[pl.ds(begin, DIM), 0:DIM] = hi
            u3[pl.ds(begin, DIM), DIM : 2 * DIM] = hi
            u3[pl.ds(begin, DIM), 2 * DIM : 3 * DIM] = lo
        gain_sum[...] += total

    pipeline(length // 512, aim_block, upstream_block)

    gain_grad = jnp.sum(gain_sum[...].T, axis=0, keepdims=True)
    row_index = lax.broadcasted_iota(jnp.int32, (8, DIM), 0)
    for slot in range(shards):
        tile1[slot] = jnp.where(row_index == 0, loss_rows[slot], jnp.broadcast_to(gain_grad, (8, DIM)))
    stage1[me] = tile1[0]
    for slot, peer in enumerate(peers):
        pltpu.make_async_remote_copy(
            tile1.at[slot + 1], stage1.at[me], small_send.at[1], small_recv.at[1],
            device_id={"seq": peer}, device_id_type=MESH,
        ).start()

    def value_grad_block(turn, carry):
        block = turn
        at = pl.multiple_of(block * 512, 512)
        got[SLOT[VALUE], pl.ds(at, 512), :] = by_rows(at, u3.at[:, DIM : 3 * DIM])
        for quarter in range(4):
            give(VALUE, block * 4 + quarter)
        return carry

    lax.fori_loop(0, shards // 4, value_grad_block, 0)

    hi_a, lo_a, hi_b, lo_b = (perm.at[:, at : at + 256] for at in range(0, 1024, 256))

    def prob_grad_block(turn, buffer):
        at = pl.multiple_of(turn * 256, 256)
        buffer[...] = dot_nt(v3[...], u3[pl.ds(at, 256), :])

    def score_grad_block(turn, buffer, high, low):
        at = pl.multiple_of(turn * 256, 256)
        shift = delta[0:1, pl.ds(at, 256)]
        for row in range(0, length, CHUNK):
            here = (slice(row, row + CHUNK), pl.ds(at, 256))
            weights = e_hi[here].astype(F32) + e_lo[here].astype(F32)
            hi, lo = split((buffer[row : row + CHUNK, :] - shift) * weights)
            high[row : row + CHUNK, :] = hi
            low[row : row + CHUNK, :] = lo
            e_hi[here] = hi
            e_lo[here] = lo

    def query_grad_block(turn, high, low):
        at = pl.multiple_of(turn * 256, 256)
        grad = by_columns(kt, high[...], low[...]) * SCALE
        for half in range(2):
            begin = pl.multiple_of(at + half * DIM, DIM)
            got[SLOT[QUERY], pl.ds(begin, DIM), :] = grad[:, half * DIM : (half + 1) * DIM].T

    give_queries = give_pair(QUERY)
    prob_grad_block(0, score_a)
    prob_grad_block(1, score_b)
    score_grad_block(0, score_a, hi_a, lo_a)

    def gradient_pair(pair, carry):
        turn = 2 * pair + 1
        prob_grad_block(turn + 1, score_a)
        score_grad_block(turn, score_b, hi_b, lo_b)
        query_grad_block(turn - 1, hi_a, lo_a)
        prob_grad_block(turn + 2, score_b)
        score_grad_block(turn + 1, score_a, hi_a, lo_a)
        query_grad_block(turn, hi_b, lo_b)
        give_queries(turn - 1)
        give_queries(turn)
        return carry

    last = shards // 2 - 1
    lax.fori_loop(0, last // 2, gradient_pair, 0)
    score_grad_block(last, score_b, hi_b, lo_b)
    query_grad_block(last - 1, hi_a, lo_a)
    query_grad_block(last, hi_b, lo_b)
    give_queries(last - 1)
    give_queries(last)

    wait_small(1, stage1, shards - 1)
    loss = jnp.zeros((1, DIM), F32)
    for shard in range(shards):
        loss = loss + stage1[shard, 0:1, :]
    excess = jnp.maximum(0.5 * loss / WIDTH - meta[REF : REF + 1, :], 0.0)
    hit = lax.broadcasted_iota(jnp.int32, (DIM, DIM), 0).astype(F32) == meta[BUCKET : BUCKET + 1, :]
    sums = lax.dot_general(
        jnp.where(row_index == 0, jnp.broadcast_to(excess, (8, DIM)), 1.0), jnp.where(hit, 1.0, 0.0),
        (((1,), (1,)), ((), ())), precision=HIGHEST, preferred_element_type=F32,
    )
    for shard in range(shards):
        tile2[shard : shard + 1, :] = stage1[shard, 1:2, :]
    tile2[shards : shards + 8, :] = sums
    tile2[shards + 2 : shards + 4, :] = meta[EMB : EMB + 2, :]
    stage2[sample] = tile2[...]
    for turn in range(1, copies):
        other = lax.rem(sample + turn, copies)
        pltpu.make_async_remote_copy(
            tile2, stage2.at[sample], small_send.at[2], small_recv.at[2],
            device_id={"dp": other}, device_id_type=MESH,
        ).start()

    def key_grad_block(turn, carry):
        block = turn
        at = pl.multiple_of(block * 512, 512)
        got[SLOT[KEY], pl.ds(at, 512), :] = by_rows(at, q3.at[:, DIM : 3 * DIM]) * (1.0 / LOG2E)
        for quarter in range(4):
            give(KEY, block * 4 + quarter)
        return carry

    lax.fori_loop(0, shards // 4, key_grad_block, 0)

    if copies > 1:
        wait_small(2, stage2, copies - 1)
    sums = jnp.zeros((8, DIM), F32)
    for other in range(copies):
        sums = sums + stage2[other, shards : shards + 8, :]
    tile3[...] = sums
    stage3[me] = sums
    for peer in peers:
        pltpu.make_async_remote_copy(
            tile3, stage3.at[me], small_send.at[3], small_recv.at[3],
            device_id={"seq": peer}, device_id_type=MESH,
        ).start()

    by_sample = jnp.concatenate(
        [
            jnp.concatenate([stage2[other, row : row + 1, :] for row in (shards + 2, shards + 3)], axis=1)
            for other in range(copies)
        ],
        axis=0,
    )
    by_frequency = by_sample.T
    for head in range(shards):
        gains = jnp.concatenate([stage2[other, head : head + 1, :] for other in range(copies)], axis=0)
        weight_out[:, head * DIM : (head + 1) * DIM] = lax.dot_general(
            by_frequency, gains, (((1,), (0,)), ((), ())), precision=HIGHEST, preferred_element_type=F32
        )
    wait_small(3, stage3, shards - 1)
    sums = jnp.zeros((8, DIM), F32)
    for shard in range(shards):
        sums = sums + stage3[shard]
    mean = sums[0:1, :] / jnp.maximum(sums[1:2, :], 1.0)
    updated = meta[MIX : MIX + 1, :] * (1.0 + RATE * mean)
    updated = jnp.where(lane < BUCKETS, updated, 0.0)
    mixture = BUCKETS * updated / jnp.sum(updated, axis=1, keepdims=True)
    mix_out[...] = mixture[:, :BUCKETS]

    others = (shards - 1) * DIM
    for part in (KEY, QUERY, VALUE, AIM):
        if part in (VALUE, AIM):
            wait_sent(part)
        sent = got.at[SLOT[part], pl.ds(0, others), :]
        pltpu.make_async_copy(sent, sent, back_send.at[part]).wait()
        base = att_out if part == AIM else grad_out
        landed = base.at[:, PART_COLUMN[part] : PART_COLUMN[part] + WIDTH]
        pltpu.make_async_copy(landed, landed, back_recv.at[part]).wait()
    wait_small_send(0, meta_all, shards - 1)
    wait_small_send(1, stage1, shards - 1)
    if copies > 1:
        wait_small_send(2, stage2, copies - 1)
    wait_small_send(3, stage3, shards - 1)


def move_out(*refs):
    count = len(refs) // 2
    sources, outputs, sems = refs[:count], refs[count : 2 * count], refs[-1]
    moves = []
    for source, output in zip(sources, outputs):
        pieces = 4 if source.shape[0] >= DIM else 1
        rows = source.shape[0] // pieces
        for piece in range(pieces):
            part = pl.ds(piece * rows, rows)
            moves.append(pltpu.make_async_copy(source.at[part], output.at[part], sems.at[len(moves)]))
    for move in moves:
        move.start()
    for move in moves:
        move.wait()


def body(reader_rows, reader_targets, dest_pos, bucket_ids, ref_loss, timesteps, mod_weight, mixture_old):
    shards, copies = lax.axis_size("seq"), lax.axis_size("dp")
    length = shards * DIM
    half = FREQ_DIM // 2
    frequency = np.exp(-math.log(10000.0) * np.arange(half) / half).astype(np.float32)[None, :]
    any_spec = pl.BlockSpec(memory_space=pl.ANY)
    vmem_spec = pl.BlockSpec(memory_space=pltpu.VMEM)
    dma = pltpu.SemaphoreType.DMA
    smem_spec = pl.BlockSpec(memory_space=pltpu.SMEM)
    attended, grads, weight_grad, mixture = pl.pallas_call(
        functools.partial(kernel, shards, copies),
        out_shape=(
            pltpu.VMEM((DIM, WIDTH), F32),
            pltpu.VMEM((DIM, 3 * WIDTH), F32),
            pltpu.VMEM((FREQ_DIM, WIDTH), F32),
            pltpu.VMEM((1, BUCKETS), F32),
        ),
        in_specs=[any_spec, any_spec, vmem_spec, vmem_spec, vmem_spec, smem_spec, smem_spec, vmem_spec, any_spec],
        out_specs=(vmem_spec, vmem_spec, vmem_spec, vmem_spec),
        scratch_shapes=[
            pltpu.VMEM((8, DIM), F32),
            pltpu.VMEM((shards, 8, DIM), F32),
            pltpu.VMEM((4, length, DIM), F32),
            pltpu.VMEM((FREQ_DIM, DIM), F32),
            pltpu.VMEM((length, length), BF16),
            pltpu.VMEM((length, 2 * DIM), BF16),
            pltpu.VMEM((length, 3 * DIM), BF16),
            pltpu.VMEM((2 * DIM, length), BF16),
            pltpu.VMEM((length, 3 * DIM), BF16),
            pltpu.VMEM((length, 3 * DIM), BF16),
            pltpu.VMEM((2 * DIM, length), BF16),
            pltpu.VMEM((length, 3 * DIM), BF16),
            pltpu.VMEM((length, length), BF16),
            pltpu.VMEM((length, length), BF16),
            pltpu.VMEM((DIM, length), F32),
            pltpu.VMEM((8, length), F32),
            pltpu.VMEM((8, length), F32),
            pltpu.VMEM((DIM, DIM), F32),
            pltpu.VMEM((length, 256), F32),
            pltpu.VMEM((length, 256), F32),
            pltpu.VMEM((shards, 8, DIM), F32),
            pltpu.VMEM((shards, 8, DIM), F32),
            pltpu.VMEM((shards, 8, DIM), F32),
            pltpu.VMEM((copies, shards + 8, DIM), F32),
            pltpu.VMEM((shards + 8, DIM), F32),
            pltpu.VMEM((shards, 8, DIM), F32),
            pltpu.VMEM((8, DIM), F32),
            dma((4,)), dma((4,)), dma((4,)), dma((4,)), dma((4,)), dma((4,)), dma,
        ],
        compiler_params=pltpu.CompilerParams(
            collective_id=0, has_side_effects=True, vmem_limit_bytes=56 * 1024 * 1024
        ),
        name="attend",
    )(reader_rows[0], reader_targets[0], dest_pos, bucket_ids, ref_loss, timesteps, mixture_old, frequency, mod_weight)
    results = (attended, grads, weight_grad, mixture)
    attended, grads, weight_grad, mixture = pl.pallas_call(
        move_out,
        out_shape=tuple(jax.ShapeDtypeStruct(item.shape, F32) for item in results),
        in_specs=[vmem_spec] * 4,
        out_specs=(any_spec,) * 4,
        scratch_shapes=[dma((13,))],
        compiler_params=pltpu.CompilerParams(vmem_limit_bytes=1024 * 1024),
        name="move_out",
    )(*(pltpu.with_memory_space_constraint(item, pltpu.VMEM) for item in results))
    return attended[None], grads[None], weight_grad, mixture[0]


def solution(mesh):
    return jax.shard_map(
        body,
        mesh=mesh,
        in_specs=(
            P("dp", "seq", None), P("dp", "seq", None), P("dp", "seq"), P("dp", "seq"),
            P("dp", "seq"), P("dp"), P(), P(),
        ),
        out_specs=(P("dp", "seq", None), P("dp", "seq", None), P(), P()),
        check_vma=False,
    )
```

```python
import functools
import math

import jax
import jax.numpy as jnp
import numpy as np
from jax import lax
from jax.experimental import pallas as pl
from jax.experimental.pallas import tpu as pltpu
from jax.sharding import PartitionSpec as P

HEADS = 16
DIM = 128
FREQ_DIM = 256
BUCKETS = 16
WIDTH = HEADS * DIM
RATE = 10.0
CHUNK = 64
LOG2E = 1.4426950408889634
SCALE = DIM ** (-0.5)
MESH = pl.DeviceIdType.MESH
HIGHEST = lax.Precision.HIGHEST
BF16 = jnp.bfloat16
F32 = jnp.float32

POS, WEIGHT, BUCKET, REF, EMB, MIX = 0, 1, 2, 3, 4, 6
KEY, QUERY, VALUE, AIM = 0, 1, 2, 3
SLOT = {AIM: KEY, VALUE: QUERY, QUERY: VALUE, KEY: AIM}
PART_COLUMN = {KEY: WIDTH, QUERY: 0, VALUE: 2 * WIDTH, AIM: 0}


def split(x):
    hi = x.astype(BF16)
    return hi, (x - hi.astype(F32)).astype(BF16)


def dot(a, b):
    return lax.dot_general(a, b, (((1,), (0,)), ((), ())), preferred_element_type=F32)


def dot_nt(a, b):
    return lax.dot_general(a, b, (((1,), (1,)), ((), ())), preferred_element_type=F32)


def kernel(
    shards, copies, rows, aims, places_in, buckets_in, ref_in, steps_in, old_in, frequency_in, mod_w,
    att_out, grad_out, weight_out, mix_out,
    places, buckets, ref_row, frequency, steps, old, meta, meta_all, got, mod_buf, perm, cat, k3, kt, q3, v3, vt, u3, e_hi, e_lo, head_out, inv_sum, delta,
    gain_sum, score_a, score_b, loss_rows, stage1, tile1, stage2, tile2, stage3, tile3,
    send_sem, recv_sem, back_send, back_recv, small_send, small_recv, mod_sem, operand_sem,
):
    length = shards * DIM
    me = lax.axis_index("seq")
    sample = lax.axis_index("dp")
    my_z, my_y = me // 4, lax.rem(me, 4)

    side = 1 - 2 * lax.rem(sample, 2)

    def shard_at(slot):
        along, shift = lax.rem(slot, 4), slot // 4
        return lax.rem(my_z + 4 + side * along, 4) * 4 + lax.rem(my_y + 8 + side * (along + shift), 4)

    peers = [shard_at(slot) for slot in range(1, shards)]

    barrier = pltpu.get_barrier_semaphore()
    for peer in peers:
        pl.semaphore_signal(barrier, inc=1, device_id={"seq": peer}, device_id_type=MESH)
    for turn in range(1, copies):
        other = lax.rem(sample + turn, copies)
        pl.semaphore_signal(barrier, inc=1, device_id={"dp": other}, device_id_type=MESH)

    operands = [
        pltpu.make_async_copy(source, into, operand_sem.at[index])
        for index, (source, into) in enumerate(
            (
                (places_in, places), (buckets_in, buckets), (ref_in, ref_row), (frequency_in, frequency),
                (steps_in, steps), (old_in, old),
            )
        )
    ]
    for operand in operands:
        operand.start()
    mod_copy = pltpu.make_async_copy(
        mod_w.at[:, pl.ds(pl.multiple_of(me * DIM, DIM), DIM)], mod_buf, mod_sem
    )
    mod_copy.start()
    pl.semaphore_wait(barrier, shards - 1 + copies - 1)

    def source(part, head):
        base = aims if part == AIM else rows
        return base.at[:, pl.ds(pl.multiple_of(PART_COLUMN[part] + head * DIM, DIM), DIM)]

    def landing(part):
        return got.at[part, pl.ds(pl.multiple_of(me * DIM, DIM), DIM), :]

    def send(part):
        pltpu.make_async_copy(source(part, me), landing(part), recv_sem.at[part]).start()
        for peer in peers:
            pltpu.make_async_remote_copy(
                source(part, peer), landing(part), send_sem.at[part], recv_sem.at[part],
                device_id={"seq": peer}, device_id_type=MESH,
            ).start()

    def wait_sent(part):
        sent = got.at[part, pl.ds(0, (shards - 1) * DIM), :]
        pltpu.make_async_copy(sent, sent, send_sem.at[part]).wait()

    send(KEY)

    for operand in operands:
        operand.wait()
    meta[POS : POS + 1, :] = places[...].astype(F32)
    bucket_row = buckets[...]
    lane = lax.broadcasted_iota(jnp.int32, (1, DIM), 1)
    weight_row = jnp.zeros((1, DIM), F32)
    old_row = jnp.zeros((1, DIM), F32)
    for bucket in range(BUCKETS):
        weight_row = weight_row + jnp.where(bucket_row == bucket, old[bucket], 0.0)
        old_row = old_row + jnp.where(lane == bucket, old[bucket], 0.0)
    meta[WEIGHT : WEIGHT + 1, :] = weight_row
    meta[BUCKET : BUCKET + 1, :] = bucket_row.astype(F32)
    meta[REF : REF + 1, :] = ref_row[...]
    angles = steps[0].astype(F32) * frequency[...]
    for row, wave in ((EMB, jnp.cos(angles)), (EMB + 1, jnp.sin(angles))):
        meta[row : row + 1, :] = wave / (1.0 + jnp.exp(-wave))
    meta[MIX : MIX + 1, :] = old_row
    meta[MIX + 1 : MIX + 2, :] = jnp.zeros((1, DIM), F32)
    meta_all[me] = meta[...]
    for peer in peers:
        pltpu.make_async_remote_copy(
            meta.at[pl.ds(0, 2)], meta_all.at[me, pl.ds(0, 2)], small_send.at[0], small_recv.at[0],
            device_id={"seq": peer}, device_id_type=MESH,
        ).start()
    send(QUERY)

    def wait_small(sem, buffer, count, depth=2):
        taken = buffer.at[pl.ds(0, count), pl.ds(0, depth)]
        pltpu.make_async_copy(taken, taken, sem).wait()

    mod_copy.wait()
    embedding = jnp.concatenate([meta[EMB : EMB + 1, :], meta[EMB + 1 : EMB + 2, :]], axis=1)
    embedding = jnp.broadcast_to(embedding, (8, FREQ_DIM))
    gain_row = 1.0 + lax.dot_general(
        embedding, mod_buf[...], (((1,), (0,)), ((), ())), precision=HIGHEST, preferred_element_type=F32
    )
    gain = jnp.broadcast_to(gain_row[0:1, :], (DIM, DIM)).T

    wait_small(small_recv.at[0], meta_all, shards - 1)

    def perm_block(block, carry):
        at = pl.multiple_of(block * 256, 256)
        inside = lax.broadcasted_iota(jnp.int32, (DIM, DIM), 0)
        place = jnp.concatenate([inside + shard_at(2 * block + half) * DIM for half in range(2)], axis=0).astype(F32)
        for shard in range(shards):
            hit = place == meta_all[shard, POS : POS + 1, :]
            perm[pl.ds(at, 256), shard * DIM : (shard + 1) * DIM] = jnp.where(hit, 1.0, 0.0).astype(BF16)
        return carry

    lax.fori_loop(0, length // 256, perm_block, 0)

    def pipeline(count, make, use, finish=None):
        def both(at, last):
            make(at + 1, score_b)
            use(at, score_a)
            if not last:
                make(at + 2, score_a)
            use(at + 1, score_b)
            if finish is not None:
                finish(at)
                finish(at + 1)

        def one(pair, carry):
            both(2 * pair, False)
            return carry

        make(0, score_a)
        lax.fori_loop(0, count // 2 - 1, one, 0)
        both(count - 2, True)

    def arrive(part, factor):
        pltpu.make_async_copy(got.at[part], got.at[part], recv_sem.at[part]).wait()

        def one(block, carry):
            at = pl.multiple_of(block * 256, 256)
            hi, lo = split(got[part, pl.ds(at, 256), :] * factor)
            cat[pl.ds(at, 256), 0:DIM] = hi
            cat[pl.ds(at, 256), DIM : 2 * DIM] = lo
            return carry

        lax.fori_loop(0, length // 256, one, 0)

    def reorder(part, factor, into, transposed):
        arrive(part, factor)

        def make(block, buffer):
            at = pl.multiple_of(block * 512, 512)
            buffer[0:512, :] = dot(perm[pl.ds(at, 512), :], cat[...])

        def use(block, buffer):
            at = pl.multiple_of(block * 512, 512)
            placed = buffer[0:512, :]
            hi, lo = placed[:, :DIM].astype(BF16), placed[:, DIM:].astype(BF16)
            into[pl.ds(at, 512), 0:DIM] = hi
            into[pl.ds(at, 512), DIM : 2 * DIM] = hi if part == QUERY else lo
            into[pl.ds(at, 512), 2 * DIM : 3 * DIM] = lo if part == QUERY else hi
            if transposed is not None:
                hi, lo = split((placed[:, :DIM] + placed[:, DIM:]).T)
                transposed[0:DIM, pl.ds(at, 512)] = hi
                transposed[DIM : 2 * DIM, pl.ds(at, 512)] = lo

        pipeline(length // 512, make, use)

    def by_columns(left, high, low):
        full = dot(left[...], high)
        return full[:DIM] + full[DIM:] + dot(left[0:DIM, :], low)

    def by_rows(at, right):
        full = dot(e_hi[pl.ds(at, 512), :], right[...])
        return full[:, :DIM] + full[:, DIM:] + dot(e_lo[pl.ds(at, 512), :], right[:, 0:DIM])

    wait_sent(KEY)
    send(VALUE)
    reorder(KEY, 1.0, k3, kt)
    wait_sent(QUERY)
    send(AIM)
    reorder(QUERY, SCALE * LOG2E, q3, None)

    def score_block(block, buffer):
        at = pl.multiple_of(block * 256, 256)
        buffer[...] = dot_nt(k3[...], q3[pl.ds(at, 256), :])

    def softmax_block(block, buffer):
        at = pl.multiple_of(block * 256, 256)
        top = jnp.full((8, 256), -jnp.inf, F32)
        for row in range(0, length, CHUNK):
            top = jnp.maximum(top, jnp.max(buffer[row : row + CHUNK, :].reshape(CHUNK // 8, 8, 256), axis=0))
        top = jnp.max(top, axis=0, keepdims=True)
        sums = jnp.zeros((8, 256), F32)
        for row in range(0, length, CHUNK):
            weights = jnp.exp2(buffer[row : row + CHUNK, :] - top)
            sums = sums + jnp.sum(weights.reshape(CHUNK // 8, 8, 256), axis=0)
            hi, lo = split(weights)
            e_hi[row : row + CHUNK, pl.ds(at, 256)] = hi
            e_lo[row : row + CHUNK, pl.ds(at, 256)] = lo
        inv_sum[:, pl.ds(at, 256)] = jnp.broadcast_to(1.0 / jnp.sum(sums, axis=0, keepdims=True), (8, 256))

    pipeline(length // 256, score_block, softmax_block)

    def target(part):
        base = att_out if part == AIM else grad_out
        return base.at[:, pl.ds(pl.multiple_of(PART_COLUMN[part] + me * DIM, DIM), DIM)]

    def give(part, slot):
        block = got.at[SLOT[part], pl.ds(pl.multiple_of(slot * DIM, DIM), DIM), :]
        shard = shard_at(slot)

        @pl.when(shard != me)
        def _():
            pltpu.make_async_remote_copy(
                block, target(part), back_send.at[part], back_recv.at[part],
                device_id={"seq": shard}, device_id_type=MESH,
            ).start()

        @pl.when(shard == me)
        def _():
            pltpu.make_async_copy(block, target(part), back_recv.at[part]).start()

    reorder(VALUE, 1.0, v3, vt)

    def output_block(turn, buffer):
        at = pl.multiple_of(turn * 256, 256)
        buffer[0:DIM, :] = by_columns(vt, e_hi[:, pl.ds(at, 256)], e_lo[:, pl.ds(at, 256)])

    def attended_block(turn, buffer):
        at = pl.multiple_of(turn * 256, 256)
        out = buffer[0:DIM, :] * inv_sum[0:1, pl.ds(at, 256)]
        head_out[:, pl.ds(at, 256)] = out
        for half in range(2):
            begin = pl.multiple_of(at + half * DIM, DIM)
            got[SLOT[AIM], pl.ds(begin, DIM), :] = (gain * out[:, half * DIM : (half + 1) * DIM]).T

    def give_pair(part):
        def finish(turn):
            for half in range(2):
                give(part, turn * 2 + half)

        return finish

    pipeline(shards // 2, output_block, attended_block, give_pair(AIM))

    arrive(AIM, 1.0)

    def aim_block(block, buffer):
        at = pl.multiple_of(block * 512, 512)
        buffer[0:512, :] = dot(perm[pl.ds(at, 512), :], cat[...])

    gain_sum[...] = jnp.zeros((DIM, DIM), F32)

    def upstream_block(block, buffer):
        at = pl.multiple_of(block * 512, 512)
        placed = buffer[0:512, :]
        aim = placed[:, :DIM] + placed[:, DIM:]
        total = jnp.zeros((DIM, DIM), F32)
        for quarter in range(4):
            slot = block * 4 + quarter
            begin = pl.multiple_of(at + quarter * DIM, DIM)
            out = head_out[:, pl.ds(begin, DIM)]
            gap = gain * out - aim[quarter * DIM : (quarter + 1) * DIM, :].T
            loss_rows[slot] = jnp.broadcast_to(jnp.sum(gap * gap, axis=0, keepdims=True), (8, DIM))
            up_a = gap * meta_all[shard_at(slot), WEIGHT : WEIGHT + 1, :]
            total = total + up_a * out
            up = gain * up_a * inv_sum[0:1, pl.ds(begin, DIM)]
            delta[:, pl.ds(begin, DIM)] = jnp.broadcast_to(jnp.sum(up * out, axis=0, keepdims=True), (8, DIM))
            hi, lo = split(up.T)
            u3[pl.ds(begin, DIM), 0:DIM] = hi
            u3[pl.ds(begin, DIM), DIM : 2 * DIM] = hi
            u3[pl.ds(begin, DIM), 2 * DIM : 3 * DIM] = lo
        gain_sum[...] += total

    pipeline(length // 512, aim_block, upstream_block)

    gain_grad = jnp.sum(gain_sum[...].T, axis=0, keepdims=True)
    row_index = lax.broadcasted_iota(jnp.int32, (8, DIM), 0)
    for slot in range(shards):
        tile1[slot] = jnp.where(row_index == 0, loss_rows[slot], jnp.broadcast_to(gain_grad, (8, DIM)))
    stage1[me] = tile1[0]
    for slot, peer in enumerate(peers):
        pltpu.make_async_remote_copy(
            tile1.at[slot + 1, pl.ds(0, 2)], stage1.at[me, pl.ds(0, 2)], small_send.at[1], small_recv.at[1],
            device_id={"seq": peer}, device_id_type=MESH,
        ).start()

    def value_grad_block(turn, carry):
        block = turn
        at = pl.multiple_of(block * 512, 512)
        got[SLOT[VALUE], pl.ds(at, 512), :] = by_rows(at, u3.at[:, DIM : 3 * DIM])
        for quarter in range(4):
            give(VALUE, block * 4 + quarter)
        return carry

    lax.fori_loop(0, shards // 4, value_grad_block, 0)

    def exchange_losses():
        wait_small(small_recv.at[1], stage1, shards - 1)
        loss = jnp.zeros((1, DIM), F32)
        for shard in range(shards):
            loss = loss + stage1[shard, 0:1, :]
        excess = jnp.maximum(0.5 * loss / WIDTH - meta[REF : REF + 1, :], 0.0)
        hit = lax.broadcasted_iota(jnp.int32, (DIM, DIM), 0).astype(F32) == meta[BUCKET : BUCKET + 1, :]
        sums = lax.dot_general(
            jnp.where(row_index == 0, jnp.broadcast_to(excess, (8, DIM)), 1.0), jnp.where(hit, 1.0, 0.0),
            (((1,), (1,)), ((), ())), precision=HIGHEST, preferred_element_type=F32,
        )
        for shard in range(shards):
            tile2[shard : shard + 1, :] = stage1[shard, 1:2, :]
        tile2[shards : shards + 2, :] = sums[0:2, :]
        tile2[shards + 2 : shards + 4, :] = meta[EMB : EMB + 2, :]
        stage2[sample] = tile2[...]
        for turn in range(1, copies):
            other = lax.rem(sample + turn, copies)
            pltpu.make_async_remote_copy(
                tile2.at[pl.ds(0, shards + 4)], stage2.at[sample, pl.ds(0, shards + 4)], small_send.at[2], small_recv.at[2],
                device_id={"dp": other}, device_id_type=MESH,
            ).start()

    hi_a, lo_a, hi_b, lo_b = (perm.at[:, at : at + 256] for at in range(0, 1024, 256))

    def prob_grad_block(turn, buffer):
        at = pl.multiple_of(turn * 256, 256)
        buffer[...] = dot_nt(v3[...], u3[pl.ds(at, 256), :])

    def score_grad_block(turn, buffer, high, low):
        at = pl.multiple_of(turn * 256, 256)
        shift = delta[0:1, pl.ds(at, 256)]
        for row in range(0, length, CHUNK):
            here = (slice(row, row + CHUNK), pl.ds(at, 256))
            weights = e_hi[here].astype(F32) + e_lo[here].astype(F32)
            hi, lo = split((buffer[row : row + CHUNK, :] - shift) * weights)
            high[row : row + CHUNK, :] = hi
            low[row : row + CHUNK, :] = lo
            e_hi[here] = hi
            e_lo[here] = lo

    def query_grad_block(turn, high, low):
        at = pl.multiple_of(turn * 256, 256)
        grad = by_columns(kt, high[...], low[...]) * SCALE
        for half in range(2):
            begin = pl.multiple_of(at + half * DIM, DIM)
            got[SLOT[QUERY], pl.ds(begin, DIM), :] = grad[:, half * DIM : (half + 1) * DIM].T

    give_queries = give_pair(QUERY)
    prob_grad_block(0, score_a)
    prob_grad_block(1, score_b)
    score_grad_block(0, score_a, hi_a, lo_a)

    def gradient_pair(pair, carry):
        turn = 2 * pair + 1
        prob_grad_block(turn + 1, score_a)
        score_grad_block(turn, score_b, hi_b, lo_b)
        query_grad_block(turn - 1, hi_a, lo_a)
        prob_grad_block(turn + 2, score_b)
        score_grad_block(turn + 1, score_a, hi_a, lo_a)
        query_grad_block(turn, hi_b, lo_b)
        give_queries(turn - 1)
        give_queries(turn)
        pl.when(pair == 1)(exchange_losses)
        return carry

    last = shards // 2 - 1
    lax.fori_loop(0, last // 2, gradient_pair, 0)
    score_grad_block(last, score_b, hi_b, lo_b)
    query_grad_block(last - 1, hi_a, lo_a)
    query_grad_block(last, hi_b, lo_b)
    give_queries(last - 1)
    give_queries(last)

    def exchange_sums():
        if copies > 1:
            wait_small(small_recv.at[2], stage2, copies - 1, shards + 4)
        sums = jnp.zeros((2, DIM), F32)
        for other in range(copies):
            sums = sums + stage2[other, shards : shards + 2, :]
        tile3[0:2, :] = sums
        stage3[me, 0:2, :] = sums
        for peer in peers:
            pltpu.make_async_remote_copy(
                tile3.at[pl.ds(0, 2)], stage3.at[me, pl.ds(0, 2)], small_send.at[3], small_recv.at[3],
                device_id={"seq": peer}, device_id_type=MESH,
            ).start()

    def key_grad_block(turn, carry):
        block = turn
        at = pl.multiple_of(block * 512, 512)
        got[SLOT[KEY], pl.ds(at, 512), :] = by_rows(at, q3.at[:, DIM : 3 * DIM]) * (1.0 / LOG2E)
        for quarter in range(4):
            give(KEY, block * 4 + quarter)
        pl.when(turn == 1)(exchange_sums)
        return carry

    lax.fori_loop(0, shards // 4, key_grad_block, 0)

    by_sample = jnp.concatenate(
        [
            jnp.concatenate([stage2[other, row : row + 1, :] for row in (shards + 2, shards + 3)], axis=1)
            for other in range(copies)
        ],
        axis=0,
    )
    by_frequency = by_sample.T
    for head in range(shards):
        gains = jnp.concatenate([stage2[other, head : head + 1, :] for other in range(copies)], axis=0)
        weight_out[:, head * DIM : (head + 1) * DIM] = lax.dot_general(
            by_frequency, gains, (((1,), (0,)), ((), ())), precision=HIGHEST, preferred_element_type=F32
        )
    wait_small(small_recv.at[3], stage3, shards - 1)
    sums = jnp.zeros((2, DIM), F32)
    for shard in range(shards):
        sums = sums + stage3[shard, 0:2, :]
    mean = sums[0:1, :] / jnp.maximum(sums[1:2, :], 1.0)
    updated = meta[MIX : MIX + 1, :] * (1.0 + RATE * mean)
    updated = jnp.where(lane < BUCKETS, updated, 0.0)
    mixture = BUCKETS * updated / jnp.sum(updated, axis=1, keepdims=True)
    mix_out[...] = mixture[:, :BUCKETS]

    others = (shards - 1) * DIM
    for part in (KEY, QUERY, VALUE, AIM):
        if part in (VALUE, AIM):
            wait_sent(part)
        sent = got.at[SLOT[part], pl.ds(0, others), :]
        pltpu.make_async_copy(sent, sent, back_send.at[part]).wait()
        base = att_out if part == AIM else grad_out
        landed = base.at[:, PART_COLUMN[part] : PART_COLUMN[part] + WIDTH]
        pltpu.make_async_copy(landed, landed, back_recv.at[part]).wait()
    wait_small(small_send.at[0], meta_all, shards - 1)
    wait_small(small_send.at[1], stage1, shards - 1)
    if copies > 1:
        wait_small(small_send.at[2], stage2, copies - 1, shards + 4)
    wait_small(small_send.at[3], stage3, shards - 1)


def move_out(*refs):
    count = len(refs) // 2
    sources, outputs, sems = refs[:count], refs[count : 2 * count], refs[-1]
    moves = []
    for source, output in zip(sources, outputs):
        pieces = 4 if source.shape[0] >= DIM else 1
        rows = source.shape[0] // pieces
        for piece in range(pieces):
            part = pl.ds(piece * rows, rows)
            moves.append(pltpu.make_async_copy(source.at[part], output.at[part], sems.at[len(moves)]))
    for move in moves:
        move.start()
    for move in moves:
        move.wait()


def body(reader_rows, reader_targets, dest_pos, bucket_ids, ref_loss, timesteps, mod_weight, mixture_old):
    shards, copies = lax.axis_size("seq"), lax.axis_size("dp")
    length = shards * DIM
    half = FREQ_DIM // 2
    frequency = np.exp(-math.log(10000.0) * np.arange(half) / half).astype(np.float32)[None, :]
    any_spec = pl.BlockSpec(memory_space=pl.ANY)
    vmem_spec = pl.BlockSpec(memory_space=pltpu.VMEM)
    dma = pltpu.SemaphoreType.DMA
    attended, grads, weight_grad, mixture = pl.pallas_call(
        functools.partial(kernel, shards, copies),
        out_shape=(
            pltpu.VMEM((DIM, WIDTH), F32),
            pltpu.VMEM((DIM, 3 * WIDTH), F32),
            pltpu.VMEM((FREQ_DIM, WIDTH), F32),
            pltpu.VMEM((1, BUCKETS), F32),
        ),
        in_specs=[any_spec] * 9,
        out_specs=(vmem_spec, vmem_spec, vmem_spec, vmem_spec),
        scratch_shapes=[
            pltpu.VMEM((1, DIM), jnp.int32),
            pltpu.VMEM((1, DIM), jnp.int32),
            pltpu.VMEM((1, DIM), F32),
            pltpu.VMEM((1, DIM), F32),
            pltpu.SMEM((1,), jnp.int32),
            pltpu.SMEM((BUCKETS,), F32),
            pltpu.VMEM((8, DIM), F32),
            pltpu.VMEM((shards, 8, DIM), F32),
            pltpu.VMEM((4, length, DIM), F32),
            pltpu.VMEM((FREQ_DIM, DIM), F32),
            pltpu.VMEM((length, length), BF16),
            pltpu.VMEM((length, 2 * DIM), BF16),
            pltpu.VMEM((length, 3 * DIM), BF16),
            pltpu.VMEM((2 * DIM, length), BF16),
            pltpu.VMEM((length, 3 * DIM), BF16),
            pltpu.VMEM((length, 3 * DIM), BF16),
            pltpu.VMEM((2 * DIM, length), BF16),
            pltpu.VMEM((length, 3 * DIM), BF16),
            pltpu.VMEM((length, length), BF16),
            pltpu.VMEM((length, length), BF16),
            pltpu.VMEM((DIM, length), F32),
            pltpu.VMEM((8, length), F32),
            pltpu.VMEM((8, length), F32),
            pltpu.VMEM((DIM, DIM), F32),
            pltpu.VMEM((length, 256), F32),
            pltpu.VMEM((length, 256), F32),
            pltpu.VMEM((shards, 8, DIM), F32),
            pltpu.VMEM((shards, 8, DIM), F32),
            pltpu.VMEM((shards, 8, DIM), F32),
            pltpu.VMEM((copies, shards + 8, DIM), F32),
            pltpu.VMEM((shards + 8, DIM), F32),
            pltpu.VMEM((shards, 8, DIM), F32),
            pltpu.VMEM((8, DIM), F32),
            dma((4,)), dma((4,)), dma((4,)), dma((4,)), dma((4,)), dma((4,)), dma, dma((6,)),
        ],
        compiler_params=pltpu.CompilerParams(
            collective_id=0, has_side_effects=True, vmem_limit_bytes=56 * 1024 * 1024
        ),
        name="attend",
    )(reader_rows[0], reader_targets[0], dest_pos, bucket_ids, ref_loss, timesteps, mixture_old, frequency, mod_weight)
    results = (attended, grads, weight_grad, mixture)
    attended, grads, weight_grad, mixture = pl.pallas_call(
        move_out,
        out_shape=tuple(jax.ShapeDtypeStruct(item.shape, F32) for item in results),
        in_specs=[vmem_spec] * 4,
        out_specs=(any_spec,) * 4,
        scratch_shapes=[dma((13,))],
        compiler_params=pltpu.CompilerParams(vmem_limit_bytes=1024 * 1024),
        name="move_out",
    )(*(pltpu.with_memory_space_constraint(item, pltpu.VMEM) for item in results))
    return attended[None], grads[None], weight_grad, mixture[0]


def solution(mesh):
    return jax.shard_map(
        body,
        mesh=mesh,
        in_specs=(
            P("dp", "seq", None), P("dp", "seq", None), P("dp", "seq"), P("dp", "seq"),
            P("dp", "seq"), P("dp"), P(), P(),
        ),
        out_specs=(P("dp", "seq", None), P("dp", "seq", None), P(), P()),
        check_vma=False,
    )
```

```python
import functools
import math

import jax
import jax.numpy as jnp
import numpy as np
from jax import lax
from jax.experimental import pallas as pl
from jax.experimental.pallas import tpu as pltpu
from jax.sharding import PartitionSpec as P

HEADS = 16
DIM = 128
FREQ_DIM = 256
BUCKETS = 16
WIDTH = HEADS * DIM
RATE = 10.0
COLS = 512
CHUNK = 32
LOG2E = 1.4426950408889634
SCALE = DIM ** (-0.5)
MESH = pl.DeviceIdType.MESH
HIGHEST = lax.Precision.HIGHEST
BF16 = jnp.bfloat16
F32 = jnp.float32

POS, WEIGHT, BUCKET, REF, EMB, MIX = 0, 1, 2, 3, 4, 6
KEY, QUERY, VALUE, AIM = 0, 1, 2, 3
SLOT = {AIM: KEY, VALUE: QUERY, QUERY: VALUE, KEY: AIM}
PART_COLUMN = {KEY: WIDTH, QUERY: 0, VALUE: 2 * WIDTH, AIM: 0}


def split(x):
    hi = x.astype(BF16)
    return hi, (x - hi.astype(F32)).astype(BF16)


def dot(a, b):
    return lax.dot_general(a, b, (((1,), (0,)), ((), ())), preferred_element_type=F32)


def dot_nt(a, b):
    return lax.dot_general(a, b, (((1,), (1,)), ((), ())), preferred_element_type=F32)


def kernel(
    shards, copies, rows, aims, places_in, buckets_in, ref_in, steps_in, old_in, frequency_in, mod_w,
    att_out, grad_out, weight_out, mix_out,
    places, buckets, ref_row, frequency, steps, old, meta, meta_all, got, mod_buf, perm, cat, k3, kt, q3, v3, vt, u3, e_hi, e_lo, head_out, inv_sum, delta,
    gain_sum, score_a, score_b, loss_rows, stage1, tile1, stage2, tile2, stage3, tile3,
    send_sem, recv_sem, back_send, back_recv, small_send, small_recv, mod_sem, operand_sem,
):
    length = shards * DIM
    me = lax.axis_index("seq")
    sample = lax.axis_index("dp")
    my_z, my_y = me // 4, lax.rem(me, 4)

    side = 1 - 2 * lax.rem(sample, 2)

    def shard_at(slot):
        along, shift = lax.rem(slot, 4), slot // 4
        return lax.rem(my_z + 4 + side * along, 4) * 4 + lax.rem(my_y + 8 + side * (along + shift), 4)

    peers = [shard_at(slot) for slot in range(1, shards)]

    barrier = pltpu.get_barrier_semaphore()
    for peer in peers:
        pl.semaphore_signal(barrier, inc=1, device_id={"seq": peer}, device_id_type=MESH)
    for turn in range(1, copies):
        other = lax.rem(sample + turn, copies)
        pl.semaphore_signal(barrier, inc=1, device_id={"dp": other}, device_id_type=MESH)

    operands = [
        pltpu.make_async_copy(source, into, operand_sem.at[index])
        for index, (source, into) in enumerate(
            (
                (places_in, places), (buckets_in, buckets), (ref_in, ref_row), (frequency_in, frequency),
                (steps_in, steps), (old_in, old),
            )
        )
    ]
    for operand in operands:
        operand.start()
    mod_copy = pltpu.make_async_copy(
        mod_w.at[:, pl.ds(pl.multiple_of(me * DIM, DIM), DIM)], mod_buf, mod_sem
    )
    mod_copy.start()
    pl.semaphore_wait(barrier, shards - 1 + copies - 1)

    def source(part, head):
        base = aims if part == AIM else rows
        return base.at[:, pl.ds(pl.multiple_of(PART_COLUMN[part] + head * DIM, DIM), DIM)]

    def landing(part):
        return got.at[part, pl.ds(pl.multiple_of(me * DIM, DIM), DIM), :]

    def send(part):
        pltpu.make_async_copy(source(part, me), landing(part), recv_sem.at[part]).start()
        for peer in peers:
            pltpu.make_async_remote_copy(
                source(part, peer), landing(part), send_sem.at[part], recv_sem.at[part],
                device_id={"seq": peer}, device_id_type=MESH,
            ).start()

    def wait_sent(part):
        sent = got.at[part, pl.ds(0, (shards - 1) * DIM), :]
        pltpu.make_async_copy(sent, sent, send_sem.at[part]).wait()

    send(KEY)

    for operand in operands:
        operand.wait()
    meta[POS : POS + 1, :] = places[...].astype(F32)
    bucket_row = buckets[...]
    lane = lax.broadcasted_iota(jnp.int32, (1, DIM), 1)
    weight_row = jnp.zeros((1, DIM), F32)
    old_row = jnp.zeros((1, DIM), F32)
    for bucket in range(BUCKETS):
        weight_row = weight_row + jnp.where(bucket_row == bucket, old[bucket], 0.0)
        old_row = old_row + jnp.where(lane == bucket, old[bucket], 0.0)
    meta[WEIGHT : WEIGHT + 1, :] = weight_row
    meta[BUCKET : BUCKET + 1, :] = bucket_row.astype(F32)
    meta[REF : REF + 1, :] = ref_row[...]
    angles = steps[0].astype(F32) * frequency[...]
    for row, wave in ((EMB, jnp.cos(angles)), (EMB + 1, jnp.sin(angles))):
        meta[row : row + 1, :] = wave / (1.0 + jnp.exp(-wave))
    meta[MIX : MIX + 1, :] = old_row
    meta[MIX + 1 : MIX + 2, :] = jnp.zeros((1, DIM), F32)
    meta_all[me] = meta[...]
    for peer in peers:
        pltpu.make_async_remote_copy(
            meta.at[pl.ds(0, 2)], meta_all.at[me, pl.ds(0, 2)], small_send.at[0], small_recv.at[0],
            device_id={"seq": peer}, device_id_type=MESH,
        ).start()
    send(QUERY)

    def wait_small(sem, buffer, count, depth=2):
        taken = buffer.at[pl.ds(0, count), pl.ds(0, depth)]
        pltpu.make_async_copy(taken, taken, sem).wait()

    mod_copy.wait()
    embedding = jnp.concatenate([meta[EMB : EMB + 1, :], meta[EMB + 1 : EMB + 2, :]], axis=1)
    embedding = jnp.broadcast_to(embedding, (8, FREQ_DIM))
    gain_row = 1.0 + lax.dot_general(
        embedding, mod_buf[...], (((1,), (0,)), ((), ())), precision=HIGHEST, preferred_element_type=F32
    )
    gain = jnp.broadcast_to(gain_row[0:1, :], (DIM, DIM)).T

    wait_small(small_recv.at[0], meta_all, shards - 1)

    def perm_block(block, carry):
        at = pl.multiple_of(block * 256, 256)
        inside = lax.broadcasted_iota(jnp.int32, (DIM, DIM), 0)
        place = jnp.concatenate([inside + shard_at(2 * block + half) * DIM for half in range(2)], axis=0).astype(F32)
        for shard in range(shards):
            hit = place == meta_all[shard, POS : POS + 1, :]
            perm[pl.ds(at, 256), shard * DIM : (shard + 1) * DIM] = jnp.where(hit, 1.0, 0.0).astype(BF16)
        return carry

    lax.fori_loop(0, length // 256, perm_block, 0)

    def pipeline(count, make, use, finish=None):
        def both(at, last):
            make(at + 1, score_b)
            use(at, score_a)
            if not last:
                make(at + 2, score_a)
            use(at + 1, score_b)
            if finish is not None:
                finish(at)
                finish(at + 1)

        def one(pair, carry):
            both(2 * pair, False)
            return carry

        make(0, score_a)
        lax.fori_loop(0, count // 2 - 1, one, 0)
        both(count - 2, True)

    def arrive(part, factor):
        pltpu.make_async_copy(got.at[part], got.at[part], recv_sem.at[part]).wait()

        def one(block, carry):
            at = pl.multiple_of(block * 256, 256)
            hi, lo = split(got[part, pl.ds(at, 256), :] * factor)
            cat[pl.ds(at, 256), 0:DIM] = hi
            cat[pl.ds(at, 256), DIM : 2 * DIM] = lo
            return carry

        lax.fori_loop(0, length // 256, one, 0)

    def reorder(part, factor, into, transposed):
        arrive(part, factor)

        def make(block, buffer):
            at = pl.multiple_of(block * 512, 512)
            buffer[0:512, 0:256] = dot(perm[pl.ds(at, 512), :], cat[...])

        def use(block, buffer):
            at = pl.multiple_of(block * 512, 512)
            placed = buffer[0:512, 0:256]
            hi, lo = placed[:, :DIM].astype(BF16), placed[:, DIM:].astype(BF16)
            into[pl.ds(at, 512), 0:DIM] = hi
            into[pl.ds(at, 512), DIM : 2 * DIM] = hi if part == QUERY else lo
            into[pl.ds(at, 512), 2 * DIM : 3 * DIM] = lo if part == QUERY else hi
            if transposed is not None:
                hi, lo = split((placed[:, :DIM] + placed[:, DIM:]).T)
                transposed[0:DIM, pl.ds(at, 512)] = hi
                transposed[DIM : 2 * DIM, pl.ds(at, 512)] = lo

        pipeline(length // 512, make, use)

    def by_columns(left, high, low):
        full = dot(left[...], high)
        return full[:DIM] + full[DIM:] + dot(left[0:DIM, :], low)

    def by_rows(at, right):
        full = dot(e_hi[pl.ds(at, 512), :], right[...])
        return full[:, :DIM] + full[:, DIM:] + dot(e_lo[pl.ds(at, 512), :], right[:, 0:DIM])

    wait_sent(KEY)
    send(VALUE)
    reorder(KEY, 1.0, k3, kt)
    wait_sent(QUERY)
    send(AIM)
    reorder(QUERY, SCALE * LOG2E, q3, None)

    def score_block(block, buffer):
        at = pl.multiple_of(block * COLS, COLS)
        buffer[...] = dot_nt(k3[...], q3[pl.ds(at, COLS), :])

    def softmax_block(block, buffer):
        at = pl.multiple_of(block * COLS, COLS)
        top = jnp.full((8, COLS), -jnp.inf, F32)
        for row in range(0, length, CHUNK):
            top = jnp.maximum(top, jnp.max(buffer[row : row + CHUNK, :].reshape(CHUNK // 8, 8, COLS), axis=0))
        top = jnp.max(top, axis=0, keepdims=True)
        sums = jnp.zeros((8, COLS), F32)
        for row in range(0, length, CHUNK):
            weights = jnp.exp2(buffer[row : row + CHUNK, :] - top)
            sums = sums + jnp.sum(weights.reshape(CHUNK // 8, 8, COLS), axis=0)
            hi, lo = split(weights)
            e_hi[row : row + CHUNK, pl.ds(at, COLS)] = hi
            e_lo[row : row + CHUNK, pl.ds(at, COLS)] = lo
        inv_sum[:, pl.ds(at, COLS)] = jnp.broadcast_to(1.0 / jnp.sum(sums, axis=0, keepdims=True), (8, COLS))

    pipeline(length // COLS, score_block, softmax_block)

    def target(part):
        base = att_out if part == AIM else grad_out
        return base.at[:, pl.ds(pl.multiple_of(PART_COLUMN[part] + me * DIM, DIM), DIM)]

    def give(part, slot):
        block = got.at[SLOT[part], pl.ds(pl.multiple_of(slot * DIM, DIM), DIM), :]
        shard = shard_at(slot)

        @pl.when(shard != me)
        def _():
            pltpu.make_async_remote_copy(
                block, target(part), back_send.at[part], back_recv.at[part],
                device_id={"seq": shard}, device_id_type=MESH,
            ).start()

        @pl.when(shard == me)
        def _():
            pltpu.make_async_copy(block, target(part), back_recv.at[part]).start()

    reorder(VALUE, 1.0, v3, vt)

    def output_block(turn, buffer):
        at = pl.multiple_of(turn * COLS, COLS)
        buffer[0:DIM, :] = by_columns(vt, e_hi[:, pl.ds(at, COLS)], e_lo[:, pl.ds(at, COLS)])

    def attended_block(turn, buffer):
        at = pl.multiple_of(turn * COLS, COLS)
        out = buffer[0:DIM, :] * inv_sum[0:1, pl.ds(at, COLS)]
        head_out[:, pl.ds(at, COLS)] = out
        for half in range(COLS // DIM):
            begin = pl.multiple_of(at + half * DIM, DIM)
            got[SLOT[AIM], pl.ds(begin, DIM), :] = (gain * out[:, half * DIM : (half + 1) * DIM]).T

    def give_pair(part):
        def finish(turn):
            for half in range(COLS // DIM):
                give(part, turn * (COLS // DIM) + half)

        return finish

    pipeline(length // COLS, output_block, attended_block, give_pair(AIM))

    arrive(AIM, 1.0)

    def aim_block(block, buffer):
        at = pl.multiple_of(block * 512, 512)
        buffer[0:512, 0:256] = dot(perm[pl.ds(at, 512), :], cat[...])

    gain_sum[...] = jnp.zeros((DIM, DIM), F32)

    def upstream_block(block, buffer):
        at = pl.multiple_of(block * 512, 512)
        placed = buffer[0:512, 0:256]
        aim = placed[:, :DIM] + placed[:, DIM:]
        total = jnp.zeros((DIM, DIM), F32)
        for quarter in range(4):
            slot = block * 4 + quarter
            begin = pl.multiple_of(at + quarter * DIM, DIM)
            out = head_out[:, pl.ds(begin, DIM)]
            gap = gain * out - aim[quarter * DIM : (quarter + 1) * DIM, :].T
            loss_rows[slot] = jnp.broadcast_to(jnp.sum(gap * gap, axis=0, keepdims=True), (8, DIM))
            up_a = gap * meta_all[shard_at(slot), WEIGHT : WEIGHT + 1, :]
            total = total + up_a * out
            up = gain * up_a * inv_sum[0:1, pl.ds(begin, DIM)]
            delta[:, pl.ds(begin, DIM)] = jnp.broadcast_to(jnp.sum(up * out, axis=0, keepdims=True), (8, DIM))
            hi, lo = split(up.T)
            u3[pl.ds(begin, DIM), 0:DIM] = hi
            u3[pl.ds(begin, DIM), DIM : 2 * DIM] = hi
            u3[pl.ds(begin, DIM), 2 * DIM : 3 * DIM] = lo
        gain_sum[...] += total

    pipeline(length // 512, aim_block, upstream_block)

    gain_grad = jnp.sum(gain_sum[...].T, axis=0, keepdims=True)
    row_index = lax.broadcasted_iota(jnp.int32, (8, DIM), 0)
    for slot in range(shards):
        tile1[slot] = jnp.where(row_index == 0, loss_rows[slot], jnp.broadcast_to(gain_grad, (8, DIM)))
    stage1[me] = tile1[0]
    for slot, peer in enumerate(peers):
        pltpu.make_async_remote_copy(
            tile1.at[slot + 1, pl.ds(0, 2)], stage1.at[me, pl.ds(0, 2)], small_send.at[1], small_recv.at[1],
            device_id={"seq": peer}, device_id_type=MESH,
        ).start()

    def value_grad_block(turn, carry):
        block = turn
        at = pl.multiple_of(block * 512, 512)
        got[SLOT[VALUE], pl.ds(at, 512), :] = by_rows(at, u3.at[:, DIM : 3 * DIM])
        for quarter in range(4):
            give(VALUE, block * 4 + quarter)
        return carry

    lax.fori_loop(0, shards // 4, value_grad_block, 0)

    def exchange_losses():
        wait_small(small_recv.at[1], stage1, shards - 1)
        loss = jnp.zeros((1, DIM), F32)
        for shard in range(shards):
            loss = loss + stage1[shard, 0:1, :]
        excess = jnp.maximum(0.5 * loss / WIDTH - meta[REF : REF + 1, :], 0.0)
        hit = lax.broadcasted_iota(jnp.int32, (DIM, DIM), 0).astype(F32) == meta[BUCKET : BUCKET + 1, :]
        sums = lax.dot_general(
            jnp.where(row_index == 0, jnp.broadcast_to(excess, (8, DIM)), 1.0), jnp.where(hit, 1.0, 0.0),
            (((1,), (1,)), ((), ())), precision=HIGHEST, preferred_element_type=F32,
        )
        for shard in range(shards):
            tile2[shard : shard + 1, :] = stage1[shard, 1:2, :]
        tile2[shards : shards + 2, :] = sums[0:2, :]
        tile2[shards + 2 : shards + 4, :] = meta[EMB : EMB + 2, :]
        stage2[sample] = tile2[...]
        for turn in range(1, copies):
            other = lax.rem(sample + turn, copies)
            pltpu.make_async_remote_copy(
                tile2.at[pl.ds(0, shards + 4)], stage2.at[sample, pl.ds(0, shards + 4)], small_send.at[2], small_recv.at[2],
                device_id={"dp": other}, device_id_type=MESH,
            ).start()

    hi_a, lo_a, hi_b, lo_b = (perm.at[:, at : at + COLS] for at in range(0, 4 * COLS, COLS))

    def prob_grad_block(turn, buffer):
        at = pl.multiple_of(turn * COLS, COLS)
        buffer[...] = dot_nt(v3[...], u3[pl.ds(at, COLS), :])

    def score_grad_block(turn, buffer, high, low):
        at = pl.multiple_of(turn * COLS, COLS)
        shift = delta[0:1, pl.ds(at, COLS)]
        for row in range(0, length, CHUNK):
            here = (slice(row, row + CHUNK), pl.ds(at, COLS))
            weights = e_hi[here].astype(F32) + e_lo[here].astype(F32)
            hi, lo = split((buffer[row : row + CHUNK, :] - shift) * weights)
            high[row : row + CHUNK, :] = hi
            low[row : row + CHUNK, :] = lo
            e_hi[here] = hi
            e_lo[here] = lo

    def query_grad_block(turn, high, low):
        at = pl.multiple_of(turn * COLS, COLS)
        grad = by_columns(kt, high[...], low[...]) * SCALE
        for half in range(COLS // DIM):
            begin = pl.multiple_of(at + half * DIM, DIM)
            got[SLOT[QUERY], pl.ds(begin, DIM), :] = grad[:, half * DIM : (half + 1) * DIM].T

    give_queries = give_pair(QUERY)
    prob_grad_block(0, score_a)
    prob_grad_block(1, score_b)
    score_grad_block(0, score_a, hi_a, lo_a)

    def gradient_pair(pair, carry):
        turn = 2 * pair + 1
        prob_grad_block(turn + 1, score_a)
        score_grad_block(turn, score_b, hi_b, lo_b)
        query_grad_block(turn - 1, hi_a, lo_a)
        prob_grad_block(turn + 2, score_b)
        score_grad_block(turn + 1, score_a, hi_a, lo_a)
        query_grad_block(turn, hi_b, lo_b)
        give_queries(turn - 1)
        give_queries(turn)
        pl.when(pair == last // 2 - 1)(exchange_losses)
        return carry

    last = length // COLS - 1
    lax.fori_loop(0, last // 2, gradient_pair, 0)
    score_grad_block(last, score_b, hi_b, lo_b)
    query_grad_block(last - 1, hi_a, lo_a)
    query_grad_block(last, hi_b, lo_b)
    give_queries(last - 1)
    give_queries(last)

    def exchange_sums():
        if copies > 1:
            wait_small(small_recv.at[2], stage2, copies - 1, shards + 4)
        sums = jnp.zeros((2, DIM), F32)
        for other in range(copies):
            sums = sums + stage2[other, shards : shards + 2, :]
        tile3[0:2, :] = sums
        stage3[me, 0:2, :] = sums
        for peer in peers:
            pltpu.make_async_remote_copy(
                tile3.at[pl.ds(0, 2)], stage3.at[me, pl.ds(0, 2)], small_send.at[3], small_recv.at[3],
                device_id={"seq": peer}, device_id_type=MESH,
            ).start()

    def key_grad_block(turn, carry):
        block = turn
        at = pl.multiple_of(block * 512, 512)
        got[SLOT[KEY], pl.ds(at, 512), :] = by_rows(at, q3.at[:, DIM : 3 * DIM]) * (1.0 / LOG2E)
        for quarter in range(4):
            give(KEY, block * 4 + quarter)
        pl.when(turn == 1)(exchange_sums)
        return carry

    lax.fori_loop(0, shards // 4, key_grad_block, 0)

    by_sample = jnp.concatenate(
        [
            jnp.concatenate([stage2[other, row : row + 1, :] for row in (shards + 2, shards + 3)], axis=1)
            for other in range(copies)
        ],
        axis=0,
    )
    by_frequency = by_sample.T
    for head in range(shards):
        gains = jnp.concatenate([stage2[other, head : head + 1, :] for other in range(copies)], axis=0)
        weight_out[:, head * DIM : (head + 1) * DIM] = lax.dot_general(
            by_frequency, gains, (((1,), (0,)), ((), ())), precision=HIGHEST, preferred_element_type=F32
        )
    wait_small(small_recv.at[3], stage3, shards - 1)
    sums = jnp.zeros((2, DIM), F32)
    for shard in range(shards):
        sums = sums + stage3[shard, 0:2, :]
    mean = sums[0:1, :] / jnp.maximum(sums[1:2, :], 1.0)
    updated = meta[MIX : MIX + 1, :] * (1.0 + RATE * mean)
    updated = jnp.where(lane < BUCKETS, updated, 0.0)
    mixture = BUCKETS * updated / jnp.sum(updated, axis=1, keepdims=True)
    mix_out[...] = mixture[:, :BUCKETS]

    others = (shards - 1) * DIM
    for part in (KEY, QUERY, VALUE, AIM):
        if part in (VALUE, AIM):
            wait_sent(part)
        sent = got.at[SLOT[part], pl.ds(0, others), :]
        pltpu.make_async_copy(sent, sent, back_send.at[part]).wait()
        base = att_out if part == AIM else grad_out
        landed = base.at[:, PART_COLUMN[part] : PART_COLUMN[part] + WIDTH]
        pltpu.make_async_copy(landed, landed, back_recv.at[part]).wait()
    wait_small(small_send.at[0], meta_all, shards - 1)
    wait_small(small_send.at[1], stage1, shards - 1)
    if copies > 1:
        wait_small(small_send.at[2], stage2, copies - 1, shards + 4)
    wait_small(small_send.at[3], stage3, shards - 1)


def move_out(*refs):
    count = len(refs) // 2
    sources, outputs, sems = refs[:count], refs[count : 2 * count], refs[-1]
    moves = []
    for source, output in zip(sources, outputs):
        pieces = 4 if source.shape[0] >= DIM else 1
        rows = source.shape[0] // pieces
        for piece in range(pieces):
            part = pl.ds(piece * rows, rows)
            moves.append(pltpu.make_async_copy(source.at[part], output.at[part], sems.at[len(moves)]))
    for move in moves:
        move.start()
    for move in moves:
        move.wait()


def body(reader_rows, reader_targets, dest_pos, bucket_ids, ref_loss, timesteps, mod_weight, mixture_old):
    shards, copies = lax.axis_size("seq"), lax.axis_size("dp")
    length = shards * DIM
    half = FREQ_DIM // 2
    frequency = np.exp(-math.log(10000.0) * np.arange(half) / half).astype(np.float32)[None, :]
    any_spec = pl.BlockSpec(memory_space=pl.ANY)
    vmem_spec = pl.BlockSpec(memory_space=pltpu.VMEM)
    dma = pltpu.SemaphoreType.DMA
    attended, grads, weight_grad, mixture = pl.pallas_call(
        functools.partial(kernel, shards, copies),
        out_shape=(
            pltpu.VMEM((DIM, WIDTH), F32),
            pltpu.VMEM((DIM, 3 * WIDTH), F32),
            pltpu.VMEM((FREQ_DIM, WIDTH), F32),
            pltpu.VMEM((1, BUCKETS), F32),
        ),
        in_specs=[any_spec] * 9,
        out_specs=(vmem_spec, vmem_spec, vmem_spec, vmem_spec),
        scratch_shapes=[
            pltpu.VMEM((1, DIM), jnp.int32),
            pltpu.VMEM((1, DIM), jnp.int32),
            pltpu.VMEM((1, DIM), F32),
            pltpu.VMEM((1, DIM), F32),
            pltpu.SMEM((1,), jnp.int32),
            pltpu.SMEM((BUCKETS,), F32),
            pltpu.VMEM((8, DIM), F32),
            pltpu.VMEM((shards, 8, DIM), F32),
            pltpu.VMEM((4, length, DIM), F32),
            pltpu.VMEM((FREQ_DIM, DIM), F32),
            pltpu.VMEM((length, length), BF16),
            pltpu.VMEM((length, 2 * DIM), BF16),
            pltpu.VMEM((length, 3 * DIM), BF16),
            pltpu.VMEM((2 * DIM, length), BF16),
            pltpu.VMEM((length, 3 * DIM), BF16),
            pltpu.VMEM((length, 3 * DIM), BF16),
            pltpu.VMEM((2 * DIM, length), BF16),
            pltpu.VMEM((length, 3 * DIM), BF16),
            pltpu.VMEM((length, length), BF16),
            pltpu.VMEM((length, length), BF16),
            pltpu.VMEM((DIM, length), F32),
            pltpu.VMEM((8, length), F32),
            pltpu.VMEM((8, length), F32),
            pltpu.VMEM((DIM, DIM), F32),
            pltpu.VMEM((length, COLS), F32),
            pltpu.VMEM((length, COLS), F32),
            pltpu.VMEM((shards, 8, DIM), F32),
            pltpu.VMEM((shards, 8, DIM), F32),
            pltpu.VMEM((shards, 8, DIM), F32),
            pltpu.VMEM((copies, shards + 8, DIM), F32),
            pltpu.VMEM((shards + 8, DIM), F32),
            pltpu.VMEM((shards, 8, DIM), F32),
            pltpu.VMEM((8, DIM), F32),
            dma((4,)), dma((4,)), dma((4,)), dma((4,)), dma((4,)), dma((4,)), dma, dma((6,)),
        ],
        compiler_params=pltpu.CompilerParams(
            collective_id=0, has_side_effects=True, vmem_limit_bytes=56 * 1024 * 1024
        ),
        name="attend",
    )(reader_rows[0], reader_targets[0], dest_pos, bucket_ids, ref_loss, timesteps, mixture_old, frequency, mod_weight)
    results = (attended, grads, weight_grad, mixture)
    attended, grads, weight_grad, mixture = pl.pallas_call(
        move_out,
        out_shape=tuple(jax.ShapeDtypeStruct(item.shape, F32) for item in results),
        in_specs=[vmem_spec] * 4,
        out_specs=(any_spec,) * 4,
        scratch_shapes=[dma((13,))],
        compiler_params=pltpu.CompilerParams(vmem_limit_bytes=1024 * 1024),
        name="move_out",
    )(*(pltpu.with_memory_space_constraint(item, pltpu.VMEM) for item in results))
    return attended[None], grads[None], weight_grad, mixture[0]


def solution(mesh):
    return jax.shard_map(
        body,
        mesh=mesh,
        in_specs=(
            P("dp", "seq", None), P("dp", "seq", None), P("dp", "seq"), P("dp", "seq"),
            P("dp", "seq"), P("dp"), P(), P(),
        ),
        out_specs=(P("dp", "seq", None), P("dp", "seq", None), P(), P()),
        check_vma=False,
    )
```

```python
import functools
import math

import jax
import jax.numpy as jnp
import numpy as np
from jax import lax
from jax.experimental import pallas as pl
from jax.experimental.pallas import tpu as pltpu
from jax.sharding import PartitionSpec as P

HEADS = 16
DIM = 128
FREQ_DIM = 256
BUCKETS = 16
WIDTH = HEADS * DIM
RATE = 10.0
CHUNK = 64
LOG2E = 1.4426950408889634
SCALE = DIM ** (-0.5)
MESH = pl.DeviceIdType.MESH
HIGHEST = lax.Precision.HIGHEST
BF16 = jnp.bfloat16
F32 = jnp.float32

POS, WEIGHT, BUCKET, REF, EMB, MIX = 0, 1, 2, 3, 4, 6
KEY, QUERY, VALUE, AIM = 0, 1, 2, 3
SLOT = {AIM: KEY, VALUE: QUERY, QUERY: VALUE, KEY: AIM}
PART_COLUMN = {KEY: WIDTH, QUERY: 0, VALUE: 2 * WIDTH, AIM: 0}


def split(x):
    hi = x.astype(BF16)
    return hi, (x - hi.astype(F32)).astype(BF16)


def dot(a, b):
    return lax.dot_general(a, b, (((1,), (0,)), ((), ())), preferred_element_type=F32)


def dot_nt(a, b):
    return lax.dot_general(a, b, (((1,), (1,)), ((), ())), preferred_element_type=F32)


def kernel(
    shards, copies, rows, aims, places_in, buckets_in, ref_in, steps_in, old_in, frequency_in, mod_w,
    att_out, grad_out, weight_out, mix_out,
    places, buckets, ref_row, frequency, steps, old, meta, meta_all, got, mod_buf, perm, cat, k3, kt, q3, v3, vt, u3, e_hi, e_lo, head_out, inv_sum, delta,
    gain_sum, score_a, score_b, loss_rows, stage1, tile1, stage2, tile2, stage3, tile3,
    send_sem, recv_sem, back_send, back_recv, small_send, small_recv, mod_sem, operand_sem,
):
    length = shards * DIM
    me = lax.axis_index("seq")
    sample = lax.axis_index("dp")
    my_z, my_y = me // 4, lax.rem(me, 4)

    core = lax.rem(sample, 2)
    side = 1 - 2 * core

    def shard_at(slot):
        along, shift = lax.rem(slot, 4), slot // 4
        by_z, by_y = along + core * shift, along + (1 - core) * shift
        return lax.rem(my_z + 8 + side * by_z, 4) * 4 + lax.rem(my_y + 8 + side * by_y, 4)

    peers = [shard_at(slot) for slot in range(1, shards)]

    barrier = pltpu.get_barrier_semaphore()
    for peer in peers:
        pl.semaphore_signal(barrier, inc=1, device_id={"seq": peer}, device_id_type=MESH)
    for turn in range(1, copies):
        other = lax.rem(sample + turn, copies)
        pl.semaphore_signal(barrier, inc=1, device_id={"dp": other}, device_id_type=MESH)

    operands = [
        pltpu.make_async_copy(source, into, operand_sem.at[index])
        for index, (source, into) in enumerate(
            (
                (places_in, places), (buckets_in, buckets), (ref_in, ref_row), (frequency_in, frequency),
                (steps_in, steps), (old_in, old),
            )
        )
    ]
    for operand in operands:
        operand.start()
    mod_copy = pltpu.make_async_copy(
        mod_w.at[:, pl.ds(pl.multiple_of(me * DIM, DIM), DIM)], mod_buf, mod_sem
    )
    mod_copy.start()
    pl.semaphore_wait(barrier, shards - 1 + copies - 1)

    def source(part, head):
        base = aims if part == AIM else rows
        return base.at[:, pl.ds(pl.multiple_of(PART_COLUMN[part] + head * DIM, DIM), DIM)]

    def landing(part):
        return got.at[part, pl.ds(pl.multiple_of(me * DIM, DIM), DIM), :]

    def send(part):
        pltpu.make_async_copy(source(part, me), landing(part), recv_sem.at[part]).start()
        for peer in peers:
            pltpu.make_async_remote_copy(
                source(part, peer), landing(part), send_sem.at[part], recv_sem.at[part],
                device_id={"seq": peer}, device_id_type=MESH,
            ).start()

    def wait_sent(part):
        sent = got.at[part, pl.ds(0, (shards - 1) * DIM), :]
        pltpu.make_async_copy(sent, sent, send_sem.at[part]).wait()

    send(KEY)

    for operand in operands:
        operand.wait()
    meta[POS : POS + 1, :] = places[...].astype(F32)
    bucket_row = buckets[...]
    lane = lax.broadcasted_iota(jnp.int32, (1, DIM), 1)
    weight_row = jnp.zeros((1, DIM), F32)
    old_row = jnp.zeros((1, DIM), F32)
    for bucket in range(BUCKETS):
        weight_row = weight_row + jnp.where(bucket_row == bucket, old[bucket], 0.0)
        old_row = old_row + jnp.where(lane == bucket, old[bucket], 0.0)
    meta[WEIGHT : WEIGHT + 1, :] = weight_row
    meta[BUCKET : BUCKET + 1, :] = bucket_row.astype(F32)
    meta[REF : REF + 1, :] = ref_row[...]
    angles = steps[0].astype(F32) * frequency[...]
    for row, wave in ((EMB, jnp.cos(angles)), (EMB + 1, jnp.sin(angles))):
        meta[row : row + 1, :] = wave / (1.0 + jnp.exp(-wave))
    meta[MIX : MIX + 1, :] = old_row
    meta[MIX + 1 : MIX + 2, :] = jnp.zeros((1, DIM), F32)
    meta_all[me] = meta[...]
    for peer in peers:
        pltpu.make_async_remote_copy(
            meta.at[pl.ds(0, 2)], meta_all.at[me, pl.ds(0, 2)], small_send.at[0], small_recv.at[0],
            device_id={"seq": peer}, device_id_type=MESH,
        ).start()
    send(QUERY)

    def wait_small(sem, buffer, count, depth=2):
        taken = buffer.at[pl.ds(0, count), pl.ds(0, depth)]
        pltpu.make_async_copy(taken, taken, sem).wait()

    mod_copy.wait()
    embedding = jnp.concatenate([meta[EMB : EMB + 1, :], meta[EMB + 1 : EMB + 2, :]], axis=1)
    embedding = jnp.broadcast_to(embedding, (8, FREQ_DIM))
    gain_row = 1.0 + lax.dot_general(
        embedding, mod_buf[...], (((1,), (0,)), ((), ())), precision=HIGHEST, preferred_element_type=F32
    )
    gain = jnp.broadcast_to(gain_row[0:1, :], (DIM, DIM)).T

    wait_small(small_recv.at[0], meta_all, shards - 1)

    def perm_block(block, carry):
        at = pl.multiple_of(block * 256, 256)
        inside = lax.broadcasted_iota(jnp.int32, (DIM, DIM), 0)
        place = jnp.concatenate([inside + shard_at(2 * block + half) * DIM for half in range(2)], axis=0).astype(F32)
        for shard in range(shards):
            hit = place == meta_all[shard, POS : POS + 1, :]
            perm[pl.ds(at, 256), shard * DIM : (shard + 1) * DIM] = jnp.where(hit, 1.0, 0.0).astype(BF16)
        return carry

    lax.fori_loop(0, length // 256, perm_block, 0)

    def pipeline(count, make, use, finish=None):
        def both(at, last):
            make(at + 1, score_b)
            use(at, score_a)
            if not last:
                make(at + 2, score_a)
            use(at + 1, score_b)
            if finish is not None:
                finish(at)
                finish(at + 1)

        def one(pair, carry):
            both(2 * pair, False)
            return carry

        make(0, score_a)
        lax.fori_loop(0, count // 2 - 1, one, 0)
        both(count - 2, True)

    def arrive(part, factor):
        pltpu.make_async_copy(got.at[part], got.at[part], recv_sem.at[part]).wait()

        def one(block, carry):
            at = pl.multiple_of(block * 256, 256)
            hi, lo = split(got[part, pl.ds(at, 256), :] * factor)
            cat[pl.ds(at, 256), 0:DIM] = hi
            cat[pl.ds(at, 256), DIM : 2 * DIM] = lo
            return carry

        lax.fori_loop(0, length // 256, one, 0)

    def reorder(part, factor, into, transposed):
        arrive(part, factor)

        def make(block, buffer):
            at = pl.multiple_of(block * 512, 512)
            buffer[0:512, :] = dot(perm[pl.ds(at, 512), :], cat[...])

        def use(block, buffer):
            at = pl.multiple_of(block * 512, 512)
            placed = buffer[0:512, :]
            hi, lo = placed[:, :DIM].astype(BF16), placed[:, DIM:].astype(BF16)
            into[pl.ds(at, 512), 0:DIM] = hi
            into[pl.ds(at, 512), DIM : 2 * DIM] = hi if part == QUERY else lo
            into[pl.ds(at, 512), 2 * DIM : 3 * DIM] = lo if part == QUERY else hi
            if transposed is not None:
                hi, lo = split((placed[:, :DIM] + placed[:, DIM:]).T)
                transposed[0:DIM, pl.ds(at, 512)] = hi
                transposed[DIM : 2 * DIM, pl.ds(at, 512)] = lo

        pipeline(length // 512, make, use)

    def by_columns(left, high, low):
        full = dot(left[...], high)
        return full[:DIM] + full[DIM:] + dot(left[0:DIM, :], low)

    def by_rows(at, right):
        full = dot(e_hi[pl.ds(at, 512), :], right[...])
        return full[:, :DIM] + full[:, DIM:] + dot(e_lo[pl.ds(at, 512), :], right[:, 0:DIM])

    wait_sent(KEY)
    send(VALUE)
    reorder(KEY, 1.0, k3, kt)
    wait_sent(QUERY)
    send(AIM)
    reorder(QUERY, SCALE * LOG2E, q3, None)

    def score_block(block, buffer):
        at = pl.multiple_of(block * 256, 256)
        buffer[...] = dot_nt(k3[...], q3[pl.ds(at, 256), :])

    def softmax_block(block, buffer):
        at = pl.multiple_of(block * 256, 256)
        top = jnp.full((8, 256), -jnp.inf, F32)
        for row in range(0, length, CHUNK):
            top = jnp.maximum(top, jnp.max(buffer[row : row + CHUNK, :].reshape(CHUNK // 8, 8, 256), axis=0))
        top = jnp.max(top, axis=0, keepdims=True)
        sums = jnp.zeros((8, 256), F32)
        for row in range(0, length, CHUNK):
            weights = jnp.exp2(buffer[row : row + CHUNK, :] - top)
            sums = sums + jnp.sum(weights.reshape(CHUNK // 8, 8, 256), axis=0)
            hi, lo = split(weights)
            e_hi[row : row + CHUNK, pl.ds(at, 256)] = hi
            e_lo[row : row + CHUNK, pl.ds(at, 256)] = lo
        inv_sum[:, pl.ds(at, 256)] = jnp.broadcast_to(1.0 / jnp.sum(sums, axis=0, keepdims=True), (8, 256))

    pipeline(length // 256, score_block, softmax_block)

    def target(part):
        base = att_out if part == AIM else grad_out
        return base.at[:, pl.ds(pl.multiple_of(PART_COLUMN[part] + me * DIM, DIM), DIM)]

    def give(part, slot):
        block = got.at[SLOT[part], pl.ds(pl.multiple_of(slot * DIM, DIM), DIM), :]
        shard = shard_at(slot)

        @pl.when(shard != me)
        def _():
            pltpu.make_async_remote_copy(
                block, target(part), back_send.at[part], back_recv.at[part],
                device_id={"seq": shard}, device_id_type=MESH,
            ).start()

        @pl.when(shard == me)
        def _():
            pltpu.make_async_copy(block, target(part), back_recv.at[part]).start()

    reorder(VALUE, 1.0, v3, vt)

    def output_block(turn, buffer):
        at = pl.multiple_of(turn * 256, 256)
        buffer[0:DIM, :] = by_columns(vt, e_hi[:, pl.ds(at, 256)], e_lo[:, pl.ds(at, 256)])

    def attended_block(turn, buffer):
        at = pl.multiple_of(turn * 256, 256)
        out = buffer[0:DIM, :] * inv_sum[0:1, pl.ds(at, 256)]
        head_out[:, pl.ds(at, 256)] = out
        for half in range(2):
            begin = pl.multiple_of(at + half * DIM, DIM)
            got[SLOT[AIM], pl.ds(begin, DIM), :] = (gain * out[:, half * DIM : (half + 1) * DIM]).T

    def give_pair(part):
        def finish(turn):
            for half in range(2):
                give(part, turn * 2 + half)

        return finish

    pipeline(shards // 2, output_block, attended_block, give_pair(AIM))

    arrive(AIM, 1.0)

    def aim_block(block, buffer):
        at = pl.multiple_of(block * 512, 512)
        buffer[0:512, :] = dot(perm[pl.ds(at, 512), :], cat[...])

    gain_sum[...] = jnp.zeros((DIM, DIM), F32)

    def upstream_block(block, buffer):
        at = pl.multiple_of(block * 512, 512)
        placed = buffer[0:512, :]
        aim = placed[:, :DIM] + placed[:, DIM:]
        total = jnp.zeros((DIM, DIM), F32)
        for quarter in range(4):
            slot = block * 4 + quarter
            begin = pl.multiple_of(at + quarter * DIM, DIM)
            out = head_out[:, pl.ds(begin, DIM)]
            gap = gain * out - aim[quarter * DIM : (quarter + 1) * DIM, :].T
            loss_rows[slot] = jnp.broadcast_to(jnp.sum(gap * gap, axis=0, keepdims=True), (8, DIM))
            up_a = gap * meta_all[shard_at(slot), WEIGHT : WEIGHT + 1, :]
            total = total + up_a * out
            up = gain * up_a * inv_sum[0:1, pl.ds(begin, DIM)]
            delta[:, pl.ds(begin, DIM)] = jnp.broadcast_to(jnp.sum(up * out, axis=0, keepdims=True), (8, DIM))
            hi, lo = split(up.T)
            u3[pl.ds(begin, DIM), 0:DIM] = hi
            u3[pl.ds(begin, DIM), DIM : 2 * DIM] = hi
            u3[pl.ds(begin, DIM), 2 * DIM : 3 * DIM] = lo
        gain_sum[...] += total

    pipeline(length // 512, aim_block, upstream_block)

    gain_grad = jnp.sum(gain_sum[...].T, axis=0, keepdims=True)
    row_index = lax.broadcasted_iota(jnp.int32, (8, DIM), 0)
    for slot in range(shards):
        tile1[slot] = jnp.where(row_index == 0, loss_rows[slot], jnp.broadcast_to(gain_grad, (8, DIM)))
    stage1[me] = tile1[0]
    for slot, peer in enumerate(peers):
        pltpu.make_async_remote_copy(
            tile1.at[slot + 1, pl.ds(0, 2)], stage1.at[me, pl.ds(0, 2)], small_send.at[1], small_recv.at[1],
            device_id={"seq": peer}, device_id_type=MESH,
        ).start()

    def value_grad_block(turn, carry):
        block = turn
        at = pl.multiple_of(block * 512, 512)
        got[SLOT[VALUE], pl.ds(at, 512), :] = by_rows(at, u3.at[:, DIM : 3 * DIM])
        for quarter in range(4):
            give(VALUE, block * 4 + quarter)
        return carry

    lax.fori_loop(0, shards // 4, value_grad_block, 0)

    def exchange_losses():
        wait_small(small_recv.at[1], stage1, shards - 1)
        loss = jnp.zeros((1, DIM), F32)
        for shard in range(shards):
            loss = loss + stage1[shard, 0:1, :]
        excess = jnp.maximum(0.5 * loss / WIDTH - meta[REF : REF + 1, :], 0.0)
        hit = lax.broadcasted_iota(jnp.int32, (DIM, DIM), 0).astype(F32) == meta[BUCKET : BUCKET + 1, :]
        sums = lax.dot_general(
            jnp.where(row_index == 0, jnp.broadcast_to(excess, (8, DIM)), 1.0), jnp.where(hit, 1.0, 0.0),
            (((1,), (1,)), ((), ())), precision=HIGHEST, preferred_element_type=F32,
        )
        for shard in range(shards):
            tile2[shard : shard + 1, :] = stage1[shard, 1:2, :]
        tile2[shards : shards + 2, :] = sums[0:2, :]
        tile2[shards + 2 : shards + 4, :] = meta[EMB : EMB + 2, :]
        stage2[sample] = tile2[...]
        for turn in range(1, copies):
            other = lax.rem(sample + turn, copies)
            pltpu.make_async_remote_copy(
                tile2.at[pl.ds(0, shards + 4)], stage2.at[sample, pl.ds(0, shards + 4)], small_send.at[2], small_recv.at[2],
                device_id={"dp": other}, device_id_type=MESH,
            ).start()

    hi_a, lo_a, hi_b, lo_b = (perm.at[:, at : at + 256] for at in range(0, 1024, 256))

    def prob_grad_block(turn, buffer):
        at = pl.multiple_of(turn * 256, 256)
        buffer[...] = dot_nt(v3[...], u3[pl.ds(at, 256), :])

    def score_grad_block(turn, buffer, high, low):
        at = pl.multiple_of(turn * 256, 256)
        shift = delta[0:1, pl.ds(at, 256)]
        for row in range(0, length, CHUNK):
            here = (slice(row, row + CHUNK), pl.ds(at, 256))
            weights = e_hi[here].astype(F32) + e_lo[here].astype(F32)
            hi, lo = split((buffer[row : row + CHUNK, :] - shift) * weights)
            high[row : row + CHUNK, :] = hi
            low[row : row + CHUNK, :] = lo
            e_hi[here] = hi
            e_lo[here] = lo

    def query_grad_block(turn, high, low):
        at = pl.multiple_of(turn * 256, 256)
        grad = by_columns(kt, high[...], low[...]) * SCALE
        for half in range(2):
            begin = pl.multiple_of(at + half * DIM, DIM)
            got[SLOT[QUERY], pl.ds(begin, DIM), :] = grad[:, half * DIM : (half + 1) * DIM].T

    give_queries = give_pair(QUERY)
    prob_grad_block(0, score_a)
    prob_grad_block(1, score_b)
    score_grad_block(0, score_a, hi_a, lo_a)

    def gradient_pair(pair, carry):
        turn = 2 * pair + 1
        prob_grad_block(turn + 1, score_a)
        score_grad_block(turn, score_b, hi_b, lo_b)
        query_grad_block(turn - 1, hi_a, lo_a)
        prob_grad_block(turn + 2, score_b)
        score_grad_block(turn + 1, score_a, hi_a, lo_a)
        query_grad_block(turn, hi_b, lo_b)
        give_queries(turn - 1)
        give_queries(turn)
        pl.when(pair == 1)(exchange_losses)
        return carry

    last = shards // 2 - 1
    lax.fori_loop(0, last // 2, gradient_pair, 0)
    score_grad_block(last, score_b, hi_b, lo_b)
    query_grad_block(last - 1, hi_a, lo_a)
    query_grad_block(last, hi_b, lo_b)
    give_queries(last - 1)
    give_queries(last)

    def exchange_sums():
        if copies > 1:
            wait_small(small_recv.at[2], stage2, copies - 1, shards + 4)
        sums = jnp.zeros((2, DIM), F32)
        for other in range(copies):
            sums = sums + stage2[other, shards : shards + 2, :]
        tile3[0:2, :] = sums
        stage3[me, 0:2, :] = sums
        for peer in peers:
            pltpu.make_async_remote_copy(
                tile3.at[pl.ds(0, 2)], stage3.at[me, pl.ds(0, 2)], small_send.at[3], small_recv.at[3],
                device_id={"seq": peer}, device_id_type=MESH,
            ).start()

    def key_grad_block(turn, carry):
        block = turn
        at = pl.multiple_of(block * 512, 512)
        got[SLOT[KEY], pl.ds(at, 512), :] = by_rows(at, q3.at[:, DIM : 3 * DIM]) * (1.0 / LOG2E)
        for quarter in range(4):
            give(KEY, block * 4 + quarter)
        pl.when(turn == 1)(exchange_sums)
        return carry

    lax.fori_loop(0, shards // 4, key_grad_block, 0)

    by_sample = jnp.concatenate(
        [
            jnp.concatenate([stage2[other, row : row + 1, :] for row in (shards + 2, shards + 3)], axis=1)
            for other in range(copies)
        ],
        axis=0,
    )
    by_frequency = by_sample.T
    for head in range(shards):
        gains = jnp.concatenate([stage2[other, head : head + 1, :] for other in range(copies)], axis=0)
        weight_out[:, head * DIM : (head + 1) * DIM] = lax.dot_general(
            by_frequency, gains, (((1,), (0,)), ((), ())), precision=HIGHEST, preferred_element_type=F32
        )
    wait_small(small_recv.at[3], stage3, shards - 1)
    sums = jnp.zeros((2, DIM), F32)
    for shard in range(shards):
        sums = sums + stage3[shard, 0:2, :]
    mean = sums[0:1, :] / jnp.maximum(sums[1:2, :], 1.0)
    updated = meta[MIX : MIX + 1, :] * (1.0 + RATE * mean)
    updated = jnp.where(lane < BUCKETS, updated, 0.0)
    mixture = BUCKETS * updated / jnp.sum(updated, axis=1, keepdims=True)
    mix_out[...] = mixture[:, :BUCKETS]

    others = (shards - 1) * DIM
    for part in (KEY, QUERY, VALUE, AIM):
        if part in (VALUE, AIM):
            wait_sent(part)
        sent = got.at[SLOT[part], pl.ds(0, others), :]
        pltpu.make_async_copy(sent, sent, back_send.at[part]).wait()
        base = att_out if part == AIM else grad_out
        landed = base.at[:, PART_COLUMN[part] : PART_COLUMN[part] + WIDTH]
        pltpu.make_async_copy(landed, landed, back_recv.at[part]).wait()
    wait_small(small_send.at[0], meta_all, shards - 1)
    wait_small(small_send.at[1], stage1, shards - 1)
    if copies > 1:
        wait_small(small_send.at[2], stage2, copies - 1, shards + 4)
    wait_small(small_send.at[3], stage3, shards - 1)


def move_out(*refs):
    count = len(refs) // 2
    sources, outputs, sems = refs[:count], refs[count : 2 * count], refs[-1]
    moves = []
    for source, output in zip(sources, outputs):
        pieces = 8 if source.shape[0] >= DIM else 1
        rows = source.shape[0] // pieces
        for piece in range(pieces):
            part = pl.ds(piece * rows, rows)
            moves.append(pltpu.make_async_copy(source.at[part], output.at[part], sems.at[len(moves)]))
    for move in moves:
        move.start()
    for move in moves:
        move.wait()


def body(reader_rows, reader_targets, dest_pos, bucket_ids, ref_loss, timesteps, mod_weight, mixture_old):
    shards, copies = lax.axis_size("seq"), lax.axis_size("dp")
    length = shards * DIM
    half = FREQ_DIM // 2
    frequency = np.exp(-math.log(10000.0) * np.arange(half) / half).astype(np.float32)[None, :]
    any_spec = pl.BlockSpec(memory_space=pl.ANY)
    vmem_spec = pl.BlockSpec(memory_space=pltpu.VMEM)
    dma = pltpu.SemaphoreType.DMA
    attended, grads, weight_grad, mixture = pl.pallas_call(
        functools.partial(kernel, shards, copies),
        out_shape=(
            pltpu.VMEM((DIM, WIDTH), F32),
            pltpu.VMEM((DIM, 3 * WIDTH), F32),
            pltpu.VMEM((FREQ_DIM, WIDTH), F32),
            pltpu.VMEM((1, BUCKETS), F32),
        ),
        in_specs=[any_spec] * 9,
        out_specs=(vmem_spec, vmem_spec, vmem_spec, vmem_spec),
        scratch_shapes=[
            pltpu.VMEM((1, DIM), jnp.int32),
            pltpu.VMEM((1, DIM), jnp.int32),
            pltpu.VMEM((1, DIM), F32),
            pltpu.VMEM((1, DIM), F32),
            pltpu.SMEM((1,), jnp.int32),
            pltpu.SMEM((BUCKETS,), F32),
            pltpu.VMEM((8, DIM), F32),
            pltpu.VMEM((shards, 8, DIM), F32),
            pltpu.VMEM((4, length, DIM), F32),
            pltpu.VMEM((FREQ_DIM, DIM), F32),
            pltpu.VMEM((length, length), BF16),
            pltpu.VMEM((length, 2 * DIM), BF16),
            pltpu.VMEM((length, 3 * DIM), BF16),
            pltpu.VMEM((2 * DIM, length), BF16),
            pltpu.VMEM((length, 3 * DIM), BF16),
            pltpu.VMEM((length, 3 * DIM), BF16),
            pltpu.VMEM((2 * DIM, length), BF16),
            pltpu.VMEM((length, 3 * DIM), BF16),
            pltpu.VMEM((length, length), BF16),
            pltpu.VMEM((length, length), BF16),
            pltpu.VMEM((DIM, length), F32),
            pltpu.VMEM((8, length), F32),
            pltpu.VMEM((8, length), F32),
            pltpu.VMEM((DIM, DIM), F32),
            pltpu.VMEM((length, 256), F32),
            pltpu.VMEM((length, 256), F32),
            pltpu.VMEM((shards, 8, DIM), F32),
            pltpu.VMEM((shards, 8, DIM), F32),
            pltpu.VMEM((shards, 8, DIM), F32),
            pltpu.VMEM((copies, shards + 8, DIM), F32),
            pltpu.VMEM((shards + 8, DIM), F32),
            pltpu.VMEM((shards, 8, DIM), F32),
            pltpu.VMEM((8, DIM), F32),
            dma((4,)), dma((4,)), dma((4,)), dma((4,)), dma((4,)), dma((4,)), dma, dma((6,)),
        ],
        compiler_params=pltpu.CompilerParams(
            collective_id=0, has_side_effects=True, vmem_limit_bytes=56 * 1024 * 1024
        ),
        name="attend",
    )(reader_rows[0], reader_targets[0], dest_pos, bucket_ids, ref_loss, timesteps, mixture_old, frequency, mod_weight)
    results = (attended, grads, weight_grad, mixture)
    attended, grads, weight_grad, mixture = pl.pallas_call(
        move_out,
        out_shape=tuple(jax.ShapeDtypeStruct(item.shape, F32) for item in results),
        in_specs=[vmem_spec] * 4,
        out_specs=(any_spec,) * 4,
        scratch_shapes=[dma((25,))],
        compiler_params=pltpu.CompilerParams(vmem_limit_bytes=1024 * 1024),
        name="move_out",
    )(*(pltpu.with_memory_space_constraint(item, pltpu.VMEM) for item in results))
    return attended[None], grads[None], weight_grad, mixture[0]


def solution(mesh):
    return jax.shard_map(
        body,
        mesh=mesh,
        in_specs=(
            P("dp", "seq", None), P("dp", "seq", None), P("dp", "seq"), P("dp", "seq"),
            P("dp", "seq"), P("dp"), P(), P(),
        ),
        out_specs=(P("dp", "seq", None), P("dp", "seq", None), P(), P()),
        check_vma=False,
    )
```

```python
import functools
import math

import jax
import jax.numpy as jnp
import numpy as np
from jax import lax
from jax.experimental import pallas as pl
from jax.experimental.pallas import tpu as pltpu
from jax.sharding import PartitionSpec as P

HEADS = 16
DIM = 128
FREQ_DIM = 256
BUCKETS = 16
WIDTH = HEADS * DIM
RATE = 10.0
CHUNK = 64
LOG2E = 1.4426950408889634
SCALE = DIM ** (-0.5)
MESH = pl.DeviceIdType.MESH
HIGHEST = lax.Precision.HIGHEST
BF16 = jnp.bfloat16
F32 = jnp.float32

POS, WEIGHT, BUCKET, REF, EMB, MIX = 0, 1, 2, 3, 4, 6
KEY, QUERY, VALUE, AIM = 0, 1, 2, 3
SLOT = {AIM: KEY, VALUE: QUERY, QUERY: VALUE, KEY: AIM}
PART_COLUMN = {KEY: WIDTH, QUERY: 0, VALUE: 2 * WIDTH, AIM: 0}


def split(x):
    hi = x.astype(BF16)
    return hi, (x - hi.astype(F32)).astype(BF16)


def dot(a, b):
    return lax.dot_general(a, b, (((1,), (0,)), ((), ())), preferred_element_type=F32)


def dot_nt(a, b):
    return lax.dot_general(a, b, (((1,), (1,)), ((), ())), preferred_element_type=F32)


def kernel(
    shards, copies, rows, aims, places_in, buckets_in, ref_in, steps_in, old_in, frequency_in, mod_w,
    back_out, weight_out, mix_out,
    places, buckets, ref_row, frequency, steps, old, meta, meta_all, got, mod_buf, perm, cat, k3, kt, q3, v3, vt, u3, e_hi, e_lo, head_out, inv_sum, delta,
    gain_sum, score_a, score_b, loss_rows, stage1, tile1, stage2, tile2, stage3, tile3,
    send_sem, recv_sem, back_send, back_recv, small_send, small_recv, mod_sem, operand_sem,
):
    length = shards * DIM
    me = lax.axis_index("seq")
    sample = lax.axis_index("dp")
    my_z, my_y = me // 4, lax.rem(me, 4)

    side = 1 - 2 * lax.rem(sample, 2)

    def shard_at(slot):
        along, shift = lax.rem(slot, 4), slot // 4
        return lax.rem(my_z + 4 + side * along, 4) * 4 + lax.rem(my_y + 8 + side * (along + shift), 4)

    peers = [shard_at(slot) for slot in range(1, shards)]

    barrier = pltpu.get_barrier_semaphore()
    for peer in peers:
        pl.semaphore_signal(barrier, inc=1, device_id={"seq": peer}, device_id_type=MESH)
    for turn in range(1, copies):
        other = lax.rem(sample + turn, copies)
        pl.semaphore_signal(barrier, inc=1, device_id={"dp": other}, device_id_type=MESH)

    operands = [
        pltpu.make_async_copy(source, into, operand_sem.at[index])
        for index, (source, into) in enumerate(
            (
                (places_in, places), (buckets_in, buckets), (ref_in, ref_row), (frequency_in, frequency),
                (steps_in, steps), (old_in, old),
            )
        )
    ]
    for operand in operands:
        operand.start()
    mod_copy = pltpu.make_async_copy(
        mod_w.at[:, pl.ds(pl.multiple_of(me * DIM, DIM), DIM)], mod_buf, mod_sem
    )
    mod_copy.start()
    pl.semaphore_wait(barrier, shards - 1 + copies - 1)

    def source(part, head):
        base = aims if part == AIM else rows
        return base.at[:, pl.ds(pl.multiple_of(PART_COLUMN[part] + head * DIM, DIM), DIM)]

    def landing(part):
        return got.at[part, pl.ds(pl.multiple_of(me * DIM, DIM), DIM), :]

    def send(part):
        pltpu.make_async_copy(source(part, me), landing(part), recv_sem.at[part]).start()
        for peer in peers:
            pltpu.make_async_remote_copy(
                source(part, peer), landing(part), send_sem.at[part], recv_sem.at[part],
                device_id={"seq": peer}, device_id_type=MESH,
            ).start()

    def wait_sent(part):
        sent = got.at[part, pl.ds(0, (shards - 1) * DIM), :]
        pltpu.make_async_copy(sent, sent, send_sem.at[part]).wait()

    send(KEY)

    for operand in operands:
        operand.wait()
    meta[POS : POS + 1, :] = places[...].astype(F32)
    bucket_row = buckets[...]
    lane = lax.broadcasted_iota(jnp.int32, (1, DIM), 1)
    weight_row = jnp.zeros((1, DIM), F32)
    old_row = jnp.zeros((1, DIM), F32)
    for bucket in range(BUCKETS):
        weight_row = weight_row + jnp.where(bucket_row == bucket, old[bucket], 0.0)
        old_row = old_row + jnp.where(lane == bucket, old[bucket], 0.0)
    meta[WEIGHT : WEIGHT + 1, :] = weight_row
    meta[BUCKET : BUCKET + 1, :] = bucket_row.astype(F32)
    meta[REF : REF + 1, :] = ref_row[...]
    angles = steps[0].astype(F32) * frequency[...]
    for row, wave in ((EMB, jnp.cos(angles)), (EMB + 1, jnp.sin(angles))):
        meta[row : row + 1, :] = wave / (1.0 + jnp.exp(-wave))
    meta[MIX : MIX + 1, :] = old_row
    meta[MIX + 1 : MIX + 2, :] = jnp.zeros((1, DIM), F32)
    meta_all[me] = meta[...]
    for peer in peers:
        pltpu.make_async_remote_copy(
            meta.at[pl.ds(0, 2)], meta_all.at[me, pl.ds(0, 2)], small_send.at[0], small_recv.at[0],
            device_id={"seq": peer}, device_id_type=MESH,
        ).start()
    send(QUERY)

    def wait_small(sem, buffer, count, depth=2):
        taken = buffer.at[pl.ds(0, count), pl.ds(0, depth)]
        pltpu.make_async_copy(taken, taken, sem).wait()

    mod_copy.wait()
    embedding = jnp.concatenate([meta[EMB : EMB + 1, :], meta[EMB + 1 : EMB + 2, :]], axis=1)
    embedding = jnp.broadcast_to(embedding, (8, FREQ_DIM))
    gain_row = 1.0 + lax.dot_general(
        embedding, mod_buf[...], (((1,), (0,)), ((), ())), precision=HIGHEST, preferred_element_type=F32
    )
    gain = jnp.broadcast_to(gain_row[0:1, :], (DIM, DIM)).T

    wait_small(small_recv.at[0], meta_all, shards - 1)

    def perm_block(block, carry):
        at = pl.multiple_of(block * 256, 256)
        inside = lax.broadcasted_iota(jnp.int32, (DIM, DIM), 0)
        place = jnp.concatenate([inside + shard_at(2 * block + half) * DIM for half in range(2)], axis=0).astype(F32)
        for shard in range(shards):
            hit = place == meta_all[shard, POS : POS + 1, :]
            perm[pl.ds(at, 256), shard * DIM : (shard + 1) * DIM] = jnp.where(hit, 1.0, 0.0).astype(BF16)
        return carry

    lax.fori_loop(0, length // 256, perm_block, 0)

    def pipeline(count, make, use, finish=None):
        def both(at, last):
            make(at + 1, score_b)
            use(at, score_a)
            if not last:
                make(at + 2, score_a)
            use(at + 1, score_b)
            if finish is not None:
                finish(at)
                finish(at + 1)

        def one(pair, carry):
            both(2 * pair, False)
            return carry

        make(0, score_a)
        lax.fori_loop(0, count // 2 - 1, one, 0)
        both(count - 2, True)

    def arrive(part, factor):
        pltpu.make_async_copy(got.at[part], got.at[part], recv_sem.at[part]).wait()

        def one(block, carry):
            at = pl.multiple_of(block * 256, 256)
            hi, lo = split(got[part, pl.ds(at, 256), :] * factor)
            cat[pl.ds(at, 256), 0:DIM] = hi
            cat[pl.ds(at, 256), DIM : 2 * DIM] = lo
            return carry

        lax.fori_loop(0, length // 256, one, 0)

    def reorder(part, factor, into, transposed):
        arrive(part, factor)

        def make(block, buffer):
            at = pl.multiple_of(block * 512, 512)
            buffer[0:512, :] = dot(perm[pl.ds(at, 512), :], cat[...])

        def use(block, buffer):
            at = pl.multiple_of(block * 512, 512)
            placed = buffer[0:512, :]
            hi, lo = placed[:, :DIM].astype(BF16), placed[:, DIM:].astype(BF16)
            into[pl.ds(at, 512), 0:DIM] = hi
            into[pl.ds(at, 512), DIM : 2 * DIM] = hi if part == QUERY else lo
            into[pl.ds(at, 512), 2 * DIM : 3 * DIM] = lo if part == QUERY else hi
            if transposed is not None:
                hi, lo = split((placed[:, :DIM] + placed[:, DIM:]).T)
                transposed[0:DIM, pl.ds(at, 512)] = hi
                transposed[DIM : 2 * DIM, pl.ds(at, 512)] = lo

        pipeline(length // 512, make, use)

    def by_columns(left, high, low):
        full = dot(left[...], high)
        return full[:DIM] + full[DIM:] + dot(left[0:DIM, :], low)

    def by_rows(at, right):
        full = dot(e_hi[pl.ds(at, 512), :], right[...])
        return full[:, :DIM] + full[:, DIM:] + dot(e_lo[pl.ds(at, 512), :], right[:, 0:DIM])

    wait_sent(KEY)
    send(VALUE)
    reorder(KEY, 1.0, k3, kt)
    wait_sent(QUERY)
    send(AIM)
    reorder(QUERY, SCALE * LOG2E, q3, None)

    def score_block(block, buffer):
        at = pl.multiple_of(block * 256, 256)
        buffer[...] = dot_nt(k3[...], q3[pl.ds(at, 256), :])

    def softmax_block(block, buffer):
        at = pl.multiple_of(block * 256, 256)
        top = jnp.full((8, 256), -jnp.inf, F32)
        for row in range(0, length, CHUNK):
            top = jnp.maximum(top, jnp.max(buffer[row : row + CHUNK, :].reshape(CHUNK // 8, 8, 256), axis=0))
        top = jnp.max(top, axis=0, keepdims=True)
        sums = jnp.zeros((8, 256), F32)
        for row in range(0, length, CHUNK):
            weights = jnp.exp2(buffer[row : row + CHUNK, :] - top)
            sums = sums + jnp.sum(weights.reshape(CHUNK // 8, 8, 256), axis=0)
            hi, lo = split(weights)
            e_hi[row : row + CHUNK, pl.ds(at, 256)] = hi
            e_lo[row : row + CHUNK, pl.ds(at, 256)] = lo
        inv_sum[:, pl.ds(at, 256)] = jnp.broadcast_to(1.0 / jnp.sum(sums, axis=0, keepdims=True), (8, 256))

    pipeline(length // 256, score_block, softmax_block)

    def target(part):
        return back_out.at[part, me]

    def give(part, slot):
        block = got.at[SLOT[part], pl.ds(pl.multiple_of(slot * DIM, DIM), DIM), :]
        shard = shard_at(slot)

        @pl.when(shard != me)
        def _():
            pltpu.make_async_remote_copy(
                block, target(part), back_send.at[part], back_recv.at[part],
                device_id={"seq": shard}, device_id_type=MESH,
            ).start()

        @pl.when(shard == me)
        def _():
            pltpu.make_async_copy(block, target(part), back_recv.at[part]).start()

    reorder(VALUE, 1.0, v3, vt)

    def output_block(turn, buffer):
        at = pl.multiple_of(turn * 256, 256)
        buffer[0:DIM, :] = by_columns(vt, e_hi[:, pl.ds(at, 256)], e_lo[:, pl.ds(at, 256)])

    def attended_block(turn, buffer):
        at = pl.multiple_of(turn * 256, 256)
        out = buffer[0:DIM, :] * inv_sum[0:1, pl.ds(at, 256)]
        head_out[:, pl.ds(at, 256)] = out
        for half in range(2):
            begin = pl.multiple_of(at + half * DIM, DIM)
            got[SLOT[AIM], pl.ds(begin, DIM), :] = (gain * out[:, half * DIM : (half + 1) * DIM]).T

    def give_pair(part):
        def finish(turn):
            for half in range(2):
                give(part, turn * 2 + half)

        return finish

    pipeline(shards // 2, output_block, attended_block, give_pair(AIM))

    arrive(AIM, 1.0)

    def aim_block(block, buffer):
        at = pl.multiple_of(block * 512, 512)
        buffer[0:512, :] = dot(perm[pl.ds(at, 512), :], cat[...])

    gain_sum[...] = jnp.zeros((DIM, DIM), F32)

    def upstream_block(block, buffer):
        at = pl.multiple_of(block * 512, 512)
        placed = buffer[0:512, :]
        aim = placed[:, :DIM] + placed[:, DIM:]
        total = jnp.zeros((DIM, DIM), F32)
        for quarter in range(4):
            slot = block * 4 + quarter
            begin = pl.multiple_of(at + quarter * DIM, DIM)
            out = head_out[:, pl.ds(begin, DIM)]
            gap = gain * out - aim[quarter * DIM : (quarter + 1) * DIM, :].T
            loss_rows[slot] = jnp.broadcast_to(jnp.sum(gap * gap, axis=0, keepdims=True), (8, DIM))
            up_a = gap * meta_all[shard_at(slot), WEIGHT : WEIGHT + 1, :]
            total = total + up_a * out
            up = gain * up_a * inv_sum[0:1, pl.ds(begin, DIM)]
            delta[:, pl.ds(begin, DIM)] = jnp.broadcast_to(jnp.sum(up * out, axis=0, keepdims=True), (8, DIM))
            hi, lo = split(up.T)
            u3[pl.ds(begin, DIM), 0:DIM] = hi
            u3[pl.ds(begin, DIM), DIM : 2 * DIM] = hi
            u3[pl.ds(begin, DIM), 2 * DIM : 3 * DIM] = lo
        gain_sum[...] += total

    pipeline(length // 512, aim_block, upstream_block)

    gain_grad = jnp.sum(gain_sum[...].T, axis=0, keepdims=True)
    row_index = lax.broadcasted_iota(jnp.int32, (8, DIM), 0)
    for slot in range(shards):
        tile1[slot] = jnp.where(row_index == 0, loss_rows[slot], jnp.broadcast_to(gain_grad, (8, DIM)))
    stage1[me] = tile1[0]
    for slot, peer in enumerate(peers):
        pltpu.make_async_remote_copy(
            tile1.at[slot + 1, pl.ds(0, 2)], stage1.at[me, pl.ds(0, 2)], small_send.at[1], small_recv.at[1],
            device_id={"seq": peer}, device_id_type=MESH,
        ).start()

    def value_grad_block(turn, carry):
        block = turn
        at = pl.multiple_of(block * 512, 512)
        got[SLOT[VALUE], pl.ds(at, 512), :] = by_rows(at, u3.at[:, DIM : 3 * DIM])
        for quarter in range(4):
            give(VALUE, block * 4 + quarter)
        return carry

    lax.fori_loop(0, shards // 4, value_grad_block, 0)

    def exchange_losses():
        wait_small(small_recv.at[1], stage1, shards - 1)
        loss = jnp.zeros((1, DIM), F32)
        for shard in range(shards):
            loss = loss + stage1[shard, 0:1, :]
        excess = jnp.maximum(0.5 * loss / WIDTH - meta[REF : REF + 1, :], 0.0)
        hit = lax.broadcasted_iota(jnp.int32, (DIM, DIM), 0).astype(F32) == meta[BUCKET : BUCKET + 1, :]
        sums = lax.dot_general(
            jnp.where(row_index == 0, jnp.broadcast_to(excess, (8, DIM)), 1.0), jnp.where(hit, 1.0, 0.0),
            (((1,), (1,)), ((), ())), precision=HIGHEST, preferred_element_type=F32,
        )
        for shard in range(shards):
            tile2[shard : shard + 1, :] = stage1[shard, 1:2, :]
        tile2[shards : shards + 2, :] = sums[0:2, :]
        tile2[shards + 2 : shards + 4, :] = meta[EMB : EMB + 2, :]
        stage2[sample] = tile2[...]
        for turn in range(1, copies):
            other = lax.rem(sample + turn, copies)
            pltpu.make_async_remote_copy(
                tile2.at[pl.ds(0, shards + 4)], stage2.at[sample, pl.ds(0, shards + 4)], small_send.at[2], small_recv.at[2],
                device_id={"dp": other}, device_id_type=MESH,
            ).start()

    hi_a, lo_a, hi_b, lo_b = (perm.at[:, at : at + 256] for at in range(0, 1024, 256))

    def prob_grad_block(turn, buffer):
        at = pl.multiple_of(turn * 256, 256)
        buffer[...] = dot_nt(v3[...], u3[pl.ds(at, 256), :])

    def score_grad_block(turn, buffer, high, low):
        at = pl.multiple_of(turn * 256, 256)
        shift = delta[0:1, pl.ds(at, 256)]
        for row in range(0, length, CHUNK):
            here = (slice(row, row + CHUNK), pl.ds(at, 256))
            weights = e_hi[here].astype(F32) + e_lo[here].astype(F32)
            hi, lo = split((buffer[row : row + CHUNK, :] - shift) * weights)
            high[row : row + CHUNK, :] = hi
            low[row : row + CHUNK, :] = lo
            e_hi[here] = hi
            e_lo[here] = lo

    def query_grad_block(turn, high, low):
        at = pl.multiple_of(turn * 256, 256)
        grad = by_columns(kt, high[...], low[...]) * SCALE
        for half in range(2):
            begin = pl.multiple_of(at + half * DIM, DIM)
            got[SLOT[QUERY], pl.ds(begin, DIM), :] = grad[:, half * DIM : (half + 1) * DIM].T

    give_queries = give_pair(QUERY)
    prob_grad_block(0, score_a)
    prob_grad_block(1, score_b)
    score_grad_block(0, score_a, hi_a, lo_a)

    def gradient_pair(pair, carry):
        turn = 2 * pair + 1
        prob_grad_block(turn + 1, score_a)
        score_grad_block(turn, score_b, hi_b, lo_b)
        query_grad_block(turn - 1, hi_a, lo_a)
        prob_grad_block(turn + 2, score_b)
        score_grad_block(turn + 1, score_a, hi_a, lo_a)
        query_grad_block(turn, hi_b, lo_b)
        give_queries(turn - 1)
        give_queries(turn)
        pl.when(pair == 1)(exchange_losses)
        return carry

    last = shards // 2 - 1
    lax.fori_loop(0, last // 2, gradient_pair, 0)
    score_grad_block(last, score_b, hi_b, lo_b)
    query_grad_block(last - 1, hi_a, lo_a)
    query_grad_block(last, hi_b, lo_b)
    give_queries(last - 1)
    give_queries(last)

    def exchange_sums():
        if copies > 1:
            wait_small(small_recv.at[2], stage2, copies - 1, shards + 4)
        sums = jnp.zeros((2, DIM), F32)
        for other in range(copies):
            sums = sums + stage2[other, shards : shards + 2, :]
        tile3[0:2, :] = sums
        stage3[me, 0:2, :] = sums
        for peer in peers:
            pltpu.make_async_remote_copy(
                tile3.at[pl.ds(0, 2)], stage3.at[me, pl.ds(0, 2)], small_send.at[3], small_recv.at[3],
                device_id={"seq": peer}, device_id_type=MESH,
            ).start()

    def key_grad_block(turn, carry):
        block = turn
        at = pl.multiple_of(block * 512, 512)
        got[SLOT[KEY], pl.ds(at, 512), :] = by_rows(at, q3.at[:, DIM : 3 * DIM]) * (1.0 / LOG2E)
        for quarter in range(4):
            give(KEY, block * 4 + quarter)
        pl.when(turn == 1)(exchange_sums)
        return carry

    lax.fori_loop(0, shards // 4, key_grad_block, 0)

    by_sample = jnp.concatenate(
        [
            jnp.concatenate([stage2[other, row : row + 1, :] for row in (shards + 2, shards + 3)], axis=1)
            for other in range(copies)
        ],
        axis=0,
    )
    by_frequency = by_sample.T
    for head in range(shards):
        gains = jnp.concatenate([stage2[other, head : head + 1, :] for other in range(copies)], axis=0)
        weight_out[:, head * DIM : (head + 1) * DIM] = lax.dot_general(
            by_frequency, gains, (((1,), (0,)), ((), ())), precision=HIGHEST, preferred_element_type=F32
        )
    wait_small(small_recv.at[3], stage3, shards - 1)
    sums = jnp.zeros((2, DIM), F32)
    for shard in range(shards):
        sums = sums + stage3[shard, 0:2, :]
    mean = sums[0:1, :] / jnp.maximum(sums[1:2, :], 1.0)
    updated = meta[MIX : MIX + 1, :] * (1.0 + RATE * mean)
    updated = jnp.where(lane < BUCKETS, updated, 0.0)
    mixture = BUCKETS * updated / jnp.sum(updated, axis=1, keepdims=True)
    mix_out[...] = mixture[:, :BUCKETS]

    others = (shards - 1) * DIM
    for part in (KEY, QUERY, VALUE, AIM):
        if part in (VALUE, AIM):
            wait_sent(part)
        sent = got.at[SLOT[part], pl.ds(0, others), :]
        pltpu.make_async_copy(sent, sent, back_send.at[part]).wait()
        pltpu.make_async_copy(back_out.at[part], back_out.at[part], back_recv.at[part]).wait()
    wait_small(small_send.at[0], meta_all, shards - 1)
    wait_small(small_send.at[1], stage1, shards - 1)
    if copies > 1:
        wait_small(small_send.at[2], stage2, copies - 1, shards + 4)
    wait_small(small_send.at[3], stage3, shards - 1)


def move_out(back, weight, mixture, att_out, grad_out, weight_out, mix_out, sems):
    for head in range(HEADS):
        for part in (KEY, QUERY, VALUE, AIM):
            base = att_out if part == AIM else grad_out
            columns = pl.ds(PART_COLUMN[part] + head * DIM, DIM)
            pltpu.make_async_copy(back.at[part, head], base.at[:, columns], sems.at[part]).start()
    others = [
        pltpu.make_async_copy(weight, weight_out, sems.at[4]),
        pltpu.make_async_copy(mixture, mix_out, sems.at[5]),
    ]
    for other in others:
        other.start()
    for other in others:
        other.wait()
    for part in (KEY, QUERY, VALUE, AIM):
        pltpu.make_async_copy(back.at[part], back.at[part], sems.at[part]).wait()


def body(reader_rows, reader_targets, dest_pos, bucket_ids, ref_loss, timesteps, mod_weight, mixture_old):
    shards, copies = lax.axis_size("seq"), lax.axis_size("dp")
    length = shards * DIM
    half = FREQ_DIM // 2
    frequency = np.exp(-math.log(10000.0) * np.arange(half) / half).astype(np.float32)[None, :]
    any_spec = pl.BlockSpec(memory_space=pl.ANY)
    vmem_spec = pl.BlockSpec(memory_space=pltpu.VMEM)
    dma = pltpu.SemaphoreType.DMA
    results = pl.pallas_call(
        functools.partial(kernel, shards, copies),
        out_shape=(
            pltpu.VMEM((4, HEADS, DIM, DIM), F32),
            pltpu.VMEM((FREQ_DIM, WIDTH), F32),
            pltpu.VMEM((1, BUCKETS), F32),
        ),
        in_specs=[any_spec] * 9,
        out_specs=(vmem_spec, vmem_spec, vmem_spec),
        scratch_shapes=[
            pltpu.VMEM((1, DIM), jnp.int32),
            pltpu.VMEM((1, DIM), jnp.int32),
            pltpu.VMEM((1, DIM), F32),
            pltpu.VMEM((1, DIM), F32),
            pltpu.SMEM((1,), jnp.int32),
            pltpu.SMEM((BUCKETS,), F32),
            pltpu.VMEM((8, DIM), F32),
            pltpu.VMEM((shards, 8, DIM), F32),
            pltpu.VMEM((4, length, DIM), F32),
            pltpu.VMEM((FREQ_DIM, DIM), F32),
            pltpu.VMEM((length, length), BF16),
            pltpu.VMEM((length, 2 * DIM), BF16),
            pltpu.VMEM((length, 3 * DIM), BF16),
            pltpu.VMEM((2 * DIM, length), BF16),
            pltpu.VMEM((length, 3 * DIM), BF16),
            pltpu.VMEM((length, 3 * DIM), BF16),
            pltpu.VMEM((2 * DIM, length), BF16),
            pltpu.VMEM((length, 3 * DIM), BF16),
            pltpu.VMEM((length, length), BF16),
            pltpu.VMEM((length, length), BF16),
            pltpu.VMEM((DIM, length), F32),
            pltpu.VMEM((8, length), F32),
            pltpu.VMEM((8, length), F32),
            pltpu.VMEM((DIM, DIM), F32),
            pltpu.VMEM((length, 256), F32),
            pltpu.VMEM((length, 256), F32),
            pltpu.VMEM((shards, 8, DIM), F32),
            pltpu.VMEM((shards, 8, DIM), F32),
            pltpu.VMEM((shards, 8, DIM), F32),
            pltpu.VMEM((copies, shards + 8, DIM), F32),
            pltpu.VMEM((shards + 8, DIM), F32),
            pltpu.VMEM((shards, 8, DIM), F32),
            pltpu.VMEM((8, DIM), F32),
            dma((4,)), dma((4,)), dma((4,)), dma((4,)), dma((4,)), dma((4,)), dma, dma((6,)),
        ],
        compiler_params=pltpu.CompilerParams(
            collective_id=0, has_side_effects=True, vmem_limit_bytes=56 * 1024 * 1024
        ),
        name="attend",
    )(reader_rows[0], reader_targets[0], dest_pos, bucket_ids, ref_loss, timesteps, mixture_old, frequency, mod_weight)
    attended, grads, weight_grad, mixture = pl.pallas_call(
        move_out,
        out_shape=tuple(
            jax.ShapeDtypeStruct(shape, F32)
            for shape in ((DIM, WIDTH), (DIM, 3 * WIDTH), (FREQ_DIM, WIDTH), (1, BUCKETS))
        ),
        in_specs=[vmem_spec] * 3,
        out_specs=(any_spec,) * 4,
        scratch_shapes=[dma((6,))],
        compiler_params=pltpu.CompilerParams(vmem_limit_bytes=1024 * 1024),
        name="move_out",
    )(*(pltpu.with_memory_space_constraint(item, pltpu.VMEM) for item in results))
    return attended[None], grads[None], weight_grad, mixture[0]


def solution(mesh):
    return jax.shard_map(
        body,
        mesh=mesh,
        in_specs=(
            P("dp", "seq", None), P("dp", "seq", None), P("dp", "seq"), P("dp", "seq"),
            P("dp", "seq"), P("dp"), P(), P(),
        ),
        out_specs=(P("dp", "seq", None), P("dp", "seq", None), P(), P()),
        check_vma=False,
    )
```

```python
import functools
import math

import jax
import jax.numpy as jnp
import numpy as np
from jax import lax
from jax.experimental import pallas as pl
from jax.experimental.pallas import tpu as pltpu
from jax.sharding import PartitionSpec as P

HEADS = 16
DIM = 128
FREQ_DIM = 256
BUCKETS = 16
WIDTH = HEADS * DIM
RATE = 10.0
CHUNK = 64
LOG2E = 1.4426950408889634
SCALE = DIM ** (-0.5)
MESH = pl.DeviceIdType.MESH
HIGHEST = lax.Precision.HIGHEST
BF16 = jnp.bfloat16
F32 = jnp.float32

STEPS = (
    (0, 0), (2, 2), (0, 1), (1, 0), (0, 3), (3, 0), (1, 1), (1, 3),
    (3, 1), (3, 3), (0, 2), (2, 0), (1, 2), (2, 1), (3, 2), (2, 3),
)


def packed(axis, first):
    return sum(step[axis] * 4**digit for digit, step in enumerate(STEPS[first : first + 8]))


POS, WEIGHT, BUCKET, REF, EMB, MIX = 0, 1, 2, 3, 4, 6
KEY, QUERY, VALUE, AIM = 0, 1, 2, 3
SLOT = {AIM: KEY, VALUE: QUERY, QUERY: VALUE, KEY: AIM}
PART_COLUMN = {KEY: WIDTH, QUERY: 0, VALUE: 2 * WIDTH, AIM: 0}


def split(x):
    hi = x.astype(BF16)
    return hi, (x - hi.astype(F32)).astype(BF16)


def dot(a, b):
    return lax.dot_general(a, b, (((1,), (0,)), ((), ())), preferred_element_type=F32)


def dot_nt(a, b):
    return lax.dot_general(a, b, (((1,), (1,)), ((), ())), preferred_element_type=F32)


def kernel(
    shards, copies, rows, aims, places_in, buckets_in, ref_in, steps_in, old_in, frequency_in, mod_w,
    att_out, grad_out, weight_out, mix_out,
    places, buckets, ref_row, frequency, steps, old, meta, meta_all, got, mod_buf, perm, cat, k3, kt, q3, v3, vt, u3, e_hi, e_lo, head_out, inv_sum, delta,
    gain_sum, score_a, score_b, loss_rows, stage1, tile1, stage2, tile2, stage3, tile3,
    send_sem, recv_sem, back_send, back_recv, small_send, small_recv, mod_sem, operand_sem,
):
    length = shards * DIM
    me = lax.axis_index("seq")
    sample = lax.axis_index("dp")
    my_z, my_y = me // 4, lax.rem(me, 4)

    side = 1 - 2 * lax.rem(sample, 2)

    def step_at(axis, slot):
        if isinstance(slot, int):
            return STEPS[slot][axis]
        digits = jnp.where(slot < 8, packed(axis, 0), packed(axis, 8))
        return lax.shift_right_logical(digits, 2 * lax.rem(slot, 8)) & 3

    def shard_at(slot):
        along_z, along_y = step_at(0, slot), step_at(1, slot)
        return lax.rem(my_z + 4 + side * along_z, 4) * 4 + lax.rem(my_y + 4 + side * along_y, 4)

    peers = [shard_at(slot) for slot in range(1, shards)]

    barrier = pltpu.get_barrier_semaphore()
    for peer in peers:
        pl.semaphore_signal(barrier, inc=1, device_id={"seq": peer}, device_id_type=MESH)
    for turn in range(1, copies):
        other = lax.rem(sample + turn, copies)
        pl.semaphore_signal(barrier, inc=1, device_id={"dp": other}, device_id_type=MESH)

    operands = [
        pltpu.make_async_copy(source, into, operand_sem.at[index])
        for index, (source, into) in enumerate(
            (
                (places_in, places), (buckets_in, buckets), (ref_in, ref_row), (frequency_in, frequency),
                (steps_in, steps), (old_in, old),
            )
        )
    ]
    for operand in operands:
        operand.start()
    mod_copy = pltpu.make_async_copy(
        mod_w.at[:, pl.ds(pl.multiple_of(me * DIM, DIM), DIM)], mod_buf, mod_sem
    )
    mod_copy.start()
    pl.semaphore_wait(barrier, shards - 1 + copies - 1)

    def source(part, head):
        base = aims if part == AIM else rows
        return base.at[:, pl.ds(pl.multiple_of(PART_COLUMN[part] + head * DIM, DIM), DIM)]

    def landing(part):
        return got.at[part, pl.ds(pl.multiple_of(me * DIM, DIM), DIM), :]

    def send(part):
        pltpu.make_async_copy(source(part, me), landing(part), recv_sem.at[part]).start()
        for peer in peers:
            pltpu.make_async_remote_copy(
                source(part, peer), landing(part), send_sem.at[part], recv_sem.at[part],
                device_id={"seq": peer}, device_id_type=MESH,
            ).start()

    def wait_sent(part):
        sent = got.at[part, pl.ds(0, (shards - 1) * DIM), :]
        pltpu.make_async_copy(sent, sent, send_sem.at[part]).wait()

    send(KEY)

    for operand in operands:
        operand.wait()
    meta[POS : POS + 1, :] = places[...].astype(F32)
    bucket_row = buckets[...]
    lane = lax.broadcasted_iota(jnp.int32, (1, DIM), 1)
    weight_row = jnp.zeros((1, DIM), F32)
    old_row = jnp.zeros((1, DIM), F32)
    for bucket in range(BUCKETS):
        weight_row = weight_row + jnp.where(bucket_row == bucket, old[bucket], 0.0)
        old_row = old_row + jnp.where(lane == bucket, old[bucket], 0.0)
    meta[WEIGHT : WEIGHT + 1, :] = weight_row
    meta[BUCKET : BUCKET + 1, :] = bucket_row.astype(F32)
    meta[REF : REF + 1, :] = ref_row[...]
    angles = steps[0].astype(F32) * frequency[...]
    for row, wave in ((EMB, jnp.cos(angles)), (EMB + 1, jnp.sin(angles))):
        meta[row : row + 1, :] = wave / (1.0 + jnp.exp(-wave))
    meta[MIX : MIX + 1, :] = old_row
    meta[MIX + 1 : MIX + 2, :] = jnp.zeros((1, DIM), F32)
    meta_all[me] = meta[...]
    for peer in peers:
        pltpu.make_async_remote_copy(
            meta.at[pl.ds(0, 2)], meta_all.at[me, pl.ds(0, 2)], small_send.at[0], small_recv.at[0],
            device_id={"seq": peer}, device_id_type=MESH,
        ).start()
    send(QUERY)

    def wait_small(sem, buffer, count, depth=2):
        taken = buffer.at[pl.ds(0, count), pl.ds(0, depth)]
        pltpu.make_async_copy(taken, taken, sem).wait()

    mod_copy.wait()
    embedding = jnp.concatenate([meta[EMB : EMB + 1, :], meta[EMB + 1 : EMB + 2, :]], axis=1)
    embedding = jnp.broadcast_to(embedding, (8, FREQ_DIM))
    gain_row = 1.0 + lax.dot_general(
        embedding, mod_buf[...], (((1,), (0,)), ((), ())), precision=HIGHEST, preferred_element_type=F32
    )
    gain = jnp.broadcast_to(gain_row[0:1, :], (DIM, DIM)).T

    wait_small(small_recv.at[0], meta_all, shards - 1)

    def perm_block(block, carry):
        at = pl.multiple_of(block * 256, 256)
        inside = lax.broadcasted_iota(jnp.int32, (DIM, DIM), 0)
        place = jnp.concatenate([inside + shard_at(2 * block + half) * DIM for half in range(2)], axis=0).astype(F32)
        for shard in range(shards):
            hit = place == meta_all[shard, POS : POS + 1, :]
            perm[pl.ds(at, 256), shard * DIM : (shard + 1) * DIM] = jnp.where(hit, 1.0, 0.0).astype(BF16)
        return carry

    lax.fori_loop(0, length // 256, perm_block, 0)

    def pipeline(count, make, use, finish=None):
        def both(at, last):
            make(at + 1, score_b)
            use(at, score_a)
            if not last:
                make(at + 2, score_a)
            use(at + 1, score_b)
            if finish is not None:
                finish(at)
                finish(at + 1)

        def one(pair, carry):
            both(2 * pair, False)
            return carry

        make(0, score_a)
        lax.fori_loop(0, count // 2 - 1, one, 0)
        both(count - 2, True)

    def arrive(part, factor):
        pltpu.make_async_copy(got.at[part], got.at[part], recv_sem.at[part]).wait()

        def one(block, carry):
            at = pl.multiple_of(block * 256, 256)
            hi, lo = split(got[part, pl.ds(at, 256), :] * factor)
            cat[pl.ds(at, 256), 0:DIM] = hi
            cat[pl.ds(at, 256), DIM : 2 * DIM] = lo
            return carry

        lax.fori_loop(0, length // 256, one, 0)

    def reorder(part, factor, into, transposed):
        arrive(part, factor)

        def make(block, buffer):
            at = pl.multiple_of(block * 512, 512)
            buffer[0:512, :] = dot(perm[pl.ds(at, 512), :], cat[...])

        def use(block, buffer):
            at = pl.multiple_of(block * 512, 512)
            placed = buffer[0:512, :]
            hi, lo = placed[:, :DIM].astype(BF16), placed[:, DIM:].astype(BF16)
            into[pl.ds(at, 512), 0:DIM] = hi
            into[pl.ds(at, 512), DIM : 2 * DIM] = hi if part == QUERY else lo
            into[pl.ds(at, 512), 2 * DIM : 3 * DIM] = lo if part == QUERY else hi
            if transposed is not None:
                hi, lo = split((placed[:, :DIM] + placed[:, DIM:]).T)
                transposed[0:DIM, pl.ds(at, 512)] = hi
                transposed[DIM : 2 * DIM, pl.ds(at, 512)] = lo

        pipeline(length // 512, make, use)

    def by_columns(left, high, low):
        full = dot(left[...], high)
        return full[:DIM] + full[DIM:] + dot(left[0:DIM, :], low)

    def by_rows(at, right):
        full = dot(e_hi[pl.ds(at, 512), :], right[...])
        return full[:, :DIM] + full[:, DIM:] + dot(e_lo[pl.ds(at, 512), :], right[:, 0:DIM])

    wait_sent(KEY)
    send(VALUE)
    reorder(KEY, 1.0, k3, kt)
    wait_sent(QUERY)
    send(AIM)
    reorder(QUERY, SCALE * LOG2E, q3, None)

    def score_block(block, buffer):
        at = pl.multiple_of(block * 256, 256)
        buffer[...] = dot_nt(k3[...], q3[pl.ds(at, 256), :])

    def softmax_block(block, buffer):
        at = pl.multiple_of(block * 256, 256)
        top = jnp.full((8, 256), -jnp.inf, F32)
        for row in range(0, length, CHUNK):
            top = jnp.maximum(top, jnp.max(buffer[row : row + CHUNK, :].reshape(CHUNK // 8, 8, 256), axis=0))
        top = jnp.max(top, axis=0, keepdims=True)
        sums = jnp.zeros((8, 256), F32)
        for row in range(0, length, CHUNK):
            weights = jnp.exp2(buffer[row : row + CHUNK, :] - top)
            sums = sums + jnp.sum(weights.reshape(CHUNK // 8, 8, 256), axis=0)
            hi, lo = split(weights)
            e_hi[row : row + CHUNK, pl.ds(at, 256)] = hi
            e_lo[row : row + CHUNK, pl.ds(at, 256)] = lo
        inv_sum[:, pl.ds(at, 256)] = jnp.broadcast_to(1.0 / jnp.sum(sums, axis=0, keepdims=True), (8, 256))

    pipeline(length // 256, score_block, softmax_block)

    def target(part):
        base = att_out if part == AIM else grad_out
        return base.at[:, pl.ds(pl.multiple_of(PART_COLUMN[part] + me * DIM, DIM), DIM)]

    def give(part, slot):
        block = got.at[SLOT[part], pl.ds(pl.multiple_of(slot * DIM, DIM), DIM), :]
        shard = shard_at(slot)

        @pl.when(shard != me)
        def _():
            pltpu.make_async_remote_copy(
                block, target(part), back_send.at[part], back_recv.at[part],
                device_id={"seq": shard}, device_id_type=MESH,
            ).start()

        @pl.when(shard == me)
        def _():
            pltpu.make_async_copy(block, target(part), back_recv.at[part]).start()

    reorder(VALUE, 1.0, v3, vt)

    def output_block(turn, buffer):
        at = pl.multiple_of(turn * 256, 256)
        buffer[0:DIM, :] = by_columns(vt, e_hi[:, pl.ds(at, 256)], e_lo[:, pl.ds(at, 256)])

    def attended_block(turn, buffer):
        at = pl.multiple_of(turn * 256, 256)
        out = buffer[0:DIM, :] * inv_sum[0:1, pl.ds(at, 256)]
        head_out[:, pl.ds(at, 256)] = out
        for half in range(2):
            begin = pl.multiple_of(at + half * DIM, DIM)
            got[SLOT[AIM], pl.ds(begin, DIM), :] = (gain * out[:, half * DIM : (half + 1) * DIM]).T

    def give_pair(part):
        def finish(turn):
            for half in range(2):
                give(part, turn * 2 + half)

        return finish

    pipeline(shards // 2, output_block, attended_block, give_pair(AIM))

    arrive(AIM, 1.0)

    def aim_block(block, buffer):
        at = pl.multiple_of(block * 512, 512)
        buffer[0:512, :] = dot(perm[pl.ds(at, 512), :], cat[...])

    gain_sum[...] = jnp.zeros((DIM, DIM), F32)

    def upstream_block(block, buffer):
        at = pl.multiple_of(block * 512, 512)
        placed = buffer[0:512, :]
        aim = placed[:, :DIM] + placed[:, DIM:]
        total = jnp.zeros((DIM, DIM), F32)
        for quarter in range(4):
            slot = block * 4 + quarter
            begin = pl.multiple_of(at + quarter * DIM, DIM)
            out = head_out[:, pl.ds(begin, DIM)]
            gap = gain * out - aim[quarter * DIM : (quarter + 1) * DIM, :].T
            loss_rows[slot] = jnp.broadcast_to(jnp.sum(gap * gap, axis=0, keepdims=True), (8, DIM))
            up_a = gap * meta_all[shard_at(slot), WEIGHT : WEIGHT + 1, :]
            total = total + up_a * out
            up = gain * up_a * inv_sum[0:1, pl.ds(begin, DIM)]
            delta[:, pl.ds(begin, DIM)] = jnp.broadcast_to(jnp.sum(up * out, axis=0, keepdims=True), (8, DIM))
            hi, lo = split(up.T)
            u3[pl.ds(begin, DIM), 0:DIM] = hi
            u3[pl.ds(begin, DIM), DIM : 2 * DIM] = hi
            u3[pl.ds(begin, DIM), 2 * DIM : 3 * DIM] = lo
        gain_sum[...] += total

    pipeline(length // 512, aim_block, upstream_block)

    gain_grad = jnp.sum(gain_sum[...].T, axis=0, keepdims=True)
    row_index = lax.broadcasted_iota(jnp.int32, (8, DIM), 0)
    for slot in range(shards):
        tile1[slot] = jnp.where(row_index == 0, loss_rows[slot], jnp.broadcast_to(gain_grad, (8, DIM)))
    stage1[me] = tile1[0]
    for slot, peer in enumerate(peers):
        pltpu.make_async_remote_copy(
            tile1.at[slot + 1, pl.ds(0, 2)], stage1.at[me, pl.ds(0, 2)], small_send.at[1], small_recv.at[1],
            device_id={"seq": peer}, device_id_type=MESH,
        ).start()

    def value_grad_block(turn, carry):
        block = turn
        at = pl.multiple_of(block * 512, 512)
        got[SLOT[VALUE], pl.ds(at, 512), :] = by_rows(at, u3.at[:, DIM : 3 * DIM])
        for quarter in range(4):
            give(VALUE, block * 4 + quarter)
        return carry

    lax.fori_loop(0, shards // 4, value_grad_block, 0)

    def exchange_losses():
        wait_small(small_recv.at[1], stage1, shards - 1)
        loss = jnp.zeros((1, DIM), F32)
        for shard in range(shards):
            loss = loss + stage1[shard, 0:1, :]
        excess = jnp.maximum(0.5 * loss / WIDTH - meta[REF : REF + 1, :], 0.0)
        hit = lax.broadcasted_iota(jnp.int32, (DIM, DIM), 0).astype(F32) == meta[BUCKET : BUCKET + 1, :]
        sums = lax.dot_general(
            jnp.where(row_index == 0, jnp.broadcast_to(excess, (8, DIM)), 1.0), jnp.where(hit, 1.0, 0.0),
            (((1,), (1,)), ((), ())), precision=HIGHEST, preferred_element_type=F32,
        )
        for shard in range(shards):
            tile2[shard : shard + 1, :] = stage1[shard, 1:2, :]
        tile2[shards : shards + 2, :] = sums[0:2, :]
        tile2[shards + 2 : shards + 4, :] = meta[EMB : EMB + 2, :]
        stage2[sample] = tile2[...]
        for turn in range(1, copies):
            other = lax.rem(sample + turn, copies)
            pltpu.make_async_remote_copy(
                tile2.at[pl.ds(0, shards + 4)], stage2.at[sample, pl.ds(0, shards + 4)], small_send.at[2], small_recv.at[2],
                device_id={"dp": other}, device_id_type=MESH,
            ).start()

    hi_a, lo_a, hi_b, lo_b = (perm.at[:, at : at + 256] for at in range(0, 1024, 256))

    def prob_grad_block(turn, buffer):
        at = pl.multiple_of(turn * 256, 256)
        buffer[...] = dot_nt(v3[...], u3[pl.ds(at, 256), :])

    def score_grad_block(turn, buffer, high, low):
        at = pl.multiple_of(turn * 256, 256)
        shift = delta[0:1, pl.ds(at, 256)]
        for row in range(0, length, CHUNK):
            here = (slice(row, row + CHUNK), pl.ds(at, 256))
            weights = e_hi[here].astype(F32) + e_lo[here].astype(F32)
            hi, lo = split((buffer[row : row + CHUNK, :] - shift) * weights)
            high[row : row + CHUNK, :] = hi
            low[row : row + CHUNK, :] = lo
            e_hi[here] = hi
            e_lo[here] = lo

    def query_grad_block(turn, high, low):
        at = pl.multiple_of(turn * 256, 256)
        grad = by_columns(kt, high[...], low[...]) * SCALE
        for half in range(2):
            begin = pl.multiple_of(at + half * DIM, DIM)
            got[SLOT[QUERY], pl.ds(begin, DIM), :] = grad[:, half * DIM : (half + 1) * DIM].T

    give_queries = give_pair(QUERY)
    prob_grad_block(0, score_a)
    prob_grad_block(1, score_b)
    score_grad_block(0, score_a, hi_a, lo_a)

    def gradient_pair(pair, carry):
        turn = 2 * pair + 1
        prob_grad_block(turn + 1, score_a)
        score_grad_block(turn, score_b, hi_b, lo_b)
        query_grad_block(turn - 1, hi_a, lo_a)
        prob_grad_block(turn + 2, score_b)
        score_grad_block(turn + 1, score_a, hi_a, lo_a)
        query_grad_block(turn, hi_b, lo_b)
        give_queries(turn - 1)
        give_queries(turn)
        pl.when(pair == 1)(exchange_losses)
        return carry

    last = shards // 2 - 1
    lax.fori_loop(0, last // 2, gradient_pair, 0)
    score_grad_block(last, score_b, hi_b, lo_b)
    query_grad_block(last - 1, hi_a, lo_a)
    query_grad_block(last, hi_b, lo_b)
    give_queries(last - 1)
    give_queries(last)

    def exchange_sums():
        if copies > 1:
            wait_small(small_recv.at[2], stage2, copies - 1, shards + 4)
        sums = jnp.zeros((2, DIM), F32)
        for other in range(copies):
            sums = sums + stage2[other, shards : shards + 2, :]
        tile3[0:2, :] = sums
        stage3[me, 0:2, :] = sums
        for peer in peers:
            pltpu.make_async_remote_copy(
                tile3.at[pl.ds(0, 2)], stage3.at[me, pl.ds(0, 2)], small_send.at[3], small_recv.at[3],
                device_id={"seq": peer}, device_id_type=MESH,
            ).start()

    def key_grad_block(turn, carry):
        block = turn
        at = pl.multiple_of(block * 512, 512)
        got[SLOT[KEY], pl.ds(at, 512), :] = by_rows(at, q3.at[:, DIM : 3 * DIM]) * (1.0 / LOG2E)
        for quarter in range(4):
            give(KEY, block * 4 + quarter)
        pl.when(turn == 1)(exchange_sums)
        return carry

    lax.fori_loop(0, shards // 4, key_grad_block, 0)

    by_sample = jnp.concatenate(
        [
            jnp.concatenate([stage2[other, row : row + 1, :] for row in (shards + 2, shards + 3)], axis=1)
            for other in range(copies)
        ],
        axis=0,
    )
    by_frequency = by_sample.T
    for head in range(shards):
        gains = jnp.concatenate([stage2[other, head : head + 1, :] for other in range(copies)], axis=0)
        weight_out[:, head * DIM : (head + 1) * DIM] = lax.dot_general(
            by_frequency, gains, (((1,), (0,)), ((), ())), precision=HIGHEST, preferred_element_type=F32
        )
    wait_small(small_recv.at[3], stage3, shards - 1)
    sums = jnp.zeros((2, DIM), F32)
    for shard in range(shards):
        sums = sums + stage3[shard, 0:2, :]
    mean = sums[0:1, :] / jnp.maximum(sums[1:2, :], 1.0)
    updated = meta[MIX : MIX + 1, :] * (1.0 + RATE * mean)
    updated = jnp.where(lane < BUCKETS, updated, 0.0)
    mixture = BUCKETS * updated / jnp.sum(updated, axis=1, keepdims=True)
    mix_out[...] = mixture[:, :BUCKETS]

    others = (shards - 1) * DIM
    for part in (KEY, QUERY, VALUE, AIM):
        if part in (VALUE, AIM):
            wait_sent(part)
        sent = got.at[SLOT[part], pl.ds(0, others), :]
        pltpu.make_async_copy(sent, sent, back_send.at[part]).wait()
        base = att_out if part == AIM else grad_out
        landed = base.at[:, PART_COLUMN[part] : PART_COLUMN[part] + WIDTH]
        pltpu.make_async_copy(landed, landed, back_recv.at[part]).wait()
    wait_small(small_send.at[0], meta_all, shards - 1)
    wait_small(small_send.at[1], stage1, shards - 1)
    if copies > 1:
        wait_small(small_send.at[2], stage2, copies - 1, shards + 4)
    wait_small(small_send.at[3], stage3, shards - 1)


def move_out(*refs):
    count = len(refs) // 2
    sources, outputs, sems = refs[:count], refs[count : 2 * count], refs[-1]
    moves = []
    for source, output in zip(sources, outputs):
        pieces = 4 if source.shape[0] >= DIM else 1
        rows = source.shape[0] // pieces
        for piece in range(pieces):
            part = pl.ds(piece * rows, rows)
            moves.append(pltpu.make_async_copy(source.at[part], output.at[part], sems.at[len(moves)]))
    for move in moves:
        move.start()
    for move in moves:
        move.wait()


def body(reader_rows, reader_targets, dest_pos, bucket_ids, ref_loss, timesteps, mod_weight, mixture_old):
    shards, copies = lax.axis_size("seq"), lax.axis_size("dp")
    length = shards * DIM
    half = FREQ_DIM // 2
    frequency = np.exp(-math.log(10000.0) * np.arange(half) / half).astype(np.float32)[None, :]
    any_spec = pl.BlockSpec(memory_space=pl.ANY)
    vmem_spec = pl.BlockSpec(memory_space=pltpu.VMEM)
    dma = pltpu.SemaphoreType.DMA
    attended, grads, weight_grad, mixture = pl.pallas_call(
        functools.partial(kernel, shards, copies),
        out_shape=(
            pltpu.VMEM((DIM, WIDTH), F32),
            pltpu.VMEM((DIM, 3 * WIDTH), F32),
            pltpu.VMEM((FREQ_DIM, WIDTH), F32),
            pltpu.VMEM((1, BUCKETS), F32),
        ),
        in_specs=[any_spec] * 9,
        out_specs=(vmem_spec, vmem_spec, vmem_spec, vmem_spec),
        scratch_shapes=[
            pltpu.VMEM((1, DIM), jnp.int32),
            pltpu.VMEM((1, DIM), jnp.int32),
            pltpu.VMEM((1, DIM), F32),
            pltpu.VMEM((1, DIM), F32),
            pltpu.SMEM((1,), jnp.int32),
            pltpu.SMEM((BUCKETS,), F32),
            pltpu.VMEM((8, DIM), F32),
            pltpu.VMEM((shards, 8, DIM), F32),
            pltpu.VMEM((4, length, DIM), F32),
            pltpu.VMEM((FREQ_DIM, DIM), F32),
            pltpu.VMEM((length, length), BF16),
            pltpu.VMEM((length, 2 * DIM), BF16),
            pltpu.VMEM((length, 3 * DIM), BF16),
            pltpu.VMEM((2 * DIM, length), BF16),
            pltpu.VMEM((length, 3 * DIM), BF16),
            pltpu.VMEM((length, 3 * DIM), BF16),
            pltpu.VMEM((2 * DIM, length), BF16),
            pltpu.VMEM((length, 3 * DIM), BF16),
            pltpu.VMEM((length, length), BF16),
            pltpu.VMEM((length, length), BF16),
            pltpu.VMEM((DIM, length), F32),
            pltpu.VMEM((8, length), F32),
            pltpu.VMEM((8, length), F32),
            pltpu.VMEM((DIM, DIM), F32),
            pltpu.VMEM((length, 256), F32),
            pltpu.VMEM((length, 256), F32),
            pltpu.VMEM((shards, 8, DIM), F32),
            pltpu.VMEM((shards, 8, DIM), F32),
            pltpu.VMEM((shards, 8, DIM), F32),
            pltpu.VMEM((copies, shards + 8, DIM), F32),
            pltpu.VMEM((shards + 8, DIM), F32),
            pltpu.VMEM((shards, 8, DIM), F32),
            pltpu.VMEM((8, DIM), F32),
            dma((4,)), dma((4,)), dma((4,)), dma((4,)), dma((4,)), dma((4,)), dma, dma((6,)),
        ],
        compiler_params=pltpu.CompilerParams(
            collective_id=0, has_side_effects=True, vmem_limit_bytes=56 * 1024 * 1024
        ),
        name="attend",
    )(reader_rows[0], reader_targets[0], dest_pos, bucket_ids, ref_loss, timesteps, mixture_old, frequency, mod_weight)
    results = (attended, grads, weight_grad, mixture)
    attended, grads, weight_grad, mixture = pl.pallas_call(
        move_out,
        out_shape=tuple(jax.ShapeDtypeStruct(item.shape, F32) for item in results),
        in_specs=[vmem_spec] * 4,
        out_specs=(any_spec,) * 4,
        scratch_shapes=[dma((13,))],
        compiler_params=pltpu.CompilerParams(vmem_limit_bytes=1024 * 1024),
        name="move_out",
    )(*(pltpu.with_memory_space_constraint(item, pltpu.VMEM) for item in results))
    return attended[None], grads[None], weight_grad, mixture[0]


def solution(mesh):
    return jax.shard_map(
        body,
        mesh=mesh,
        in_specs=(
            P("dp", "seq", None), P("dp", "seq", None), P("dp", "seq"), P("dp", "seq"),
            P("dp", "seq"), P("dp"), P(), P(),
        ),
        out_specs=(P("dp", "seq", None), P("dp", "seq", None), P(), P()),
        check_vma=False,
    )
```

```python
import functools
import math

import jax
import jax.numpy as jnp
import numpy as np
from jax import lax
from jax.experimental import pallas as pl
from jax.experimental.pallas import tpu as pltpu
from jax.sharding import PartitionSpec as P

HEADS = 16
DIM = 128
FREQ_DIM = 256
BUCKETS = 16
WIDTH = HEADS * DIM
RATE = 10.0
CHUNK = 64
LOG2E = 1.4426950408889634
SCALE = DIM ** (-0.5)
MESH = pl.DeviceIdType.MESH
HIGHEST = lax.Precision.HIGHEST
BF16 = jnp.bfloat16
F32 = jnp.float32

FAR_FIRST = (2, 5, 14, 15, 6, 1, 3, 9, 11, 8, 10, 4, 13, 12, 7, 0)
POS, WEIGHT, BUCKET, REF, EMB, MIX = 0, 1, 2, 3, 4, 6
KEY, QUERY, VALUE, AIM = 0, 1, 2, 3
SLOT = {AIM: KEY, VALUE: QUERY, QUERY: VALUE, KEY: AIM}
PART_COLUMN = {KEY: WIDTH, QUERY: 0, VALUE: 2 * WIDTH, AIM: 0}


def split(x):
    hi = x.astype(BF16)
    return hi, (x - hi.astype(F32)).astype(BF16)


def dot(a, b):
    return lax.dot_general(a, b, (((1,), (0,)), ((), ())), preferred_element_type=F32)


def dot_nt(a, b):
    return lax.dot_general(a, b, (((1,), (1,)), ((), ())), preferred_element_type=F32)


def kernel(
    shards, copies, rows, aims, places_in, buckets_in, ref_in, steps_in, old_in, frequency_in, mod_w,
    att_out, grad_out, weight_out, mix_out,
    places, buckets, ref_row, frequency, steps, old, meta, meta_all, got, mod_buf, perm, cat, k3, kt, q3, v3, vt, u3, e_hi, e_lo, head_out, inv_sum, delta,
    gain_sum, score_a, score_b, loss_rows, stage1, tile1, stage2, tile2, stage3, tile3,
    send_sem, recv_sem, back_send, back_recv, small_send, small_recv, mod_sem, operand_sem,
):
    length = shards * DIM
    me = lax.axis_index("seq")
    sample = lax.axis_index("dp")
    my_z, my_y = me // 4, lax.rem(me, 4)

    side = 1 - 2 * lax.rem(sample, 2)

    def shard_at(slot):
        along, shift = lax.rem(slot, 4), slot // 4
        return lax.rem(my_z + 4 + side * along, 4) * 4 + lax.rem(my_y + 8 + side * (along + shift), 4)

    peers = [shard_at(slot) for slot in range(1, shards)]

    barrier = pltpu.get_barrier_semaphore()
    for peer in peers:
        pl.semaphore_signal(barrier, inc=1, device_id={"seq": peer}, device_id_type=MESH)
    for turn in range(1, copies):
        other = lax.rem(sample + turn, copies)
        pl.semaphore_signal(barrier, inc=1, device_id={"dp": other}, device_id_type=MESH)

    operands = [
        pltpu.make_async_copy(source, into, operand_sem.at[index])
        for index, (source, into) in enumerate(
            (
                (places_in, places), (buckets_in, buckets), (ref_in, ref_row), (frequency_in, frequency),
                (steps_in, steps), (old_in, old),
            )
        )
    ]
    for operand in operands:
        operand.start()
    mod_copy = pltpu.make_async_copy(
        mod_w.at[:, pl.ds(pl.multiple_of(me * DIM, DIM), DIM)], mod_buf, mod_sem
    )
    mod_copy.start()
    pl.semaphore_wait(barrier, shards - 1 + copies - 1)

    def source(part, head):
        base = aims if part == AIM else rows
        return base.at[:, pl.ds(pl.multiple_of(PART_COLUMN[part] + head * DIM, DIM), DIM)]

    def landing(part):
        return got.at[part, pl.ds(pl.multiple_of(me * DIM, DIM), DIM), :]

    def send(part):
        pltpu.make_async_copy(source(part, me), landing(part), recv_sem.at[part]).start()
        for peer in peers:
            pltpu.make_async_remote_copy(
                source(part, peer), landing(part), send_sem.at[part], recv_sem.at[part],
                device_id={"seq": peer}, device_id_type=MESH,
            ).start()

    def wait_sent(part):
        sent = got.at[part, pl.ds(0, (shards - 1) * DIM), :]
        pltpu.make_async_copy(sent, sent, send_sem.at[part]).wait()

    send(KEY)

    for operand in operands:
        operand.wait()
    meta[POS : POS + 1, :] = places[...].astype(F32)
    bucket_row = buckets[...]
    lane = lax.broadcasted_iota(jnp.int32, (1, DIM), 1)
    weight_row = jnp.zeros((1, DIM), F32)
    old_row = jnp.zeros((1, DIM), F32)
    for bucket in range(BUCKETS):
        weight_row = weight_row + jnp.where(bucket_row == bucket, old[bucket], 0.0)
        old_row = old_row + jnp.where(lane == bucket, old[bucket], 0.0)
    meta[WEIGHT : WEIGHT + 1, :] = weight_row
    meta[BUCKET : BUCKET + 1, :] = bucket_row.astype(F32)
    meta[REF : REF + 1, :] = ref_row[...]
    angles = steps[0].astype(F32) * frequency[...]
    for row, wave in ((EMB, jnp.cos(angles)), (EMB + 1, jnp.sin(angles))):
        meta[row : row + 1, :] = wave / (1.0 + jnp.exp(-wave))
    meta[MIX : MIX + 1, :] = old_row
    meta[MIX + 1 : MIX + 2, :] = jnp.zeros((1, DIM), F32)
    meta_all[me] = meta[...]
    for peer in peers:
        pltpu.make_async_remote_copy(
            meta.at[pl.ds(0, 2)], meta_all.at[me, pl.ds(0, 2)], small_send.at[0], small_recv.at[0],
            device_id={"seq": peer}, device_id_type=MESH,
        ).start()
    send(QUERY)

    def wait_small(sem, buffer, count, depth=2):
        taken = buffer.at[pl.ds(0, count), pl.ds(0, depth)]
        pltpu.make_async_copy(taken, taken, sem).wait()

    mod_copy.wait()
    embedding = jnp.concatenate([meta[EMB : EMB + 1, :], meta[EMB + 1 : EMB + 2, :]], axis=1)
    embedding = jnp.broadcast_to(embedding, (8, FREQ_DIM))
    gain_row = 1.0 + lax.dot_general(
        embedding, mod_buf[...], (((1,), (0,)), ((), ())), precision=HIGHEST, preferred_element_type=F32
    )
    gain = jnp.broadcast_to(gain_row[0:1, :], (DIM, DIM)).T

    wait_small(small_recv.at[0], meta_all, shards - 1)

    def perm_block(block, carry):
        at = pl.multiple_of(block * 256, 256)
        inside = lax.broadcasted_iota(jnp.int32, (DIM, DIM), 0)
        place = jnp.concatenate([inside + shard_at(2 * block + half) * DIM for half in range(2)], axis=0).astype(F32)
        for shard in range(shards):
            hit = place == meta_all[shard, POS : POS + 1, :]
            perm[pl.ds(at, 256), shard * DIM : (shard + 1) * DIM] = jnp.where(hit, 1.0, 0.0).astype(BF16)
        return carry

    lax.fori_loop(0, length // 256, perm_block, 0)

    def pipeline(count, make, use, finish=None):
        def both(at, last):
            make(at + 1, score_b)
            use(at, score_a)
            if not last:
                make(at + 2, score_a)
            use(at + 1, score_b)
            if finish is not None:
                finish(at)
                finish(at + 1)

        def one(pair, carry):
            both(2 * pair, False)
            return carry

        make(0, score_a)
        lax.fori_loop(0, count // 2 - 1, one, 0)
        both(count - 2, True)

    def arrive(part, factor):
        pltpu.make_async_copy(got.at[part], got.at[part], recv_sem.at[part]).wait()

        def one(block, carry):
            at = pl.multiple_of(block * 256, 256)
            hi, lo = split(got[part, pl.ds(at, 256), :] * factor)
            cat[pl.ds(at, 256), 0:DIM] = hi
            cat[pl.ds(at, 256), DIM : 2 * DIM] = lo
            return carry

        lax.fori_loop(0, length // 256, one, 0)

    def reorder(part, factor, into, transposed):
        arrive(part, factor)

        def make(block, buffer):
            at = pl.multiple_of(block * 512, 512)
            buffer[0:512, :] = dot(perm[pl.ds(at, 512), :], cat[...])

        def use(block, buffer):
            at = pl.multiple_of(block * 512, 512)
            placed = buffer[0:512, :]
            hi, lo = placed[:, :DIM].astype(BF16), placed[:, DIM:].astype(BF16)
            into[pl.ds(at, 512), 0:DIM] = hi
            into[pl.ds(at, 512), DIM : 2 * DIM] = hi if part == QUERY else lo
            into[pl.ds(at, 512), 2 * DIM : 3 * DIM] = lo if part == QUERY else hi
            if transposed is not None:
                hi, lo = split((placed[:, :DIM] + placed[:, DIM:]).T)
                transposed[0:DIM, pl.ds(at, 512)] = hi
                transposed[DIM : 2 * DIM, pl.ds(at, 512)] = lo

        pipeline(length // 512, make, use)

    def by_columns(left, high, low):
        full = dot(left[...], high)
        return full[:DIM] + full[DIM:] + dot(left[0:DIM, :], low)

    def by_rows(at, right):
        full = dot(e_hi[pl.ds(at, 512), :], right[...])
        return full[:, :DIM] + full[:, DIM:] + dot(e_lo[pl.ds(at, 512), :], right[:, 0:DIM])

    wait_sent(KEY)
    send(VALUE)
    reorder(KEY, 1.0, k3, kt)
    wait_sent(QUERY)
    send(AIM)
    reorder(QUERY, SCALE * LOG2E, q3, None)

    def score_block(block, buffer):
        at = pl.multiple_of(block * 256, 256)
        buffer[...] = dot_nt(k3[...], q3[pl.ds(at, 256), :])

    def softmax_block(block, buffer):
        at = pl.multiple_of(block * 256, 256)
        top = jnp.full((8, 256), -jnp.inf, F32)
        for row in range(0, length, CHUNK):
            top = jnp.maximum(top, jnp.max(buffer[row : row + CHUNK, :].reshape(CHUNK // 8, 8, 256), axis=0))
        top = jnp.max(top, axis=0, keepdims=True)
        sums = jnp.zeros((8, 256), F32)
        for row in range(0, length, CHUNK):
            weights = jnp.exp2(buffer[row : row + CHUNK, :] - top)
            sums = sums + jnp.sum(weights.reshape(CHUNK // 8, 8, 256), axis=0)
            hi, lo = split(weights)
            e_hi[row : row + CHUNK, pl.ds(at, 256)] = hi
            e_lo[row : row + CHUNK, pl.ds(at, 256)] = lo
        inv_sum[:, pl.ds(at, 256)] = jnp.broadcast_to(1.0 / jnp.sum(sums, axis=0, keepdims=True), (8, 256))

    pipeline(length // 256, score_block, softmax_block)

    def target(part):
        base = att_out if part == AIM else grad_out
        return base.at[:, pl.ds(pl.multiple_of(PART_COLUMN[part] + me * DIM, DIM), DIM)]

    def give(part, slot):
        block = got.at[SLOT[part], pl.ds(pl.multiple_of(slot * DIM, DIM), DIM), :]
        shard = shard_at(slot)

        @pl.when(shard != me)
        def _():
            pltpu.make_async_remote_copy(
                block, target(part), back_send.at[part], back_recv.at[part],
                device_id={"seq": shard}, device_id_type=MESH,
            ).start()

        @pl.when(shard == me)
        def _():
            pltpu.make_async_copy(block, target(part), back_recv.at[part]).start()

    reorder(VALUE, 1.0, v3, vt)

    def output_block(turn, buffer):
        at = pl.multiple_of(turn * 256, 256)
        buffer[0:DIM, :] = by_columns(vt, e_hi[:, pl.ds(at, 256)], e_lo[:, pl.ds(at, 256)])

    def attended_block(turn, buffer):
        at = pl.multiple_of(turn * 256, 256)
        out = buffer[0:DIM, :] * inv_sum[0:1, pl.ds(at, 256)]
        head_out[:, pl.ds(at, 256)] = out
        for half in range(2):
            begin = pl.multiple_of(at + half * DIM, DIM)
            got[SLOT[AIM], pl.ds(begin, DIM), :] = (gain * out[:, half * DIM : (half + 1) * DIM]).T

    def give_pair(part):
        def finish(turn):
            for half in range(2):
                give(part, turn * 2 + half)

        return finish

    pipeline(shards // 2, output_block, attended_block, give_pair(AIM))

    arrive(AIM, 1.0)

    def aim_block(block, buffer):
        at = pl.multiple_of(block * 512, 512)
        buffer[0:512, :] = dot(perm[pl.ds(at, 512), :], cat[...])

    gain_sum[...] = jnp.zeros((DIM, DIM), F32)

    def upstream_block(block, buffer):
        at = pl.multiple_of(block * 512, 512)
        placed = buffer[0:512, :]
        aim = placed[:, :DIM] + placed[:, DIM:]
        total = jnp.zeros((DIM, DIM), F32)
        for quarter in range(4):
            slot = block * 4 + quarter
            begin = pl.multiple_of(at + quarter * DIM, DIM)
            out = head_out[:, pl.ds(begin, DIM)]
            gap = gain * out - aim[quarter * DIM : (quarter + 1) * DIM, :].T
            loss_rows[slot] = jnp.broadcast_to(jnp.sum(gap * gap, axis=0, keepdims=True), (8, DIM))
            up_a = gap * meta_all[shard_at(slot), WEIGHT : WEIGHT + 1, :]
            total = total + up_a * out
            up = gain * up_a * inv_sum[0:1, pl.ds(begin, DIM)]
            delta[:, pl.ds(begin, DIM)] = jnp.broadcast_to(jnp.sum(up * out, axis=0, keepdims=True), (8, DIM))
            hi, lo = split(up.T)
            u3[pl.ds(begin, DIM), 0:DIM] = hi
            u3[pl.ds(begin, DIM), DIM : 2 * DIM] = hi
            u3[pl.ds(begin, DIM), 2 * DIM : 3 * DIM] = lo
        gain_sum[...] += total

    pipeline(length // 512, aim_block, upstream_block)

    gain_grad = jnp.sum(gain_sum[...].T, axis=0, keepdims=True)
    row_index = lax.broadcasted_iota(jnp.int32, (8, DIM), 0)
    for slot in range(shards):
        tile1[slot] = jnp.where(row_index == 0, loss_rows[slot], jnp.broadcast_to(gain_grad, (8, DIM)))
    stage1[me] = tile1[0]
    for slot, peer in enumerate(peers):
        pltpu.make_async_remote_copy(
            tile1.at[slot + 1, pl.ds(0, 2)], stage1.at[me, pl.ds(0, 2)], small_send.at[1], small_recv.at[1],
            device_id={"seq": peer}, device_id_type=MESH,
        ).start()

    def value_grad_block(turn, carry):
        block = turn
        at = pl.multiple_of(block * 512, 512)
        got[SLOT[VALUE], pl.ds(at, 512), :] = by_rows(at, u3.at[:, DIM : 3 * DIM])
        for quarter in range(4):
            give(VALUE, block * 4 + quarter)
        return carry

    lax.fori_loop(0, shards // 4, value_grad_block, 0)

    def exchange_losses():
        wait_small(small_recv.at[1], stage1, shards - 1)
        loss = jnp.zeros((1, DIM), F32)
        for shard in range(shards):
            loss = loss + stage1[shard, 0:1, :]
        excess = jnp.maximum(0.5 * loss / WIDTH - meta[REF : REF + 1, :], 0.0)
        hit = lax.broadcasted_iota(jnp.int32, (DIM, DIM), 0).astype(F32) == meta[BUCKET : BUCKET + 1, :]
        sums = lax.dot_general(
            jnp.where(row_index == 0, jnp.broadcast_to(excess, (8, DIM)), 1.0), jnp.where(hit, 1.0, 0.0),
            (((1,), (1,)), ((), ())), precision=HIGHEST, preferred_element_type=F32,
        )
        for shard in range(shards):
            tile2[shard : shard + 1, :] = stage1[shard, 1:2, :]
        tile2[shards : shards + 2, :] = sums[0:2, :]
        tile2[shards + 2 : shards + 4, :] = meta[EMB : EMB + 2, :]
        stage2[sample] = tile2[...]
        for turn in range(1, copies):
            other = lax.rem(sample + turn, copies)
            pltpu.make_async_remote_copy(
                tile2.at[pl.ds(0, shards + 4)], stage2.at[sample, pl.ds(0, shards + 4)], small_send.at[2], small_recv.at[2],
                device_id={"dp": other}, device_id_type=MESH,
            ).start()

    hi_a, lo_a, hi_b, lo_b = (perm.at[:, at : at + 256] for at in range(0, 1024, 256))

    def prob_grad_block(turn, buffer):
        at = pl.multiple_of(turn * 256, 256)
        buffer[...] = dot_nt(v3[...], u3[pl.ds(at, 256), :])

    def score_grad_block(turn, buffer, high, low):
        at = pl.multiple_of(turn * 256, 256)
        shift = delta[0:1, pl.ds(at, 256)]
        for row in range(0, length, CHUNK):
            here = (slice(row, row + CHUNK), pl.ds(at, 256))
            weights = e_hi[here].astype(F32) + e_lo[here].astype(F32)
            hi, lo = split((buffer[row : row + CHUNK, :] - shift) * weights)
            high[row : row + CHUNK, :] = hi
            low[row : row + CHUNK, :] = lo
            e_hi[here] = hi
            e_lo[here] = lo

    def query_grad_block(turn, high, low):
        at = pl.multiple_of(turn * 256, 256)
        grad = by_columns(kt, high[...], low[...]) * SCALE
        for half in range(2):
            begin = pl.multiple_of(at + half * DIM, DIM)
            got[SLOT[QUERY], pl.ds(begin, DIM), :] = grad[:, half * DIM : (half + 1) * DIM].T

    give_queries = give_pair(QUERY)
    prob_grad_block(0, score_a)
    prob_grad_block(1, score_b)
    score_grad_block(0, score_a, hi_a, lo_a)

    def gradient_pair(pair, carry):
        turn = 2 * pair + 1
        prob_grad_block(turn + 1, score_a)
        score_grad_block(turn, score_b, hi_b, lo_b)
        query_grad_block(turn - 1, hi_a, lo_a)
        prob_grad_block(turn + 2, score_b)
        score_grad_block(turn + 1, score_a, hi_a, lo_a)
        query_grad_block(turn, hi_b, lo_b)
        give_queries(turn - 1)
        give_queries(turn)
        pl.when(pair == 1)(exchange_losses)
        return carry

    last = shards // 2 - 1
    lax.fori_loop(0, last // 2, gradient_pair, 0)
    score_grad_block(last, score_b, hi_b, lo_b)
    query_grad_block(last - 1, hi_a, lo_a)
    query_grad_block(last, hi_b, lo_b)
    give_queries(last - 1)
    give_queries(last)

    def exchange_sums():
        if copies > 1:
            wait_small(small_recv.at[2], stage2, copies - 1, shards + 4)
        sums = jnp.zeros((2, DIM), F32)
        for other in range(copies):
            sums = sums + stage2[other, shards : shards + 2, :]
        tile3[0:2, :] = sums
        stage3[me, 0:2, :] = sums
        for peer in peers:
            pltpu.make_async_remote_copy(
                tile3.at[pl.ds(0, 2)], stage3.at[me, pl.ds(0, 2)], small_send.at[3], small_recv.at[3],
                device_id={"seq": peer}, device_id_type=MESH,
            ).start()

    def key_grad_block(turn, carry):
        block = turn
        at = pl.multiple_of(block * 512, 512)
        got[SLOT[KEY], pl.ds(at, 512), :] = by_rows(at, q3.at[:, DIM : 3 * DIM]) * (1.0 / LOG2E)
        pl.when(turn == 1)(exchange_sums)
        return carry

    lax.fori_loop(0, shards // 4, key_grad_block, 0)
    for slot in FAR_FIRST:
        give(KEY, slot)

    by_sample = jnp.concatenate(
        [
            jnp.concatenate([stage2[other, row : row + 1, :] for row in (shards + 2, shards + 3)], axis=1)
            for other in range(copies)
        ],
        axis=0,
    )
    by_frequency = by_sample.T
    for head in range(shards):
        gains = jnp.concatenate([stage2[other, head : head + 1, :] for other in range(copies)], axis=0)
        weight_out[:, head * DIM : (head + 1) * DIM] = lax.dot_general(
            by_frequency, gains, (((1,), (0,)), ((), ())), precision=HIGHEST, preferred_element_type=F32
        )
    wait_small(small_recv.at[3], stage3, shards - 1)
    sums = jnp.zeros((2, DIM), F32)
    for shard in range(shards):
        sums = sums + stage3[shard, 0:2, :]
    mean = sums[0:1, :] / jnp.maximum(sums[1:2, :], 1.0)
    updated = meta[MIX : MIX + 1, :] * (1.0 + RATE * mean)
    updated = jnp.where(lane < BUCKETS, updated, 0.0)
    mixture = BUCKETS * updated / jnp.sum(updated, axis=1, keepdims=True)
    mix_out[...] = mixture[:, :BUCKETS]

    others = (shards - 1) * DIM
    for part in (KEY, QUERY, VALUE, AIM):
        if part in (VALUE, AIM):
            wait_sent(part)
        sent = got.at[SLOT[part], pl.ds(0, others), :]
        pltpu.make_async_copy(sent, sent, back_send.at[part]).wait()
        base = att_out if part == AIM else grad_out
        landed = base.at[:, PART_COLUMN[part] : PART_COLUMN[part] + WIDTH]
        pltpu.make_async_copy(landed, landed, back_recv.at[part]).wait()
    wait_small(small_send.at[0], meta_all, shards - 1)
    wait_small(small_send.at[1], stage1, shards - 1)
    if copies > 1:
        wait_small(small_send.at[2], stage2, copies - 1, shards + 4)
    wait_small(small_send.at[3], stage3, shards - 1)


def move_out(*refs):
    count = len(refs) // 2
    sources, outputs, sems = refs[:count], refs[count : 2 * count], refs[-1]
    moves = []
    for source, output in zip(sources, outputs):
        pieces = 4 if source.shape[0] >= DIM else 1
        rows = source.shape[0] // pieces
        for piece in range(pieces):
            part = pl.ds(piece * rows, rows)
            moves.append(pltpu.make_async_copy(source.at[part], output.at[part], sems.at[len(moves)]))
    for move in moves:
        move.start()
    for move in moves:
        move.wait()


def body(reader_rows, reader_targets, dest_pos, bucket_ids, ref_loss, timesteps, mod_weight, mixture_old):
    shards, copies = lax.axis_size("seq"), lax.axis_size("dp")
    length = shards * DIM
    half = FREQ_DIM // 2
    frequency = np.exp(-math.log(10000.0) * np.arange(half) / half).astype(np.float32)[None, :]
    any_spec = pl.BlockSpec(memory_space=pl.ANY)
    vmem_spec = pl.BlockSpec(memory_space=pltpu.VMEM)
    dma = pltpu.SemaphoreType.DMA
    attended, grads, weight_grad, mixture = pl.pallas_call(
        functools.partial(kernel, shards, copies),
        out_shape=(
            pltpu.VMEM((DIM, WIDTH), F32),
            pltpu.VMEM((DIM, 3 * WIDTH), F32),
            pltpu.VMEM((FREQ_DIM, WIDTH), F32),
            pltpu.VMEM((1, BUCKETS), F32),
        ),
        in_specs=[any_spec] * 9,
        out_specs=(vmem_spec, vmem_spec, vmem_spec, vmem_spec),
        scratch_shapes=[
            pltpu.VMEM((1, DIM), jnp.int32),
            pltpu.VMEM((1, DIM), jnp.int32),
            pltpu.VMEM((1, DIM), F32),
            pltpu.VMEM((1, DIM), F32),
            pltpu.SMEM((1,), jnp.int32),
            pltpu.SMEM((BUCKETS,), F32),
            pltpu.VMEM((8, DIM), F32),
            pltpu.VMEM((shards, 8, DIM), F32),
            pltpu.VMEM((4, length, DIM), F32),
            pltpu.VMEM((FREQ_DIM, DIM), F32),
            pltpu.VMEM((length, length), BF16),
            pltpu.VMEM((length, 2 * DIM), BF16),
            pltpu.VMEM((length, 3 * DIM), BF16),
            pltpu.VMEM((2 * DIM, length), BF16),
            pltpu.VMEM((length, 3 * DIM), BF16),
            pltpu.VMEM((length, 3 * DIM), BF16),
            pltpu.VMEM((2 * DIM, length), BF16),
            pltpu.VMEM((length, 3 * DIM), BF16),
            pltpu.VMEM((length, length), BF16),
            pltpu.VMEM((length, length), BF16),
            pltpu.VMEM((DIM, length), F32),
            pltpu.VMEM((8, length), F32),
            pltpu.VMEM((8, length), F32),
            pltpu.VMEM((DIM, DIM), F32),
            pltpu.VMEM((length, 256), F32),
            pltpu.VMEM((length, 256), F32),
            pltpu.VMEM((shards, 8, DIM), F32),
            pltpu.VMEM((shards, 8, DIM), F32),
            pltpu.VMEM((shards, 8, DIM), F32),
            pltpu.VMEM((copies, shards + 8, DIM), F32),
            pltpu.VMEM((shards + 8, DIM), F32),
            pltpu.VMEM((shards, 8, DIM), F32),
            pltpu.VMEM((8, DIM), F32),
            dma((4,)), dma((4,)), dma((4,)), dma((4,)), dma((4,)), dma((4,)), dma, dma((6,)),
        ],
        compiler_params=pltpu.CompilerParams(
            collective_id=0, has_side_effects=True, vmem_limit_bytes=56 * 1024 * 1024
        ),
        name="attend",
    )(reader_rows[0], reader_targets[0], dest_pos, bucket_ids, ref_loss, timesteps, mixture_old, frequency, mod_weight)
    results = (attended, grads, weight_grad, mixture)
    attended, grads, weight_grad, mixture = pl.pallas_call(
        move_out,
        out_shape=tuple(jax.ShapeDtypeStruct(item.shape, F32) for item in results),
        in_specs=[vmem_spec] * 4,
        out_specs=(any_spec,) * 4,
        scratch_shapes=[dma((13,))],
        compiler_params=pltpu.CompilerParams(vmem_limit_bytes=1024 * 1024),
        name="move_out",
    )(*(pltpu.with_memory_space_constraint(item, pltpu.VMEM) for item in results))
    return attended[None], grads[None], weight_grad, mixture[0]


def solution(mesh):
    return jax.shard_map(
        body,
        mesh=mesh,
        in_specs=(
            P("dp", "seq", None), P("dp", "seq", None), P("dp", "seq"), P("dp", "seq"),
            P("dp", "seq"), P("dp"), P(), P(),
        ),
        out_specs=(P("dp", "seq", None), P("dp", "seq", None), P(), P()),
        check_vma=False,
    )
```

```python
import functools
import math

import jax
import jax.numpy as jnp
import numpy as np
from jax import lax
from jax.experimental import pallas as pl
from jax.experimental.pallas import tpu as pltpu
from jax.sharding import PartitionSpec as P

HEADS = 16
DIM = 128
FREQ_DIM = 256
BUCKETS = 16
WIDTH = HEADS * DIM
RATE = 10.0
CHUNK = 64
LOG2E = 1.4426950408889634
SCALE = DIM ** (-0.5)
MESH = pl.DeviceIdType.MESH
HIGHEST = lax.Precision.HIGHEST
BF16 = jnp.bfloat16
F32 = jnp.float32

POS, WEIGHT, BUCKET, REF, EMB, MIX = 0, 1, 2, 3, 4, 6
KEY, QUERY, VALUE, AIM = 0, 1, 2, 3
SLOT = {AIM: KEY, VALUE: QUERY, QUERY: VALUE, KEY: AIM}
PART_COLUMN = {KEY: WIDTH, QUERY: 0, VALUE: 2 * WIDTH, AIM: 0}


def split(x):
    hi = x.astype(BF16)
    return hi, (x - hi.astype(F32)).astype(BF16)


def dot(a, b):
    return lax.dot_general(a, b, (((1,), (0,)), ((), ())), preferred_element_type=F32)


def dot_nt(a, b):
    return lax.dot_general(a, b, (((1,), (1,)), ((), ())), preferred_element_type=F32)


def kernel(
    shards, copies, rows, aims, places_in, buckets_in, ref_in, steps_in, old_in, frequency_in, mod_w,
    att_out, grad_out, weight_out, mix_out,
    places, buckets, ref_row, frequency, steps, old, meta, meta_all, got, mod_buf, perm, cat, k3, kt, q3, v3, vt, u3, e_hi, e_lo, head_out, inv_sum, delta,
    gain_sum, score_a, score_b, loss_rows, stage1, tile1, stage2, tile2, stage3, tile3,
    send_sem, recv_sem, back_send, back_recv, small_send, small_recv, mod_sem, operand_sem,
):
    length = shards * DIM
    me = lax.axis_index("seq")
    sample = lax.axis_index("dp")
    my_z, my_y = me // 4, lax.rem(me, 4)

    side = 1 - 2 * lax.rem(sample, 2)

    def shard_at(slot):
        along, shift = lax.rem(slot, 4), slot // 4
        return lax.rem(my_z + 4 + side * along, 4) * 4 + lax.rem(my_y + 8 + side * (along + shift), 4)

    peers = [shard_at(slot) for slot in range(1, shards)]

    barrier = pltpu.get_barrier_semaphore()
    for peer in peers:
        pl.semaphore_signal(barrier, inc=1, device_id={"seq": peer}, device_id_type=MESH)
    for turn in range(1, copies):
        other = lax.rem(sample + turn, copies)
        pl.semaphore_signal(barrier, inc=1, device_id={"dp": other}, device_id_type=MESH)

    operands = [
        pltpu.make_async_copy(source, into, operand_sem.at[index])
        for index, (source, into) in enumerate(
            (
                (places_in, places), (buckets_in, buckets), (ref_in, ref_row), (frequency_in, frequency),
                (steps_in, steps), (old_in, old),
            )
        )
    ]
    for operand in operands:
        operand.start()
    mod_copy = pltpu.make_async_copy(
        mod_w.at[:, pl.ds(pl.multiple_of(me * DIM, DIM), DIM)], mod_buf, mod_sem
    )
    mod_copy.start()
    pl.semaphore_wait(barrier, shards - 1 + copies - 1)

    def source(part, head):
        base = aims if part == AIM else rows
        return base.at[:, pl.ds(pl.multiple_of(PART_COLUMN[part] + head * DIM, DIM), DIM)]

    def landing(part):
        return got.at[part, pl.ds(pl.multiple_of(me * DIM, DIM), DIM), :]

    def send(part):
        pltpu.make_async_copy(source(part, me), landing(part), recv_sem.at[part]).start()
        for half in range(2):
            rows_of = pl.ds(half * (DIM // 2), DIM // 2)
            for peer in peers:
                pltpu.make_async_remote_copy(
                    source(part, peer).at[rows_of], landing(part).at[rows_of], send_sem.at[part], recv_sem.at[part],
                    device_id={"seq": peer}, device_id_type=MESH,
                ).start()

    def wait_sent(part):
        sent = got.at[part, pl.ds(0, (shards - 1) * DIM), :]
        pltpu.make_async_copy(sent, sent, send_sem.at[part]).wait()

    send(KEY)

    for operand in operands:
        operand.wait()
    meta[POS : POS + 1, :] = places[...].astype(F32)
    bucket_row = buckets[...]
    lane = lax.broadcasted_iota(jnp.int32, (1, DIM), 1)
    weight_row = jnp.zeros((1, DIM), F32)
    old_row = jnp.zeros((1, DIM), F32)
    for bucket in range(BUCKETS):
        weight_row = weight_row + jnp.where(bucket_row == bucket, old[bucket], 0.0)
        old_row = old_row + jnp.where(lane == bucket, old[bucket], 0.0)
    meta[WEIGHT : WEIGHT + 1, :] = weight_row
    meta[BUCKET : BUCKET + 1, :] = bucket_row.astype(F32)
    meta[REF : REF + 1, :] = ref_row[...]
    angles = steps[0].astype(F32) * frequency[...]
    for row, wave in ((EMB, jnp.cos(angles)), (EMB + 1, jnp.sin(angles))):
        meta[row : row + 1, :] = wave / (1.0 + jnp.exp(-wave))
    meta[MIX : MIX + 1, :] = old_row
    meta[MIX + 1 : MIX + 2, :] = jnp.zeros((1, DIM), F32)
    meta_all[me] = meta[...]
    for peer in peers:
        pltpu.make_async_remote_copy(
            meta.at[pl.ds(0, 2)], meta_all.at[me, pl.ds(0, 2)], small_send.at[0], small_recv.at[0],
            device_id={"seq": peer}, device_id_type=MESH,
        ).start()
    send(QUERY)

    def wait_small(sem, buffer, count, depth=2):
        taken = buffer.at[pl.ds(0, count), pl.ds(0, depth)]
        pltpu.make_async_copy(taken, taken, sem).wait()

    mod_copy.wait()
    embedding = jnp.concatenate([meta[EMB : EMB + 1, :], meta[EMB + 1 : EMB + 2, :]], axis=1)
    embedding = jnp.broadcast_to(embedding, (8, FREQ_DIM))
    gain_row = 1.0 + lax.dot_general(
        embedding, mod_buf[...], (((1,), (0,)), ((), ())), precision=HIGHEST, preferred_element_type=F32
    )
    gain = jnp.broadcast_to(gain_row[0:1, :], (DIM, DIM)).T

    wait_small(small_recv.at[0], meta_all, shards - 1)

    def perm_block(block, carry):
        at = pl.multiple_of(block * 256, 256)
        inside = lax.broadcasted_iota(jnp.int32, (DIM, DIM), 0)
        place = jnp.concatenate([inside + shard_at(2 * block + half) * DIM for half in range(2)], axis=0).astype(F32)
        for shard in range(shards):
            hit = place == meta_all[shard, POS : POS + 1, :]
            perm[pl.ds(at, 256), shard * DIM : (shard + 1) * DIM] = jnp.where(hit, 1.0, 0.0).astype(BF16)
        return carry

    lax.fori_loop(0, length // 256, perm_block, 0)

    def pipeline(count, make, use, finish=None):
        def both(at, last):
            make(at + 1, score_b)
            use(at, score_a)
            if not last:
                make(at + 2, score_a)
            use(at + 1, score_b)
            if finish is not None:
                finish(at)
                finish(at + 1)

        def one(pair, carry):
            both(2 * pair, False)
            return carry

        make(0, score_a)
        lax.fori_loop(0, count // 2 - 1, one, 0)
        both(count - 2, True)

    def arrive(part, factor):
        pltpu.make_async_copy(got.at[part], got.at[part], recv_sem.at[part]).wait()

        def one(block, carry):
            at = pl.multiple_of(block * 256, 256)
            hi, lo = split(got[part, pl.ds(at, 256), :] * factor)
            cat[pl.ds(at, 256), 0:DIM] = hi
            cat[pl.ds(at, 256), DIM : 2 * DIM] = lo
            return carry

        lax.fori_loop(0, length // 256, one, 0)

    def reorder(part, factor, into, transposed):
        arrive(part, factor)

        def make(block, buffer):
            at = pl.multiple_of(block * 512, 512)
            buffer[0:512, :] = dot(perm[pl.ds(at, 512), :], cat[...])

        def use(block, buffer):
            at = pl.multiple_of(block * 512, 512)
            placed = buffer[0:512, :]
            hi, lo = placed[:, :DIM].astype(BF16), placed[:, DIM:].astype(BF16)
            into[pl.ds(at, 512), 0:DIM] = hi
            into[pl.ds(at, 512), DIM : 2 * DIM] = hi if part == QUERY else lo
            into[pl.ds(at, 512), 2 * DIM : 3 * DIM] = lo if part == QUERY else hi
            if transposed is not None:
                hi, lo = split((placed[:, :DIM] + placed[:, DIM:]).T)
                transposed[0:DIM, pl.ds(at, 512)] = hi
                transposed[DIM : 2 * DIM, pl.ds(at, 512)] = lo

        pipeline(length // 512, make, use)

    def by_columns(left, high, low):
        full = dot(left[...], high)
        return full[:DIM] + full[DIM:] + dot(left[0:DIM, :], low)

    def by_rows(at, right):
        full = dot(e_hi[pl.ds(at, 512), :], right[...])
        return full[:, :DIM] + full[:, DIM:] + dot(e_lo[pl.ds(at, 512), :], right[:, 0:DIM])

    wait_sent(KEY)
    send(VALUE)
    reorder(KEY, 1.0, k3, kt)
    wait_sent(QUERY)
    send(AIM)
    reorder(QUERY, SCALE * LOG2E, q3, None)

    def score_block(block, buffer):
        at = pl.multiple_of(block * 256, 256)
        buffer[...] = dot_nt(k3[...], q3[pl.ds(at, 256), :])

    def softmax_block(block, buffer):
        at = pl.multiple_of(block * 256, 256)
        top = jnp.full((8, 256), -jnp.inf, F32)
        for row in range(0, length, CHUNK):
            top = jnp.maximum(top, jnp.max(buffer[row : row + CHUNK, :].reshape(CHUNK // 8, 8, 256), axis=0))
        top = jnp.max(top, axis=0, keepdims=True)
        sums = jnp.zeros((8, 256), F32)
        for row in range(0, length, CHUNK):
            weights = jnp.exp2(buffer[row : row + CHUNK, :] - top)
            sums = sums + jnp.sum(weights.reshape(CHUNK // 8, 8, 256), axis=0)
            hi, lo = split(weights)
            e_hi[row : row + CHUNK, pl.ds(at, 256)] = hi
            e_lo[row : row + CHUNK, pl.ds(at, 256)] = lo
        inv_sum[:, pl.ds(at, 256)] = jnp.broadcast_to(1.0 / jnp.sum(sums, axis=0, keepdims=True), (8, 256))

    pipeline(length // 256, score_block, softmax_block)

    def target(part):
        base = att_out if part == AIM else grad_out
        return base.at[:, pl.ds(pl.multiple_of(PART_COLUMN[part] + me * DIM, DIM), DIM)]

    def give(part, slot):
        block = got.at[SLOT[part], pl.ds(pl.multiple_of(slot * DIM, DIM), DIM), :]
        shard = shard_at(slot)

        @pl.when(shard != me)
        def _():
            pltpu.make_async_remote_copy(
                block, target(part), back_send.at[part], back_recv.at[part],
                device_id={"seq": shard}, device_id_type=MESH,
            ).start()

        @pl.when(shard == me)
        def _():
            pltpu.make_async_copy(block, target(part), back_recv.at[part]).start()

    reorder(VALUE, 1.0, v3, vt)

    def output_block(turn, buffer):
        at = pl.multiple_of(turn * 256, 256)
        buffer[0:DIM, :] = by_columns(vt, e_hi[:, pl.ds(at, 256)], e_lo[:, pl.ds(at, 256)])

    def attended_block(turn, buffer):
        at = pl.multiple_of(turn * 256, 256)
        out = buffer[0:DIM, :] * inv_sum[0:1, pl.ds(at, 256)]
        head_out[:, pl.ds(at, 256)] = out
        for half in range(2):
            begin = pl.multiple_of(at + half * DIM, DIM)
            got[SLOT[AIM], pl.ds(begin, DIM), :] = (gain * out[:, half * DIM : (half + 1) * DIM]).T

    def give_pair(part):
        def finish(turn):
            for half in range(2):
                give(part, turn * 2 + half)

        return finish

    pipeline(shards // 2, output_block, attended_block, give_pair(AIM))

    arrive(AIM, 1.0)

    def aim_block(block, buffer):
        at = pl.multiple_of(block * 512, 512)
        buffer[0:512, :] = dot(perm[pl.ds(at, 512), :], cat[...])

    gain_sum[...] = jnp.zeros((DIM, DIM), F32)

    def upstream_block(block, buffer):
        at = pl.multiple_of(block * 512, 512)
        placed = buffer[0:512, :]
        aim = placed[:, :DIM] + placed[:, DIM:]
        total = jnp.zeros((DIM, DIM), F32)
        for quarter in range(4):
            slot = block * 4 + quarter
            begin = pl.multiple_of(at + quarter * DIM, DIM)
            out = head_out[:, pl.ds(begin, DIM)]
            gap = gain * out - aim[quarter * DIM : (quarter + 1) * DIM, :].T
            loss_rows[slot] = jnp.broadcast_to(jnp.sum(gap * gap, axis=0, keepdims=True), (8, DIM))
            up_a = gap * meta_all[shard_at(slot), WEIGHT : WEIGHT + 1, :]
            total = total + up_a * out
            up = gain * up_a * inv_sum[0:1, pl.ds(begin, DIM)]
            delta[:, pl.ds(begin, DIM)] = jnp.broadcast_to(jnp.sum(up * out, axis=0, keepdims=True), (8, DIM))
            hi, lo = split(up.T)
            u3[pl.ds(begin, DIM), 0:DIM] = hi
            u3[pl.ds(begin, DIM), DIM : 2 * DIM] = hi
            u3[pl.ds(begin, DIM), 2 * DIM : 3 * DIM] = lo
        gain_sum[...] += total

    pipeline(length // 512, aim_block, upstream_block)

    gain_grad = jnp.sum(gain_sum[...].T, axis=0, keepdims=True)
    row_index = lax.broadcasted_iota(jnp.int32, (8, DIM), 0)
    for slot in range(shards):
        tile1[slot] = jnp.where(row_index == 0, loss_rows[slot], jnp.broadcast_to(gain_grad, (8, DIM)))
    stage1[me] = tile1[0]
    for slot, peer in enumerate(peers):
        pltpu.make_async_remote_copy(
            tile1.at[slot + 1, pl.ds(0, 2)], stage1.at[me, pl.ds(0, 2)], small_send.at[1], small_recv.at[1],
            device_id={"seq": peer}, device_id_type=MESH,
        ).start()

    def value_grad_block(turn, carry):
        block = turn
        at = pl.multiple_of(block * 512, 512)
        got[SLOT[VALUE], pl.ds(at, 512), :] = by_rows(at, u3.at[:, DIM : 3 * DIM])
        for quarter in range(4):
            give(VALUE, block * 4 + quarter)
        return carry

    lax.fori_loop(0, shards // 4, value_grad_block, 0)

    def exchange_losses():
        wait_small(small_recv.at[1], stage1, shards - 1)
        loss = jnp.zeros((1, DIM), F32)
        for shard in range(shards):
            loss = loss + stage1[shard, 0:1, :]
        excess = jnp.maximum(0.5 * loss / WIDTH - meta[REF : REF + 1, :], 0.0)
        hit = lax.broadcasted_iota(jnp.int32, (DIM, DIM), 0).astype(F32) == meta[BUCKET : BUCKET + 1, :]
        sums = lax.dot_general(
            jnp.where(row_index == 0, jnp.broadcast_to(excess, (8, DIM)), 1.0), jnp.where(hit, 1.0, 0.0),
            (((1,), (1,)), ((), ())), precision=HIGHEST, preferred_element_type=F32,
        )
        for shard in range(shards):
            tile2[shard : shard + 1, :] = stage1[shard, 1:2, :]
        tile2[shards : shards + 2, :] = sums[0:2, :]
        tile2[shards + 2 : shards + 4, :] = meta[EMB : EMB + 2, :]
        stage2[sample] = tile2[...]
        for turn in range(1, copies):
            other = lax.rem(sample + turn, copies)
            pltpu.make_async_remote_copy(
                tile2.at[pl.ds(0, shards + 4)], stage2.at[sample, pl.ds(0, shards + 4)], small_send.at[2], small_recv.at[2],
                device_id={"dp": other}, device_id_type=MESH,
            ).start()

    hi_a, lo_a, hi_b, lo_b = (perm.at[:, at : at + 256] for at in range(0, 1024, 256))

    def prob_grad_block(turn, buffer):
        at = pl.multiple_of(turn * 256, 256)
        buffer[...] = dot_nt(v3[...], u3[pl.ds(at, 256), :])

    def score_grad_block(turn, buffer, high, low):
        at = pl.multiple_of(turn * 256, 256)
        shift = delta[0:1, pl.ds(at, 256)]
        for row in range(0, length, CHUNK):
            here = (slice(row, row + CHUNK), pl.ds(at, 256))
            weights = e_hi[here].astype(F32) + e_lo[here].astype(F32)
            hi, lo = split((buffer[row : row + CHUNK, :] - shift) * weights)
            high[row : row + CHUNK, :] = hi
            low[row : row + CHUNK, :] = lo
            e_hi[here] = hi
            e_lo[here] = lo

    def query_grad_block(turn, high, low):
        at = pl.multiple_of(turn * 256, 256)
        grad = by_columns(kt, high[...], low[...]) * SCALE
        for half in range(2):
            begin = pl.multiple_of(at + half * DIM, DIM)
            got[SLOT[QUERY], pl.ds(begin, DIM), :] = grad[:, half * DIM : (half + 1) * DIM].T

    give_queries = give_pair(QUERY)
    prob_grad_block(0, score_a)
    prob_grad_block(1, score_b)
    score_grad_block(0, score_a, hi_a, lo_a)

    def gradient_pair(pair, carry):
        turn = 2 * pair + 1
        prob_grad_block(turn + 1, score_a)
        score_grad_block(turn, score_b, hi_b, lo_b)
        query_grad_block(turn - 1, hi_a, lo_a)
        prob_grad_block(turn + 2, score_b)
        score_grad_block(turn + 1, score_a, hi_a, lo_a)
        query_grad_block(turn, hi_b, lo_b)
        give_queries(turn - 1)
        give_queries(turn)
        pl.when(pair == 1)(exchange_losses)
        return carry

    last = shards // 2 - 1
    lax.fori_loop(0, last // 2, gradient_pair, 0)
    score_grad_block(last, score_b, hi_b, lo_b)
    query_grad_block(last - 1, hi_a, lo_a)
    query_grad_block(last, hi_b, lo_b)
    give_queries(last - 1)
    give_queries(last)

    def exchange_sums():
        if copies > 1:
            wait_small(small_recv.at[2], stage2, copies - 1, shards + 4)
        sums = jnp.zeros((2, DIM), F32)
        for other in range(copies):
            sums = sums + stage2[other, shards : shards + 2, :]
        tile3[0:2, :] = sums
        stage3[me, 0:2, :] = sums
        for peer in peers:
            pltpu.make_async_remote_copy(
                tile3.at[pl.ds(0, 2)], stage3.at[me, pl.ds(0, 2)], small_send.at[3], small_recv.at[3],
                device_id={"seq": peer}, device_id_type=MESH,
            ).start()

    def key_grad_block(turn, carry):
        block = turn
        at = pl.multiple_of(block * 512, 512)
        got[SLOT[KEY], pl.ds(at, 512), :] = by_rows(at, q3.at[:, DIM : 3 * DIM]) * (1.0 / LOG2E)
        for quarter in range(4):
            give(KEY, block * 4 + quarter)
        pl.when(turn == 1)(exchange_sums)
        return carry

    lax.fori_loop(0, shards // 4, key_grad_block, 0)

    by_sample = jnp.concatenate(
        [
            jnp.concatenate([stage2[other, row : row + 1, :] for row in (shards + 2, shards + 3)], axis=1)
            for other in range(copies)
        ],
        axis=0,
    )
    by_frequency = by_sample.T
    for head in range(shards):
        gains = jnp.concatenate([stage2[other, head : head + 1, :] for other in range(copies)], axis=0)
        weight_out[:, head * DIM : (head + 1) * DIM] = lax.dot_general(
            by_frequency, gains, (((1,), (0,)), ((), ())), precision=HIGHEST, preferred_element_type=F32
        )
    wait_small(small_recv.at[3], stage3, shards - 1)
    sums = jnp.zeros((2, DIM), F32)
    for shard in range(shards):
        sums = sums + stage3[shard, 0:2, :]
    mean = sums[0:1, :] / jnp.maximum(sums[1:2, :], 1.0)
    updated = meta[MIX : MIX + 1, :] * (1.0 + RATE * mean)
    updated = jnp.where(lane < BUCKETS, updated, 0.0)
    mixture = BUCKETS * updated / jnp.sum(updated, axis=1, keepdims=True)
    mix_out[...] = mixture[:, :BUCKETS]

    others = (shards - 1) * DIM
    for part in (KEY, QUERY, VALUE, AIM):
        if part in (VALUE, AIM):
            wait_sent(part)
        sent = got.at[SLOT[part], pl.ds(0, others), :]
        pltpu.make_async_copy(sent, sent, back_send.at[part]).wait()
        base = att_out if part == AIM else grad_out
        landed = base.at[:, PART_COLUMN[part] : PART_COLUMN[part] + WIDTH]
        pltpu.make_async_copy(landed, landed, back_recv.at[part]).wait()
    wait_small(small_send.at[0], meta_all, shards - 1)
    wait_small(small_send.at[1], stage1, shards - 1)
    if copies > 1:
        wait_small(small_send.at[2], stage2, copies - 1, shards + 4)
    wait_small(small_send.at[3], stage3, shards - 1)


def move_out(*refs):
    count = len(refs) // 2
    sources, outputs, sems = refs[:count], refs[count : 2 * count], refs[-1]
    moves = []
    for source, output in zip(sources, outputs):
        pieces = 4 if source.shape[0] >= DIM else 1
        rows = source.shape[0] // pieces
        for piece in range(pieces):
            part = pl.ds(piece * rows, rows)
            moves.append(pltpu.make_async_copy(source.at[part], output.at[part], sems.at[len(moves)]))
    for move in moves:
        move.start()
    for move in moves:
        move.wait()


def body(reader_rows, reader_targets, dest_pos, bucket_ids, ref_loss, timesteps, mod_weight, mixture_old):
    shards, copies = lax.axis_size("seq"), lax.axis_size("dp")
    length = shards * DIM
    half = FREQ_DIM // 2
    frequency = np.exp(-math.log(10000.0) * np.arange(half) / half).astype(np.float32)[None, :]
    any_spec = pl.BlockSpec(memory_space=pl.ANY)
    vmem_spec = pl.BlockSpec(memory_space=pltpu.VMEM)
    dma = pltpu.SemaphoreType.DMA
    attended, grads, weight_grad, mixture = pl.pallas_call(
        functools.partial(kernel, shards, copies),
        out_shape=(
            pltpu.VMEM((DIM, WIDTH), F32),
            pltpu.VMEM((DIM, 3 * WIDTH), F32),
            pltpu.VMEM((FREQ_DIM, WIDTH), F32),
            pltpu.VMEM((1, BUCKETS), F32),
        ),
        in_specs=[any_spec] * 9,
        out_specs=(vmem_spec, vmem_spec, vmem_spec, vmem_spec),
        scratch_shapes=[
            pltpu.VMEM((1, DIM), jnp.int32),
            pltpu.VMEM((1, DIM), jnp.int32),
            pltpu.VMEM((1, DIM), F32),
            pltpu.VMEM((1, DIM), F32),
            pltpu.SMEM((1,), jnp.int32),
            pltpu.SMEM((BUCKETS,), F32),
            pltpu.VMEM((8, DIM), F32),
            pltpu.VMEM((shards, 8, DIM), F32),
            pltpu.VMEM((4, length, DIM), F32),
            pltpu.VMEM((FREQ_DIM, DIM), F32),
            pltpu.VMEM((length, length), BF16),
            pltpu.VMEM((length, 2 * DIM), BF16),
            pltpu.VMEM((length, 3 * DIM), BF16),
            pltpu.VMEM((2 * DIM, length), BF16),
            pltpu.VMEM((length, 3 * DIM), BF16),
            pltpu.VMEM((length, 3 * DIM), BF16),
            pltpu.VMEM((2 * DIM, length), BF16),
            pltpu.VMEM((length, 3 * DIM), BF16),
            pltpu.VMEM((length, length), BF16),
            pltpu.VMEM((length, length), BF16),
            pltpu.VMEM((DIM, length), F32),
            pltpu.VMEM((8, length), F32),
            pltpu.VMEM((8, length), F32),
            pltpu.VMEM((DIM, DIM), F32),
            pltpu.VMEM((length, 256), F32),
            pltpu.VMEM((length, 256), F32),
            pltpu.VMEM((shards, 8, DIM), F32),
            pltpu.VMEM((shards, 8, DIM), F32),
            pltpu.VMEM((shards, 8, DIM), F32),
            pltpu.VMEM((copies, shards + 8, DIM), F32),
            pltpu.VMEM((shards + 8, DIM), F32),
            pltpu.VMEM((shards, 8, DIM), F32),
            pltpu.VMEM((8, DIM), F32),
            dma((4,)), dma((4,)), dma((4,)), dma((4,)), dma((4,)), dma((4,)), dma, dma((6,)),
        ],
        compiler_params=pltpu.CompilerParams(
            collective_id=0, has_side_effects=True, vmem_limit_bytes=56 * 1024 * 1024
        ),
        name="attend",
    )(reader_rows[0], reader_targets[0], dest_pos, bucket_ids, ref_loss, timesteps, mixture_old, frequency, mod_weight)
    results = (attended, grads, weight_grad, mixture)
    attended, grads, weight_grad, mixture = pl.pallas_call(
        move_out,
        out_shape=tuple(jax.ShapeDtypeStruct(item.shape, F32) for item in results),
        in_specs=[vmem_spec] * 4,
        out_specs=(any_spec,) * 4,
        scratch_shapes=[dma((13,))],
        compiler_params=pltpu.CompilerParams(vmem_limit_bytes=1024 * 1024),
        name="move_out",
    )(*(pltpu.with_memory_space_constraint(item, pltpu.VMEM) for item in results))
    return attended[None], grads[None], weight_grad, mixture[0]


def solution(mesh):
    return jax.shard_map(
        body,
        mesh=mesh,
        in_specs=(
            P("dp", "seq", None), P("dp", "seq", None), P("dp", "seq"), P("dp", "seq"),
            P("dp", "seq"), P("dp"), P(), P(),
        ),
        out_specs=(P("dp", "seq", None), P("dp", "seq", None), P(), P()),
        check_vma=False,
    )
```

```python
import functools
import math

import jax
import jax.numpy as jnp
import numpy as np
from jax import lax
from jax.experimental import pallas as pl
from jax.experimental.pallas import tpu as pltpu
from jax.sharding import PartitionSpec as P

HEADS = 16
DIM = 128
FREQ_DIM = 256
BUCKETS = 16
WIDTH = HEADS * DIM
RATE = 10.0
CHUNK = 64
LOG2E = 1.4426950408889634
SCALE = DIM ** (-0.5)
MESH = pl.DeviceIdType.MESH
HIGHEST = lax.Precision.HIGHEST
BF16 = jnp.bfloat16
F32 = jnp.float32

FAR_FIRST = (2, 5, 14, 15, 6, 1, 3, 9, 11, 8, 10, 4, 13, 12, 7, 0)
POS, WEIGHT, BUCKET, REF, EMB, MIX = 0, 1, 2, 3, 4, 6
KEY, QUERY, VALUE, AIM = 0, 1, 2, 3
SLOT = {AIM: KEY, VALUE: QUERY, QUERY: VALUE, KEY: AIM}
PART_COLUMN = {KEY: WIDTH, QUERY: 0, VALUE: 2 * WIDTH, AIM: 0}


def split(x):
    hi = x.astype(BF16)
    return hi, (x - hi.astype(F32)).astype(BF16)


def dot(a, b):
    return lax.dot_general(a, b, (((1,), (0,)), ((), ())), preferred_element_type=F32)


def dot_nt(a, b):
    return lax.dot_general(a, b, (((1,), (1,)), ((), ())), preferred_element_type=F32)


def kernel(
    shards, copies, rows, aims, places_in, buckets_in, ref_in, steps_in, old_in, frequency_in, mod_w,
    att_out, grad_out, weight_out, mix_out,
    places, buckets, ref_row, frequency, steps, old, meta, meta_all, got, mod_buf, perm, cat, k3, kt, q3, v3, vt, u3, e_hi, e_lo, head_out, inv_sum, delta,
    gain_sum, score_a, score_b, loss_rows, stage1, tile1, stage2, tile2, stage3, tile3,
    send_sem, recv_sem, back_send, back_recv, small_send, small_recv, mod_sem, operand_sem,
):
    length = shards * DIM
    me = lax.axis_index("seq")
    sample = lax.axis_index("dp")
    my_z, my_y = me // 4, lax.rem(me, 4)

    side = 1 - 2 * lax.rem(sample, 2)

    def shard_at(slot):
        along, shift = lax.rem(slot, 4), slot // 4
        return lax.rem(my_z + 4 + side * along, 4) * 4 + lax.rem(my_y + 8 + side * (along + shift), 4)

    peers = [shard_at(slot) for slot in range(1, shards)]

    barrier = pltpu.get_barrier_semaphore()
    for peer in peers:
        pl.semaphore_signal(barrier, inc=1, device_id={"seq": peer}, device_id_type=MESH)
    for turn in range(1, copies):
        other = lax.rem(sample + turn, copies)
        pl.semaphore_signal(barrier, inc=1, device_id={"dp": other}, device_id_type=MESH)

    operands = [
        pltpu.make_async_copy(source, into, operand_sem.at[index])
        for index, (source, into) in enumerate(
            (
                (places_in, places), (buckets_in, buckets), (ref_in, ref_row), (frequency_in, frequency),
                (steps_in, steps), (old_in, old),
            )
        )
    ]
    for operand in operands:
        operand.start()
    mod_copy = pltpu.make_async_copy(
        mod_w.at[:, pl.ds(pl.multiple_of(me * DIM, DIM), DIM)], mod_buf, mod_sem
    )
    mod_copy.start()
    pl.semaphore_wait(barrier, shards - 1 + copies - 1)

    def source(part, head):
        base = aims if part == AIM else rows
        return base.at[:, pl.ds(pl.multiple_of(PART_COLUMN[part] + head * DIM, DIM), DIM)]

    def landing(part):
        return got.at[part, pl.ds(pl.multiple_of(me * DIM, DIM), DIM), :]

    def send(part):
        pltpu.make_async_copy(source(part, me), landing(part), recv_sem.at[part]).start()
        for peer in peers:
            pltpu.make_async_remote_copy(
                source(part, peer), landing(part), send_sem.at[part], recv_sem.at[part],
                device_id={"seq": peer}, device_id_type=MESH,
            ).start()

    def wait_sent(part):
        sent = got.at[part, pl.ds(0, (shards - 1) * DIM), :]
        pltpu.make_async_copy(sent, sent, send_sem.at[part]).wait()

    send(KEY)

    for operand in operands:
        operand.wait()
    meta[POS : POS + 1, :] = places[...].astype(F32)
    bucket_row = buckets[...]
    lane = lax.broadcasted_iota(jnp.int32, (1, DIM), 1)
    weight_row = jnp.zeros((1, DIM), F32)
    old_row = jnp.zeros((1, DIM), F32)
    for bucket in range(BUCKETS):
        weight_row = weight_row + jnp.where(bucket_row == bucket, old[bucket], 0.0)
        old_row = old_row + jnp.where(lane == bucket, old[bucket], 0.0)
    meta[WEIGHT : WEIGHT + 1, :] = weight_row
    meta[BUCKET : BUCKET + 1, :] = bucket_row.astype(F32)
    meta[REF : REF + 1, :] = ref_row[...]
    angles = steps[0].astype(F32) * frequency[...]
    for row, wave in ((EMB, jnp.cos(angles)), (EMB + 1, jnp.sin(angles))):
        meta[row : row + 1, :] = wave / (1.0 + jnp.exp(-wave))
    meta[MIX : MIX + 1, :] = old_row
    meta[MIX + 1 : MIX + 2, :] = jnp.zeros((1, DIM), F32)
    meta_all[me] = meta[...]
    for peer in peers:
        pltpu.make_async_remote_copy(
            meta.at[pl.ds(0, 2)], meta_all.at[me, pl.ds(0, 2)], small_send.at[0], small_recv.at[0],
            device_id={"seq": peer}, device_id_type=MESH,
        ).start()
    send(QUERY)
    send(VALUE)
    send(AIM)

    def wait_small(sem, buffer, count, depth=2):
        taken = buffer.at[pl.ds(0, count), pl.ds(0, depth)]
        pltpu.make_async_copy(taken, taken, sem).wait()

    mod_copy.wait()
    embedding = jnp.concatenate([meta[EMB : EMB + 1, :], meta[EMB + 1 : EMB + 2, :]], axis=1)
    embedding = jnp.broadcast_to(embedding, (8, FREQ_DIM))
    gain_row = 1.0 + lax.dot_general(
        embedding, mod_buf[...], (((1,), (0,)), ((), ())), precision=HIGHEST, preferred_element_type=F32
    )
    gain = jnp.broadcast_to(gain_row[0:1, :], (DIM, DIM)).T

    wait_small(small_recv.at[0], meta_all, shards - 1)

    def perm_block(block, carry):
        at = pl.multiple_of(block * 256, 256)
        inside = lax.broadcasted_iota(jnp.int32, (DIM, DIM), 0)
        place = jnp.concatenate([inside + shard_at(2 * block + half) * DIM for half in range(2)], axis=0).astype(F32)
        for shard in range(shards):
            hit = place == meta_all[shard, POS : POS + 1, :]
            perm[pl.ds(at, 256), shard * DIM : (shard + 1) * DIM] = jnp.where(hit, 1.0, 0.0).astype(BF16)
        return carry

    lax.fori_loop(0, length // 256, perm_block, 0)

    def pipeline(count, make, use, finish=None):
        def both(at, last):
            make(at + 1, score_b)
            use(at, score_a)
            if not last:
                make(at + 2, score_a)
            use(at + 1, score_b)
            if finish is not None:
                finish(at)
                finish(at + 1)

        def one(pair, carry):
            both(2 * pair, False)
            return carry

        make(0, score_a)
        lax.fori_loop(0, count // 2 - 1, one, 0)
        both(count - 2, True)

    def arrive(part, factor):
        pltpu.make_async_copy(got.at[part], got.at[part], recv_sem.at[part]).wait()

        def one(block, carry):
            at = pl.multiple_of(block * 256, 256)
            hi, lo = split(got[part, pl.ds(at, 256), :] * factor)
            cat[pl.ds(at, 256), 0:DIM] = hi
            cat[pl.ds(at, 256), DIM : 2 * DIM] = lo
            return carry

        lax.fori_loop(0, length // 256, one, 0)

    def reorder(part, factor, into, transposed):
        arrive(part, factor)

        def make(block, buffer):
            at = pl.multiple_of(block * 512, 512)
            buffer[0:512, :] = dot(perm[pl.ds(at, 512), :], cat[...])

        def use(block, buffer):
            at = pl.multiple_of(block * 512, 512)
            placed = buffer[0:512, :]
            hi, lo = placed[:, :DIM].astype(BF16), placed[:, DIM:].astype(BF16)
            into[pl.ds(at, 512), 0:DIM] = hi
            into[pl.ds(at, 512), DIM : 2 * DIM] = hi if part == QUERY else lo
            into[pl.ds(at, 512), 2 * DIM : 3 * DIM] = lo if part == QUERY else hi
            if transposed is not None:
                hi, lo = split((placed[:, :DIM] + placed[:, DIM:]).T)
                transposed[0:DIM, pl.ds(at, 512)] = hi
                transposed[DIM : 2 * DIM, pl.ds(at, 512)] = lo

        pipeline(length // 512, make, use)

    def by_columns(left, high, low):
        full = dot(left[...], high)
        return full[:DIM] + full[DIM:] + dot(left[0:DIM, :], low)

    def by_rows(at, right):
        full = dot(e_hi[pl.ds(at, 512), :], right[...])
        return full[:, :DIM] + full[:, DIM:] + dot(e_lo[pl.ds(at, 512), :], right[:, 0:DIM])

    reorder(KEY, 1.0, k3, kt)
    wait_sent(KEY)
    wait_sent(QUERY)
    reorder(QUERY, SCALE * LOG2E, q3, None)

    def score_block(block, buffer):
        at = pl.multiple_of(block * 256, 256)
        buffer[...] = dot_nt(k3[...], q3[pl.ds(at, 256), :])

    def softmax_block(block, buffer):
        at = pl.multiple_of(block * 256, 256)
        top = jnp.full((8, 256), -jnp.inf, F32)
        for row in range(0, length, CHUNK):
            top = jnp.maximum(top, jnp.max(buffer[row : row + CHUNK, :].reshape(CHUNK // 8, 8, 256), axis=0))
        top = jnp.max(top, axis=0, keepdims=True)
        sums = jnp.zeros((8, 256), F32)
        for row in range(0, length, CHUNK):
            weights = jnp.exp2(buffer[row : row + CHUNK, :] - top)
            sums = sums + jnp.sum(weights.reshape(CHUNK // 8, 8, 256), axis=0)
            hi, lo = split(weights)
            e_hi[row : row + CHUNK, pl.ds(at, 256)] = hi
            e_lo[row : row + CHUNK, pl.ds(at, 256)] = lo
        inv_sum[:, pl.ds(at, 256)] = jnp.broadcast_to(1.0 / jnp.sum(sums, axis=0, keepdims=True), (8, 256))

    pipeline(length // 256, score_block, softmax_block)

    def target(part):
        base = att_out if part == AIM else grad_out
        return base.at[:, pl.ds(pl.multiple_of(PART_COLUMN[part] + me * DIM, DIM), DIM)]

    def give(part, slot):
        block = got.at[SLOT[part], pl.ds(pl.multiple_of(slot * DIM, DIM), DIM), :]
        shard = shard_at(slot)

        @pl.when(shard != me)
        def _():
            pltpu.make_async_remote_copy(
                block, target(part), back_send.at[part], back_recv.at[part],
                device_id={"seq": shard}, device_id_type=MESH,
            ).start()

        @pl.when(shard == me)
        def _():
            pltpu.make_async_copy(block, target(part), back_recv.at[part]).start()

    reorder(VALUE, 1.0, v3, vt)

    def output_block(turn, buffer):
        at = pl.multiple_of(turn * 256, 256)
        buffer[0:DIM, :] = by_columns(vt, e_hi[:, pl.ds(at, 256)], e_lo[:, pl.ds(at, 256)])

    def attended_block(turn, buffer):
        at = pl.multiple_of(turn * 256, 256)
        out = buffer[0:DIM, :] * inv_sum[0:1, pl.ds(at, 256)]
        head_out[:, pl.ds(at, 256)] = out
        for half in range(2):
            begin = pl.multiple_of(at + half * DIM, DIM)
            got[SLOT[AIM], pl.ds(begin, DIM), :] = (gain * out[:, half * DIM : (half + 1) * DIM]).T

    def give_pair(part):
        def finish(turn):
            for half in range(2):
                give(part, turn * 2 + half)

        return finish

    pipeline(shards // 2, output_block, attended_block, give_pair(AIM))

    arrive(AIM, 1.0)

    def aim_block(block, buffer):
        at = pl.multiple_of(block * 512, 512)
        buffer[0:512, :] = dot(perm[pl.ds(at, 512), :], cat[...])

    gain_sum[...] = jnp.zeros((DIM, DIM), F32)

    def upstream_block(block, buffer):
        at = pl.multiple_of(block * 512, 512)
        placed = buffer[0:512, :]
        aim = placed[:, :DIM] + placed[:, DIM:]
        total = jnp.zeros((DIM, DIM), F32)
        for quarter in range(4):
            slot = block * 4 + quarter
            begin = pl.multiple_of(at + quarter * DIM, DIM)
            out = head_out[:, pl.ds(begin, DIM)]
            gap = gain * out - aim[quarter * DIM : (quarter + 1) * DIM, :].T
            loss_rows[slot] = jnp.broadcast_to(jnp.sum(gap * gap, axis=0, keepdims=True), (8, DIM))
            up_a = gap * meta_all[shard_at(slot), WEIGHT : WEIGHT + 1, :]
            total = total + up_a * out
            up = gain * up_a * inv_sum[0:1, pl.ds(begin, DIM)]
            delta[:, pl.ds(begin, DIM)] = jnp.broadcast_to(jnp.sum(up * out, axis=0, keepdims=True), (8, DIM))
            hi, lo = split(up.T)
            u3[pl.ds(begin, DIM), 0:DIM] = hi
            u3[pl.ds(begin, DIM), DIM : 2 * DIM] = hi
            u3[pl.ds(begin, DIM), 2 * DIM : 3 * DIM] = lo
        gain_sum[...] += total

    pipeline(length // 512, aim_block, upstream_block)

    gain_grad = jnp.sum(gain_sum[...].T, axis=0, keepdims=True)
    row_index = lax.broadcasted_iota(jnp.int32, (8, DIM), 0)
    for slot in range(shards):
        tile1[slot] = jnp.where(row_index == 0, loss_rows[slot], jnp.broadcast_to(gain_grad, (8, DIM)))
    stage1[me] = tile1[0]
    for slot, peer in enumerate(peers):
        pltpu.make_async_remote_copy(
            tile1.at[slot + 1, pl.ds(0, 2)], stage1.at[me, pl.ds(0, 2)], small_send.at[1], small_recv.at[1],
            device_id={"seq": peer}, device_id_type=MESH,
        ).start()

    def value_grad_block(turn, carry):
        block = turn
        at = pl.multiple_of(block * 512, 512)
        got[SLOT[VALUE], pl.ds(at, 512), :] = by_rows(at, u3.at[:, DIM : 3 * DIM])
        for quarter in range(4):
            give(VALUE, block * 4 + quarter)
        return carry

    lax.fori_loop(0, shards // 4, value_grad_block, 0)

    def exchange_losses():
        wait_small(small_recv.at[1], stage1, shards - 1)
        loss = jnp.zeros((1, DIM), F32)
        for shard in range(shards):
            loss = loss + stage1[shard, 0:1, :]
        excess = jnp.maximum(0.5 * loss / WIDTH - meta[REF : REF + 1, :], 0.0)
        hit = lax.broadcasted_iota(jnp.int32, (DIM, DIM), 0).astype(F32) == meta[BUCKET : BUCKET + 1, :]
        sums = lax.dot_general(
            jnp.where(row_index == 0, jnp.broadcast_to(excess, (8, DIM)), 1.0), jnp.where(hit, 1.0, 0.0),
            (((1,), (1,)), ((), ())), precision=HIGHEST, preferred_element_type=F32,
        )
        for shard in range(shards):
            tile2[shard : shard + 1, :] = stage1[shard, 1:2, :]
        tile2[shards : shards + 2, :] = sums[0:2, :]
        tile2[shards + 2 : shards + 4, :] = meta[EMB : EMB + 2, :]
        stage2[sample] = tile2[...]
        for turn in range(1, copies):
            other = lax.rem(sample + turn, copies)
            pltpu.make_async_remote_copy(
                tile2.at[pl.ds(0, shards + 4)], stage2.at[sample, pl.ds(0, shards + 4)], small_send.at[2], small_recv.at[2],
                device_id={"dp": other}, device_id_type=MESH,
            ).start()

    hi_a, lo_a, hi_b, lo_b = (perm.at[:, at : at + 256] for at in range(0, 1024, 256))

    def prob_grad_block(turn, buffer):
        at = pl.multiple_of(turn * 256, 256)
        buffer[...] = dot_nt(v3[...], u3[pl.ds(at, 256), :])

    def score_grad_block(turn, buffer, high, low):
        at = pl.multiple_of(turn * 256, 256)
        shift = delta[0:1, pl.ds(at, 256)]
        for row in range(0, length, CHUNK):
            here = (slice(row, row + CHUNK), pl.ds(at, 256))
            weights = e_hi[here].astype(F32) + e_lo[here].astype(F32)
            hi, lo = split((buffer[row : row + CHUNK, :] - shift) * weights)
            high[row : row + CHUNK, :] = hi
            low[row : row + CHUNK, :] = lo
            e_hi[here] = hi
            e_lo[here] = lo

    def query_grad_block(turn, high, low):
        at = pl.multiple_of(turn * 256, 256)
        grad = by_columns(kt, high[...], low[...]) * SCALE
        for half in range(2):
            begin = pl.multiple_of(at + half * DIM, DIM)
            got[SLOT[QUERY], pl.ds(begin, DIM), :] = grad[:, half * DIM : (half + 1) * DIM].T

    give_queries = give_pair(QUERY)
    prob_grad_block(0, score_a)
    prob_grad_block(1, score_b)
    score_grad_block(0, score_a, hi_a, lo_a)

    def gradient_pair(pair, carry):
        turn = 2 * pair + 1
        prob_grad_block(turn + 1, score_a)
        score_grad_block(turn, score_b, hi_b, lo_b)
        query_grad_block(turn - 1, hi_a, lo_a)
        prob_grad_block(turn + 2, score_b)
        score_grad_block(turn + 1, score_a, hi_a, lo_a)
        query_grad_block(turn, hi_b, lo_b)
        give_queries(turn - 1)
        give_queries(turn)
        pl.when(pair == 1)(exchange_losses)
        return carry

    last = shards // 2 - 1
    lax.fori_loop(0, last // 2, gradient_pair, 0)
    score_grad_block(last, score_b, hi_b, lo_b)
    query_grad_block(last - 1, hi_a, lo_a)
    query_grad_block(last, hi_b, lo_b)
    give_queries(last - 1)
    give_queries(last)

    def exchange_sums():
        if copies > 1:
            wait_small(small_recv.at[2], stage2, copies - 1, shards + 4)
        sums = jnp.zeros((2, DIM), F32)
        for other in range(copies):
            sums = sums + stage2[other, shards : shards + 2, :]
        tile3[0:2, :] = sums
        stage3[me, 0:2, :] = sums
        for peer in peers:
            pltpu.make_async_remote_copy(
                tile3.at[pl.ds(0, 2)], stage3.at[me, pl.ds(0, 2)], small_send.at[3], small_recv.at[3],
                device_id={"seq": peer}, device_id_type=MESH,
            ).start()

    def key_grad_block(turn, carry):
        block = turn
        at = pl.multiple_of(block * 512, 512)
        got[SLOT[KEY], pl.ds(at, 512), :] = by_rows(at, q3.at[:, DIM : 3 * DIM]) * (1.0 / LOG2E)
        pl.when(turn == 1)(exchange_sums)
        return carry

    lax.fori_loop(0, shards // 4, key_grad_block, 0)
    for slot in FAR_FIRST:
        give(KEY, slot)

    by_sample = jnp.concatenate(
        [
            jnp.concatenate([stage2[other, row : row + 1, :] for row in (shards + 2, shards + 3)], axis=1)
            for other in range(copies)
        ],
        axis=0,
    )
    by_frequency = by_sample.T
    for head in range(shards):
        gains = jnp.concatenate([stage2[other, head : head + 1, :] for other in range(copies)], axis=0)
        weight_out[:, head * DIM : (head + 1) * DIM] = lax.dot_general(
            by_frequency, gains, (((1,), (0,)), ((), ())), precision=HIGHEST, preferred_element_type=F32
        )
    wait_small(small_recv.at[3], stage3, shards - 1)
    sums = jnp.zeros((2, DIM), F32)
    for shard in range(shards):
        sums = sums + stage3[shard, 0:2, :]
    mean = sums[0:1, :] / jnp.maximum(sums[1:2, :], 1.0)
    updated = meta[MIX : MIX + 1, :] * (1.0 + RATE * mean)
    updated = jnp.where(lane < BUCKETS, updated, 0.0)
    mixture = BUCKETS * updated / jnp.sum(updated, axis=1, keepdims=True)
    mix_out[...] = mixture[:, :BUCKETS]

    others = (shards - 1) * DIM
    for part in (KEY, QUERY, VALUE, AIM):
        if part in (VALUE, AIM):
            wait_sent(part)
        sent = got.at[SLOT[part], pl.ds(0, others), :]
        pltpu.make_async_copy(sent, sent, back_send.at[part]).wait()
        base = att_out if part == AIM else grad_out
        landed = base.at[:, PART_COLUMN[part] : PART_COLUMN[part] + WIDTH]
        pltpu.make_async_copy(landed, landed, back_recv.at[part]).wait()
    wait_small(small_send.at[0], meta_all, shards - 1)
    wait_small(small_send.at[1], stage1, shards - 1)
    if copies > 1:
        wait_small(small_send.at[2], stage2, copies - 1, shards + 4)
    wait_small(small_send.at[3], stage3, shards - 1)


def move_out(*refs):
    count = len(refs) // 2
    sources, outputs, sems = refs[:count], refs[count : 2 * count], refs[-1]
    moves = []
    for source, output in zip(sources, outputs):
        pieces = 4 if source.shape[0] >= DIM else 1
        rows = source.shape[0] // pieces
        for piece in range(pieces):
            part = pl.ds(piece * rows, rows)
            moves.append(pltpu.make_async_copy(source.at[part], output.at[part], sems.at[len(moves)]))
    for move in moves:
        move.start()
    for move in moves:
        move.wait()


def body(reader_rows, reader_targets, dest_pos, bucket_ids, ref_loss, timesteps, mod_weight, mixture_old):
    shards, copies = lax.axis_size("seq"), lax.axis_size("dp")
    length = shards * DIM
    half = FREQ_DIM // 2
    frequency = np.exp(-math.log(10000.0) * np.arange(half) / half).astype(np.float32)[None, :]
    any_spec = pl.BlockSpec(memory_space=pl.ANY)
    vmem_spec = pl.BlockSpec(memory_space=pltpu.VMEM)
    dma = pltpu.SemaphoreType.DMA
    attended, grads, weight_grad, mixture = pl.pallas_call(
        functools.partial(kernel, shards, copies),
        out_shape=(
            pltpu.VMEM((DIM, WIDTH), F32),
            pltpu.VMEM((DIM, 3 * WIDTH), F32),
            pltpu.VMEM((FREQ_DIM, WIDTH), F32),
            pltpu.VMEM((1, BUCKETS), F32),
        ),
        in_specs=[any_spec] * 9,
        out_specs=(vmem_spec, vmem_spec, vmem_spec, vmem_spec),
        scratch_shapes=[
            pltpu.VMEM((1, DIM), jnp.int32),
            pltpu.VMEM((1, DIM), jnp.int32),
            pltpu.VMEM((1, DIM), F32),
            pltpu.VMEM((1, DIM), F32),
            pltpu.SMEM((1,), jnp.int32),
            pltpu.SMEM((BUCKETS,), F32),
            pltpu.VMEM((8, DIM), F32),
            pltpu.VMEM((shards, 8, DIM), F32),
            pltpu.VMEM((4, length, DIM), F32),
            pltpu.VMEM((FREQ_DIM, DIM), F32),
            pltpu.VMEM((length, length), BF16),
            pltpu.VMEM((length, 2 * DIM), BF16),
            pltpu.VMEM((length, 3 * DIM), BF16),
            pltpu.VMEM((2 * DIM, length), BF16),
            pltpu.VMEM((length, 3 * DIM), BF16),
            pltpu.VMEM((length, 3 * DIM), BF16),
            pltpu.VMEM((2 * DIM, length), BF16),
            pltpu.VMEM((length, 3 * DIM), BF16),
            pltpu.VMEM((length, length), BF16),
            pltpu.VMEM((length, length), BF16),
            pltpu.VMEM((DIM, length), F32),
            pltpu.VMEM((8, length), F32),
            pltpu.VMEM((8, length), F32),
            pltpu.VMEM((DIM, DIM), F32),
            pltpu.VMEM((length, 256), F32),
            pltpu.VMEM((length, 256), F32),
            pltpu.VMEM((shards, 8, DIM), F32),
            pltpu.VMEM((shards, 8, DIM), F32),
            pltpu.VMEM((shards, 8, DIM), F32),
            pltpu.VMEM((copies, shards + 8, DIM), F32),
            pltpu.VMEM((shards + 8, DIM), F32),
            pltpu.VMEM((shards, 8, DIM), F32),
            pltpu.VMEM((8, DIM), F32),
            dma((4,)), dma((4,)), dma((4,)), dma((4,)), dma((4,)), dma((4,)), dma, dma((6,)),
        ],
        compiler_params=pltpu.CompilerParams(
            collective_id=0, has_side_effects=True, vmem_limit_bytes=56 * 1024 * 1024
        ),
        name="attend",
    )(reader_rows[0], reader_targets[0], dest_pos, bucket_ids, ref_loss, timesteps, mixture_old, frequency, mod_weight)
    results = (attended, grads, weight_grad, mixture)
    attended, grads, weight_grad, mixture = pl.pallas_call(
        move_out,
        out_shape=tuple(jax.ShapeDtypeStruct(item.shape, F32) for item in results),
        in_specs=[vmem_spec] * 4,
        out_specs=(any_spec,) * 4,
        scratch_shapes=[dma((13,))],
        compiler_params=pltpu.CompilerParams(vmem_limit_bytes=1024 * 1024),
        name="move_out",
    )(*(pltpu.with_memory_space_constraint(item, pltpu.VMEM) for item in results))
    return attended[None], grads[None], weight_grad, mixture[0]


def solution(mesh):
    return jax.shard_map(
        body,
        mesh=mesh,
        in_specs=(
            P("dp", "seq", None), P("dp", "seq", None), P("dp", "seq"), P("dp", "seq"),
            P("dp", "seq"), P("dp"), P(), P(),
        ),
        out_specs=(P("dp", "seq", None), P("dp", "seq", None), P(), P()),
        check_vma=False,
    )
```
